128 devices in a mesh: chain: 128 (over z, y, x, core).
Axes of the slice: x: 4, y: 4, z: 4, core: 2. Of those that a mesh axis runs over, the one named last changes fastest.
Arguments:
- sketch: float32 [256, 64, 256], P('chain'), may hold values from -42 to 42
- inv_diag: float32 [256, 256, 256], P('chain'), may hold values from -0.1 to 1.5
- upper: float32 [256, 256, 256], P('chain'), may hold values from -1.5 to 1.5
- lower: float32 [256, 256, 256], P('chain'), may hold values from -1.1 to 1.1
Outputs:
- basis: float32 [256, 64, 256], P('chain')
- r_factor: float32 [64, 64], replicated
The draws below stay inside these ranges and needn't reach their ends.
All inputs are finite; a program needn't handle non-finite values.
Results may differ from the reference program's by a relative error of at most 0.0003.
Values sent between devices are 32-bit elements; how exact they have to be, the bound alone decides.
A program may use at most 192 MiB of HBM per device.

```python
import math
import jax
import jax.numpy as jnp
from jax import lax

B = 256
K = 64
STATIONS = 256


def diag_scale(key):
    return jnp.exp(jax.random.uniform(jax.random.fold_in(key, 101), (STATIONS, B), jnp.float32, math.log(0.7), math.log(1.4)))


def mode_pick(key, portion):
    return (jax.random.randint(jax.random.fold_in(key, 401), (B,), 0, 10) < portion).astype(jnp.float32)


def mode_signs(key, salt):
    return jax.random.randint(jax.random.fold_in(key, salt), (B,), 0, 2).astype(jnp.float32) * 2.0 - 1.0


def decay_rates(key, salt, picked, signs):
    lengths = jnp.exp(jax.random.uniform(jax.random.fold_in(key, salt), (B,), jnp.float32, math.log(3.0), math.log(45.0)))
    jitter = jnp.exp(jax.random.uniform(jax.random.fold_in(key, salt + 1), (STATIONS, B), jnp.float32, math.log(0.7), math.log(1.4)))
    quick = jnp.exp(-1.0 / (lengths * jitter))
    horizon = jnp.exp(jax.random.uniform(jax.random.fold_in(key, salt + 3), (B,), jnp.float32, math.log(0.1), math.log(0.5)))
    spread = jnp.exp(jax.random.uniform(jax.random.fold_in(key, salt + 4), (STATIONS, B), jnp.float32, math.log(0.5), math.log(2.0)))
    lasting = jnp.exp(-horizon * spread / STATIONS)
    places = jax.random.randint(jax.random.fold_in(key, salt + 5), (2,), 0, STATIONS)
    struck = jnp.max((jnp.arange(STATIONS)[:, None] == places[None, :]).astype(jnp.float32), axis=1)
    kept_share = jax.random.uniform(jax.random.fold_in(key, salt + 6), (STATIONS, B), jnp.float32, 0.55, 0.8)
    lasting = lasting * (1.0 - struck[:, None] * (1.0 - kept_share))
    return signs * (picked * lasting + (1.0 - picked) * quick)


def mixing(key, salt):
    noise = jax.random.truncated_normal(jax.random.fold_in(key, salt), -3.0, 3.0, (STATIONS, B, B), jnp.float32)
    return jnp.eye(B, dtype=jnp.float32) + noise * (0.03 / math.sqrt(B))


def draw_sketch(key, part):
    portion = 5
    picked = mode_pick(key, portion)
    column_scale = picked * (2.0 / math.sqrt(STATIONS)) + (1.0 - picked)
    ramp = 1.0 + 2.0 * jnp.arange(STATIONS, dtype=jnp.float32) / (STATIONS - 1)
    values = jax.random.truncated_normal(jax.random.fold_in(key, 7), -5.0, 5.0, (STATIONS, K, B), jnp.float32)
    return values * ramp[:, None, None] * column_scale[None, None, :]


def draw_inv_diag(key, part):
    scale = diag_scale(key)
    return mixing(key, 201) * scale[:, None, :]


def draw_upper(key, part):
    portion = 5
    picked = mode_pick(key, portion)
    scale = diag_scale(key)
    previous = jnp.roll(scale, 1, axis=0)
    rates = decay_rates(key, 211, picked, mode_signs(key, 231))
    return (rates / previous)[:, :, None] * mixing(key, 221)


def draw_lower(key, part):
    portion = 5
    picked = mode_pick(key, portion)
    forward_signs = mode_signs(key, 231)
    own_signs = mode_signs(key, 331)
    signs = picked * -forward_signs + (1.0 - picked) * own_signs
    rates = decay_rates(key, 311, picked, signs)
    return rates[:, :, None] * mixing(key, 321)


def setup_inputs(seed: int = 0) -> dict:
    streams_of = jax.random.split(jax.random.key(seed), 5)
    sketch = draw_sketch(jax.random.fold_in(streams_of[4], 71), 0)
    inv_diag = draw_inv_diag(jax.random.fold_in(streams_of[4], 71), 0)
    upper = draw_upper(jax.random.fold_in(streams_of[4], 71), 0)
    lower = draw_lower(jax.random.fold_in(streams_of[4], 71), 0)
    return {"sketch": sketch, "inv_diag": inv_diag, "upper": upper, "lower": lower}


HIGH = lax.Precision.HIGHEST

def product(left, right):
    return jnp.dot(left.astype(jnp.float32), right.astype(jnp.float32), precision=HIGH, preferred_element_type=jnp.float32)

def forward_step(state, blocks):
    rhs, coupling, inverse = blocks
    fresh = product(rhs - product(state, coupling), inverse)
    return (fresh, fresh)

def backward_step(carry, blocks):
    state, coupling = blocks
    solved = state - carry
    return (product(solved, coupling), solved)

def reference(sketch, inv_diag, upper, lower):
    columns = sketch.shape[1]
    width = sketch.shape[2]
    blank = jnp.zeros((columns, width), jnp.float32)
    _, states = lax.scan(forward_step, blank, (sketch, upper, inv_diag))
    _, solved = lax.scan(backward_step, blank, (states, lower), reverse=True)
    gram = jnp.einsum('skb,slb->kl', solved, solved, precision=HIGH) / (STATIONS * B)
    chol = jnp.linalg.cholesky(gram)
    identity = jnp.eye(columns, dtype=jnp.float32)
    inverse = lax.linalg.triangular_solve(chol, identity, left_side=True, lower=True)
    basis = jnp.einsum('kl,slb->skb', inverse, solved, precision=HIGH)
    return (basis, jnp.transpose(chol))
```

```python
import jax
import jax.numpy as jnp
from jax import lax
from jax.experimental import pallas as pl
from jax.experimental.pallas import tpu as pltpu
from jax.sharding import PartitionSpec as P

HIGH = lax.Precision.HIGHEST
MESH = pl.DeviceIdType.MESH
F32 = jnp.float32

W = 256
K = 64
HALF_M = 128
HALF_C = 32
HALF = HALF_M + HALF_C
ROWS = 2 * HALF
SEMS = 72


def dot(a, b):
    return jnp.dot(a, b, precision=HIGH, preferred_element_type=F32)


def mat(n):
    return jnp.concatenate([n[0:HALF_M], n[HALF : HALF + HALF_M]], axis=0)


def vec(n):
    return jnp.concatenate([n[HALF_M:HALF], n[HALF + HALF_M : ROWS]], axis=0)


def pack(m, c):
    return jnp.concatenate([m[0:HALF_M], c[0:HALF_C], m[HALF_M:W], c[HALF_C:K]], axis=0)


def add_vec(r, n):
    return jnp.concatenate(
        [
            r[0:HALF_M],
            r[HALF_M:HALF] + n[HALF_M:HALF],
            r[HALF : HALF + HALF_M],
            r[HALF + HALF_M : ROWS] + n[HALF + HALF_M : ROWS],
        ],
        axis=0,
    )


def compose(f, n):
    return add_vec(dot(f, mat(n)), n)


def apply(v, n):
    return dot(v, mat(n)) + vec(n)


def identity(rows, columns):
    return (
        lax.broadcasted_iota(jnp.int32, (rows, columns), 0) == lax.broadcasted_iota(jnp.int32, (rows, columns), 1)
    ).astype(F32)


def factor(gram):
    work = jnp.concatenate([gram, identity(K, K)], axis=1)
    blocks = [work[8 * b : 8 * b + 8] for b in range(K // 8)]
    sub = lax.broadcasted_iota(jnp.int32, (8, 2 * K), 0)
    lane = lax.broadcasted_iota(jnp.int32, (8, 2 * K), 1)
    scale = [jnp.zeros((8, 2 * K), F32) for _ in range(K // 8)]
    for k in range(K):
        b, r = divmod(k, 8)
        row = jnp.broadcast_to(blocks[b][r : r + 1], (8, 2 * K))
        pivot = jnp.broadcast_to(row[:, k : k + 1], (8, 2 * K))
        scaled = row / pivot
        scale[b] = jnp.where(sub == r, pivot, scale[b])
        for i in range(b, K // 8):
            column = jnp.broadcast_to(blocks[i][:, k : k + 1], (8, 2 * K))
            if i == b:
                column = jnp.where(sub > r, column, 0.0)
            blocks[i] = blocks[i] - column * scaled
    out = jnp.concatenate([blocks[b] * lax.rsqrt(scale[b]) for b in range(K // 8)], axis=0)
    upper = jnp.where(
        lax.broadcasted_iota(jnp.int32, (K, K), 0) <= lax.broadcasted_iota(jnp.int32, (K, K), 1), out[:, 0:K], 0.0
    )
    return upper, out[:, K : 2 * K]


def kernel(
    sketch, inv_diag, upper, lower, basis, r_factor,
    own0, fc, gc, hc, y0s, y1s, dev_g, dev_h,
    xf, xg, xh, xpre, xsuf_h, xsuf_g, yf, yg, ypre, ysuf_g,
    zc, zm, zc_in, zm_in, va, va_in, zg, er, ep, ysuf_e, gsum, gx, gy, gz,
    send, recv,
):
    me = lax.axis_index("chain")
    c = lax.rem(me, 2)
    x = lax.rem(me // 2, 4)
    y = lax.rem(me // 8, 4)
    z = me // 32

    def at(zz, yy, xx, cc):
        return ((zz * 4 + yy) * 4 + xx) * 2 + cc

    sibling = at(z, y, x, 1 - c)
    xs = [at(z, y, lax.rem(x + k, 4), c) for k in range(4)]
    ys = [at(z, lax.rem(y + k, 4), x, c) for k in range(4)]
    zs = [at(lax.rem(z + k, 4), y, x, c) for k in range(4)]

    barrier = pltpu.get_barrier_semaphore()
    for other in (sibling, *xs[1:], *ys[1:], *zs[1:]):
        pl.semaphore_signal(barrier, inc=1, device_id=(other,), device_id_type=MESH)

    sent = []
    used = [0]

    def slot():
        used[0] += 1
        assert used[0] <= SEMS
        return used[0] - 1

    def start(src, dst, i, other):
        copy = pltpu.make_async_remote_copy(
            src_ref=src, dst_ref=dst, send_sem=send.at[i], recv_sem=recv.at[i], device_id=(other,), device_id_type=MESH
        )
        copy.start()
        sent.append(copy)

    def arrived(dst, i):
        pltpu.make_async_remote_copy(
            src_ref=dst, dst_ref=dst, send_sem=send.at[i], recv_sem=recv.at[i], device_id=(sibling,), device_id_type=MESH
        ).wait_recv()

    def half(ref, j, rows):
        return ref.at[j, pl.ds(pl.multiple_of(c * rows, 8), rows)]

    def other_half(ref, j, rows):
        return ref.at[j, pl.ds(pl.multiple_of((1 - c) * rows, 8), rows)]

    class Gather:
        def __init__(self, ref, rows, place, peers, steps):
            self.ref, self.rows, self.place, self.peers, self.steps = ref, rows, place, peers, steps
            self.first = {k: slot() for k in steps}
            self.second = {k: slot() for k in steps}

        def source(self, k):
            return lax.rem(self.place + 4 - k, 4)

        def start(self):
            for k in self.steps:
                part = half(self.ref, self.place, self.rows)
                start(part, part, self.first[k], self.peers[k])

        def forward(self):
            for k in self.steps:
                part = half(self.ref, self.source(k), self.rows)
                arrived(part, self.first[k])
                start(part, part, self.second[k], sibling)

        def finish(self):
            for k in self.steps:
                arrived(other_half(self.ref, self.source(k), self.rows), self.second[k])

    class Share:
        def __init__(self, ref, place, peers):
            self.ref, self.place, self.peers = ref, place, peers
            self.sems = {k: slot() for k in (1, 3, 2)}

        def start(self):
            for k in (1, 3, 2):
                start(self.ref.at[self.place], self.ref.at[self.place], self.sems[k], self.peers[k])

        def finish(self):
            for k in (1, 3, 2):
                arrived(self.ref.at[lax.rem(self.place + 4 - k, 4)], self.sems[k])

    y0s[...] = dot(pack(-upper[0], sketch[0]), inv_diag[0])
    own0[...] = dot(pack(-upper[1], sketch[1]), inv_diag[1])
    y1s[...] = compose(y0s[...], own0[...])
    fc[c] = y1s[...]
    pl.semaphore_wait(barrier, 10)
    sem_f, sem_g, sem_h = slot(), slot(), slot()
    start(fc.at[c], fc.at[c], sem_f, sibling)
    gc[c] = dot(lower[1], lower[0])
    start(gc.at[c], gc.at[c], sem_g, sibling)
    hc[c] = dot(y0s[...] - dot(y1s[...], lower[1]), lower[0])
    start(hc.at[c], hc.at[c], sem_h, sibling)
    arrived(fc.at[1 - c], sem_f)

    xf[x] = compose(fc[0], fc[1])
    gather_xf = Gather(xf, HALF, x, xs, (1, 3, 2))
    gather_xf.start()

    arrived(gc.at[1 - c], sem_g)
    arrived(hc.at[1 - c], sem_h)
    late = compose(fc[0], hc[1])
    xg[x] = dot(gc[1], gc[0])
    xh[x] = dot(late, gc[0]) + hc[0]
    second = c == 1
    dev_g[...] = jnp.where(second, identity(W, W), gc[1])
    dev_h[...] = jnp.where(second, 0.0, late)
    y0s[...] = jnp.where(second, compose(fc[0], y0s[...]), y0s[...])
    y1s[...] = jnp.where(second, xf[x], y1s[...])

    gather_xf.forward()
    gather_xf.finish()
    q01 = compose(xf[0], xf[1])
    xpre[2] = q01
    yf[y] = compose(q01, compose(xf[2], xf[3]))

    gather_yf = Gather(yf, HALF, y, ys, (1, 3, 2))
    gather_yf.start()
    gather_xg = Gather(xg, HALF_M, x, xs, (1, 3, 2))
    gather_xg.start()
    gather_xh = Gather(xh, HALF, x, xs, (1, 3, 2))
    gather_xh.start()

    eye = identity(W, W)
    xpre[0] = pack(eye, jnp.zeros((K, W), F32))
    xpre[1] = xf[0]
    xpre[3] = compose(xpre[2], xf[2])
    y0s[...] = compose(xpre[x], y0s[...])
    y1s[...] = compose(xpre[x], y1s[...])
    dev_h[...] = compose(xpre[x], dev_h[...])

    gather_yf.forward()
    gather_yf.finish()
    q01 = compose(yf[0], yf[1])
    ypre[2] = q01
    plane = compose(q01, compose(yf[2], yf[3]))

    zc[...] = vec(plane)
    zm[...] = mat(plane)
    sem_c, sem_m, sem_m2, sem_v1, sem_v2 = slot(), slot(), slot(), slot(), slot()
    start(zc, zc_in, sem_c, zs[1])

    def z_half(ref, which):
        return ref.at[pl.ds(pl.multiple_of(which * HALF_M, 8), HALF_M)]

    start(z_half(zm, c), z_half(zm_in, c), sem_m, zs[1])

    gather_xg.forward()
    gather_xg.finish()
    xsuf_g[3] = eye
    xsuf_g[2] = xg[3]
    xsuf_g[1] = dot(xg[3], xg[2])
    xsuf_g[0] = dot(xsuf_g[1], xg[1])
    yg[y] = dot(xsuf_g[0], xg[0])
    gather_yg = Gather(yg, HALF_M, y, ys, (1, 3, 2))
    gather_yg.start()

    arrived(zc_in, sem_c)
    va[...] = dot(zc_in[...], zm[...]) + zc[...]
    start(va, va_in.at[0], sem_v1, zs[1])
    start(va, va_in.at[1], sem_v2, zs[2])
    arrived(z_half(zm_in, c), sem_m)
    start(z_half(zm_in, c), z_half(zm_in, c), sem_m2, sibling)

    ypre[0] = pack(eye, jnp.zeros((K, W), F32))
    ypre[1] = yf[0]
    ypre[3] = compose(ypre[2], yf[2])

    gather_xh.forward()
    gather_xh.finish()
    xsuf_h[3] = jnp.zeros((ROWS, W), F32)
    xsuf_h[2] = compose(xpre[3], xh[3])
    xsuf_h[1] = dot(xsuf_h[2], xg[2]) + compose(xpre[2], xh[2])
    xsuf_h[0] = dot(xsuf_h[1], xg[1]) + compose(xf[0], xh[1])
    row_h = dot(xsuf_h[0], xg[0]) + xh[0]
    row_h = compose(ypre[y], row_h)

    arrived(z_half(zm_in, 1 - c), sem_m2)
    arrived(va_in.at[0], sem_v1)
    arrived(va_in.at[1], sem_v2)
    last = dot(va_in[1], zm_in[...]) + zc_in[...]
    entering = jnp.where(z == 0, 0.0, jnp.where(z == 1, zc_in[...], jnp.where(z == 2, va_in[0], last)))

    er[y] = apply(entering, row_h)
    share_er = Share(er, y, ys)
    share_er.start()

    entering = apply(entering, ypre[y])
    dev_h[...] = dot(xsuf_h[x], dev_g[...]) + dev_h[...]
    dev_g[...] = dot(xsuf_g[x], dev_g[...])
    x1 = apply(entering, y1s[...]) - apply(entering, dev_h[...])
    x0 = apply(entering, y0s[...]) - dot(x1, lower[1])

    gather_yg.forward()
    gather_yg.finish()
    ysuf_g[3] = eye
    ysuf_g[2] = yg[3]
    ysuf_g[1] = dot(yg[3], yg[2])
    ysuf_g[0] = dot(ysuf_g[1], yg[1])
    zg[z] = dot(ysuf_g[0], yg[0])
    gather_zg = Gather(zg, HALF_M, z, zs, (3, 2))
    gather_zg.start()

    share_er.finish()
    ysuf_e[3] = jnp.zeros((K, W), F32)
    ysuf_e[2] = er[3]
    ysuf_e[1] = dot(er[3], yg[2]) + er[2]
    ysuf_e[0] = dot(ysuf_e[1], yg[1]) + er[1]
    ep[z] = dot(ysuf_e[0], yg[0]) + er[0]

    share_ep = Share(ep, z, zs)
    share_ep.start()
    to_w1 = dot(ysuf_g[y], dev_g[...])
    to_w0 = dot(to_w1, lower[1])
    from_row = dot(ysuf_e[y], dev_g[...])
    x1 = x1 - from_row
    x0 = x0 + dot(from_row, lower[1])
    gather_zg.forward()
    gather_zg.finish()
    share_ep.finish()
    two = dot(ep[3], zg[2]) + ep[2]
    three = dot(two, zg[1]) + ep[1]
    entering = jnp.where(z == 3, 0.0, jnp.where(z == 2, ep[3], jnp.where(z == 1, two, three)))
    x1 = x1 - dot(entering, to_w1)
    x0 = x0 + dot(entering, to_w0)

    both = jnp.concatenate([x0, x1], axis=1)
    gram = lax.dot_general(both, both, (((1,), (1,)), ((), ())), precision=HIGH, preferred_element_type=F32)
    gsum[c] = jnp.concatenate([gram[0 : K // 2], gram[K // 2 : K]], axis=1)
    sem = slot()
    start(gsum.at[c], gsum.at[c], sem, sibling)
    arrived(gsum.at[1 - c], sem)
    gx[x] = gsum[0] + gsum[1]
    total = gx
    for ref, place, peers, after in ((gx, x, xs, (gy, y)), (gy, y, ys, (gz, z)), (gz, z, zs, None)):
        share = Share(ref, place, peers)
        share.start()
        share.finish()
        total = (ref[0] + ref[1]) + (ref[2] + ref[3])
        if after is not None:
            after[0][after[1]] = total
    total = total / (256 * W)
    gram = jnp.concatenate([total[:, 0:K], total[:, K : 2 * K]], axis=0)
    r, inverse = factor(gram)
    r_factor[...] = r
    basis[0] = dot(inverse, x0)
    basis[1] = dot(inverse, x1)
    for copy in sent:
        copy.wait_send()


def on_device(sketch, inv_diag, upper, lower):
    def buf(*shape):
        return pltpu.VMEM(shape, F32)

    affine = (ROWS, W)
    vmem = pl.BlockSpec(memory_space=pltpu.VMEM)
    scratch = [
        buf(*affine), buf(2, *affine), buf(2, W, W), buf(2, *affine), buf(*affine), buf(*affine), buf(W, W), buf(*affine),
        buf(4, *affine), buf(4, W, W), buf(4, *affine), buf(4, *affine), buf(4, *affine), buf(4, W, W),
        buf(4, *affine), buf(4, W, W), buf(4, *affine), buf(4, W, W),
        buf(K, W), buf(W, W), buf(K, W), buf(W, W), buf(K, W), buf(2, K, W), buf(4, W, W),
        buf(4, K, W), buf(4, K, W), buf(4, K, W),
        buf(2, K // 2, 2 * K), buf(4, K // 2, 2 * K), buf(4, K // 2, 2 * K), buf(4, K // 2, 2 * K),
        pltpu.SemaphoreType.DMA((SEMS,)), pltpu.SemaphoreType.DMA((SEMS,)),
    ]
    return pl.pallas_call(
        kernel,
        out_shape=(jax.ShapeDtypeStruct((2, K, W), F32), jax.ShapeDtypeStruct((K, K), F32)),
        in_specs=[vmem] * 4,
        out_specs=(vmem, vmem),
        scratch_shapes=scratch,
        compiler_params=pltpu.CompilerParams(
            collective_id=0, has_side_effects=True, vmem_limit_bytes=56 * 2**20
        ),
        name="sweeps",
    )(sketch, inv_diag, upper, lower)


def solution(mesh):
    placed = (P("chain", None, None),) * 4
    return jax.shard_map(
        on_device,
        mesh=mesh,
        in_specs=placed,
        out_specs=(P("chain", None, None), P()),
        check_vma=False,
    )
```

```python
import jax
import jax.numpy as jnp
from jax import lax
from jax.experimental import pallas as pl
from jax.experimental.pallas import tpu as pltpu
from jax.sharding import PartitionSpec as P

HIGH = lax.Precision.HIGHEST
MESH = pl.DeviceIdType.MESH
F32 = jnp.float32

W = 256
K = 64
HALF_M = 128
HALF_C = 32
HALF = HALF_M + HALF_C
ROWS = 2 * HALF
SEMS = 96


def dot(a, b):
    return jnp.dot(a, b, precision=HIGH, preferred_element_type=F32)


def mat(n):
    return jnp.concatenate([n[0:HALF_M], n[HALF : HALF + HALF_M]], axis=0)


def vec(n):
    return jnp.concatenate([n[HALF_M:HALF], n[HALF + HALF_M : ROWS]], axis=0)


def pack(m, c):
    return jnp.concatenate([m[0:HALF_M], c[0:HALF_C], m[HALF_M:W], c[HALF_C:K]], axis=0)


def add_vec(r, n):
    return jnp.concatenate(
        [
            r[0:HALF_M],
            r[HALF_M:HALF] + n[HALF_M:HALF],
            r[HALF : HALF + HALF_M],
            r[HALF + HALF_M : ROWS] + n[HALF + HALF_M : ROWS],
        ],
        axis=0,
    )


def compose(f, n):
    return add_vec(dot(f, mat(n)), n)


def apply(v, n):
    return dot(v, mat(n)) + vec(n)


def identity(rows, columns):
    return (
        lax.broadcasted_iota(jnp.int32, (rows, columns), 0) == lax.broadcasted_iota(jnp.int32, (rows, columns), 1)
    ).astype(F32)


def factor(gram):
    work = jnp.concatenate([gram, identity(K, K)], axis=1)
    count = K // 8
    blocks = [work[8 * b : 8 * b + 8] for b in range(count)]
    sub = lax.broadcasted_iota(jnp.int32, (8, 2 * K), 0)

    def wide(v):
        return jnp.broadcast_to(v, (8, 2 * K))

    out = []
    for b in range(count):
        columns = [{i: wide(blocks[i][:, 8 * b + j : 8 * b + j + 1]) for i in range(b, count)} for j in range(8)]
        corner = {(i, j): wide(columns[j][b][i : i + 1]) for j in range(8) for i in range(j, 8)}
        rows = [wide(blocks[b][j : j + 1]) for j in range(8)]
        scaled = []
        done = jnp.zeros((8, 2 * K), F32)
        pivots = jnp.ones((8, 2 * K), F32)
        for j in range(8):
            inverse = 1.0 / corner[j, j]
            scaled.append(rows[j] * inverse)
            pivots = jnp.where(sub == j, corner[j, j], pivots)
            done = jnp.where(sub == j, rows[j], done)
            for i in range(j + 1, 8):
                ratio = corner[i, j] * inverse
                rows[i] = rows[i] - ratio * rows[j]
                for n in range(i, 8):
                    corner[n, i] = corner[n, i] - corner[n, j] * ratio
                for n in range(b + 1, count):
                    columns[i][n] = columns[i][n] - columns[j][n] * ratio
        for i in range(b + 1, count):
            for j in range(8):
                blocks[i] = blocks[i] - columns[j][i] * scaled[j]
        out.append(done * lax.rsqrt(pivots))
    out = jnp.concatenate(out, axis=0)
    upper = jnp.where(
        lax.broadcasted_iota(jnp.int32, (K, K), 0) <= lax.broadcasted_iota(jnp.int32, (K, K), 1), out[:, 0:K], 0.0
    )
    return upper, out[:, K : 2 * K]


def kernel(
    sketch_in, inv_diag_in, upper_in, lower_in, basis, r_factor,
    sketch, inv_diag, upper, lower, own0, fc, gc, hc, y0s, y1s, dev_g, dev_h,
    xf, xg, xh, xpre, xsuf_h, xsuf_g, yf, yg, ypre, ysuf_g, row_h,
    zf, zc_in, zm_in, va, va_in, zg, entry, er, ep, ysuf_e, ends, tops, gown, gin, gx, gyz, gtot,
    send, recv, load,
):
    me = lax.axis_index("chain")
    c = lax.rem(me, 2)
    x = lax.rem(me // 2, 4)
    y = lax.rem(me // 8, 4)
    z = me // 32

    loads = []
    for src, dst in ((inv_diag_in, inv_diag), (upper_in, upper), (lower_in, lower)):
        for i in (0, 1):
            loads.append(pltpu.make_async_copy(src.at[i], dst.at[i], load.at[len(loads)]))
    loads.append(pltpu.make_async_copy(sketch_in, sketch, load.at[6]))
    for i in (0, 2, 6, 1, 3, 4, 5):
        loads[i].start()

    def at(zz, yy, xx, cc):
        return ((zz * 4 + yy) * 4 + xx) * 2 + cc

    def turn(place, k):
        return lax.rem(place + k, 4)

    sibling = at(z, y, x, 1 - c)
    xs = [at(z, y, turn(x, k), c) for k in range(4)]
    across = {(k, n): at(turn(z, k), turn(y, n), x, c) for k in (0, 1, 3, 2) for n in (0, 1, 3, 2) if (k, n) != (0, 0)}
    ys = [None, *(across[0, n] for n in (1, 2, 3))]
    zs = [None, *(across[k, 0] for k in (1, 2, 3))]

    barrier = pltpu.get_barrier_semaphore()
    for other in (sibling, *xs[1:], *across.values()):
        pl.semaphore_signal(barrier, inc=1, device_id=(other,), device_id_type=MESH)

    sent = []
    used = [0]

    def slot():
        used[0] += 1
        assert used[0] <= SEMS
        return used[0] - 1

    def start(src, dst, i, other):
        copy = pltpu.make_async_remote_copy(
            src_ref=src, dst_ref=dst, send_sem=send.at[i], recv_sem=recv.at[i], device_id=(other,), device_id_type=MESH
        )
        copy.start()
        sent.append(copy)

    def arrived(dst, i):
        pltpu.make_async_remote_copy(
            src_ref=dst, dst_ref=dst, send_sem=send.at[i], recv_sem=recv.at[i], device_id=(sibling,), device_id_type=MESH
        ).wait_recv()

    def drain(count):
        for copy in sent[:count]:
            copy.wait_send()
        del sent[:count]

    def rows_of(which, rows):
        return pl.ds(pl.multiple_of(which * rows, 8), rows)

    mine, others = rows_of(c, HALF), rows_of(1 - c, HALF)
    my_vec = pl.ds(pl.multiple_of(c * HALF + HALF_M, 8), HALF_C)

    def compose_half(f, n, which):
        r = dot(f, mat(n[...]))
        return jnp.concatenate(
            [r[0:HALF_M], r[HALF_M:HALF] + n[pl.ds(pl.multiple_of(which * HALF + HALF_M, 8), HALF_C)]], axis=0
        )

    class Gather:
        def __init__(self, ref, rows, place, peers, steps):
            self.ref, self.rows, self.place, self.peers, self.steps = ref, rows, place, peers, steps
            self.first = {k: slot() for k in steps}
            self.second = {k: slot() for k in steps}

        def part(self, k, which):
            return self.ref.at[turn(self.place, 4 - k), rows_of(which, self.rows)]

        def start(self):
            for k in self.steps:
                start(self.part(0, c), self.part(0, c), self.first[k], self.peers[k])

        def forward(self, between=None):
            for k in self.steps:
                arrived(self.part(k, c), self.first[k])
                start(self.part(k, c), self.part(k, c), self.second[k], sibling)
                if between is not None and k == self.steps[0]:
                    between()

        def finish(self):
            for k in self.steps:
                arrived(self.part(k, 1 - c), self.second[k])

    class Share:
        def __init__(self, ref, place, peers):
            self.ref, self.place, self.peers = ref, place, peers
            self.sems = {k: slot() for k in (1, 3, 2)}

        def start(self):
            for k in (1, 3, 2):
                start(self.ref.at[self.place], self.ref.at[self.place], self.sems[k], self.peers[k])

        def finish(self):
            for k in (1, 3, 2):
                arrived(self.ref.at[turn(self.place, 4 - k)], self.sems[k])

    def swap(ref, i):
        start(ref.at[c], ref.at[c], i, sibling)

    for i in (0, 2, 6):
        loads[i].wait()
    y0s[...] = dot(pack(-upper[0], sketch[0]), inv_diag[0])
    for i in (1, 3):
        loads[i].wait()
    own0[...] = dot(pack(-upper[1], sketch[1]), inv_diag[1])
    y1s[...] = compose(y0s[...], own0[...])
    fc[c] = y1s[...]
    pl.semaphore_wait(barrier, 1 + 3 + 15)
    sem_f, sem_g, sem_h = slot(), slot(), slot()
    swap(fc, sem_f)
    for i in (4, 5):
        loads[i].wait()
    gc[c] = dot(lower[1], lower[0])
    swap(gc, sem_g)
    arrived(fc.at[1 - c], sem_f)

    xf[x, mine] = compose_half(fc[0, mine], fc.at[1], c)
    gather_xf = Gather(xf, HALF, x, xs, (1, 3, 2))
    gather_xf.start()
    xf[x, others] = compose_half(fc[0, others], fc.at[1], 1 - c)

    hc[c] = dot(y0s[...] - dot(y1s[...], lower[1]), lower[0])
    swap(hc, sem_h)
    arrived(gc.at[1 - c], sem_g)
    xg[x] = dot(gc[1], gc[0])
    arrived(hc.at[1 - c], sem_h)
    late = compose(fc[0], hc[1])
    xh[x] = dot(late, gc[0]) + hc[0]
    second = c == 1
    eye = identity(W, W)
    dev_g[...] = jnp.where(second, eye, gc[1])
    dev_h[...] = jnp.where(second, 0.0, late)
    y0s[...] = jnp.where(second, compose(fc[0], y0s[...]), y0s[...])
    y1s[...] = jnp.where(second, xf[x], y1s[...])
    drain(3)

    gather_xg = Gather(xg, HALF_M, x, xs, (1, 3, 2))
    gather_xf.forward(gather_xg.start)
    gather_xf.finish()
    q23 = compose(xf[2], xf[3])
    xsuf_h[0] = q23
    xpre[2, mine] = compose_half(xf[0, mine], xf.at[1], c)
    yf[y, mine] = compose_half(xpre[2, mine], xsuf_h.at[0], c)

    gather_yf = Gather(yf, HALF, y, ys, (1, 3, 2))
    gather_yf.start()
    xpre[2, others] = compose_half(xf[0, others], xf.at[1], 1 - c)
    yf[y, others] = compose_half(xpre[2, others], xsuf_h.at[0], 1 - c)
    xpre[0] = pack(eye, jnp.zeros((K, W), F32))
    xpre[1] = xf[0]
    xpre[3] = compose(xpre[2], xf[2])
    y0s[...] = compose(xpre[x], y0s[...])
    y1s[...] = compose(xpre[x], y1s[...])
    dev_h[...] = compose(xpre[x], dev_h[...])
    drain(9)

    gather_xh = Gather(xh, HALF, x, xs, (1, 3, 2))
    gather_yf.forward(gather_xh.start)
    gather_xg.forward()
    gather_yf.finish()
    q23 = compose(yf[2], yf[3])
    ypre[2] = compose(yf[0], yf[1])
    zf[...] = compose(ypre[2], q23)

    sem_c, sem_m, sem_m2, sem_v1, sem_v2 = slot(), slot(), slot(), slot(), slot()
    start(zf.at[my_vec], zc_in, sem_c, zs[1])
    my_m = pl.ds(pl.multiple_of(c * HALF, 8), HALF_M)
    my_half, other_half = rows_of(c, HALF_M), rows_of(1 - c, HALF_M)
    start(zf.at[my_m], zm_in.at[my_half], sem_m, zs[1])

    gather_xg.finish()
    xsuf_g[3] = eye
    xsuf_g[2] = xg[3]
    xsuf_g[1] = dot(xg[3], xg[2])
    xsuf_g[0] = dot(xsuf_g[1], xg[1])
    yg[y] = dot(xsuf_g[0], xg[0])
    gather_yg = Gather(yg, HALF_M, y, ys, (1, 3, 2))
    gather_yg.start()
    ypre[0] = pack(eye, jnp.zeros((K, W), F32))
    ypre[1] = yf[0]

    arrived(zc_in, sem_c)
    plane_m = mat(zf[...])
    va[...] = dot(zc_in[...], plane_m) + zf[my_vec]
    start(va, va_in.at[0], sem_v1, zs[1])
    start(va, va_in.at[1], sem_v2, zs[2])
    arrived(zm_in.at[my_half], sem_m)
    start(zm_in.at[my_half], zm_in.at[my_half], sem_m2, sibling)

    gather_xh.forward()
    ypre[3] = compose(ypre[2], yf[2])
    gather_xh.finish()
    xsuf_h[3] = jnp.zeros((ROWS, W), F32)
    xsuf_h[2] = compose(xpre[3], xh[3])
    xsuf_h[1] = dot(xsuf_h[2], xg[2]) + compose(xpre[2], xh[2])
    xsuf_h[0] = dot(xsuf_h[1], xg[1]) + compose(xf[0], xh[1])
    row_h[...] = compose(ypre[y], dot(xsuf_h[0], xg[0]) + xh[0])
    drain(18)

    arrived(zm_in.at[other_half], sem_m2)
    arrived(va_in.at[0], sem_v1)
    arrived(va_in.at[1], sem_v2)
    last = dot(va_in[1], zm_in[...]) + zc_in[...]
    start_row = jnp.where(z == 0, 0.0, jnp.where(z == 1, zc_in[...], jnp.where(z == 2, va_in[0], last)))

    er[y] = dot(start_row, mat(row_h[...])) + row_h[my_vec]
    share_er = Share(er, y, ys)
    share_er.start()
    entry[c] = start_row
    sem_entry = slot()
    swap(entry, sem_entry)

    dev_h[...] = dot(xsuf_h[x], dev_g[...]) + dev_h[...]
    dev_g[...] = dot(xsuf_g[x], dev_g[...])
    arrived(entry.at[1 - c], sem_entry)
    row = apply(jnp.concatenate([entry[0], entry[1]], axis=0), ypre[y])
    x1 = apply(row, y1s[...]) - apply(row, dev_h[...])
    x0 = apply(row, y0s[...]) - dot(x1, lower[1])

    gather_yg.forward()
    gather_yg.finish()
    ysuf_g[3] = eye
    ysuf_g[2] = yg[3]
    ysuf_g[1] = dot(yg[3], yg[2])
    ysuf_g[0] = dot(ysuf_g[1], yg[1])
    zg[z] = dot(ysuf_g[0], yg[0])
    gather_zg = Gather(zg, HALF_M, z, zs, (3, 2))
    gather_zg.start()

    share_er.finish()
    ysuf_e[3] = jnp.zeros((HALF_C, W), F32)
    ysuf_e[2] = er[3]
    ysuf_e[1] = dot(er[3], yg[2]) + er[2]
    ysuf_e[0] = dot(ysuf_e[1], yg[1]) + er[1]
    ep[z] = dot(ysuf_e[0], yg[0]) + er[0]

    share_ep = Share(ep, z, zs)
    share_ep.start()
    ends[c] = ysuf_e[y]
    sem_ends = slot()
    swap(ends, sem_ends)
    to_w1 = dot(ysuf_g[y], dev_g[...])
    to_w0 = dot(to_w1, lower[1])
    arrived(ends.at[1 - c], sem_ends)
    from_row = dot(jnp.concatenate([ends[0], ends[1]], axis=0), dev_g[...])
    x1 = x1 - from_row
    x0 = x0 + dot(from_row, lower[1])
    drain(23)
    gather_zg.forward()
    gather_zg.finish()
    share_ep.finish()
    two = dot(ep[3], zg[2]) + ep[2]
    three = dot(two, zg[1]) + ep[1]
    tops[c] = jnp.where(z == 3, 0.0, jnp.where(z == 2, ep[3], jnp.where(z == 1, two, three)))
    sem_tops = slot()
    swap(tops, sem_tops)
    arrived(tops.at[1 - c], sem_tops)
    top = jnp.concatenate([tops[0], tops[1]], axis=0)
    x1 = x1 - dot(top, to_w1)
    x0 = x0 + dot(top, to_w0)

    both = jnp.concatenate([x0, x1], axis=1)
    gram = lax.dot_general(both, both, (((1,), (1,)), ((), ())), precision=HIGH, preferred_element_type=F32)
    gram = jnp.concatenate([gram[0 : K // 2], gram[K // 2 : K]], axis=1)
    gown[0] = gram[0 : K // 4]
    gown[1] = gram[K // 4 : K // 2]
    sem_gin, sem_gtot = slot(), slot()
    start(gown.at[1 - c], gin, sem_gin, sibling)
    arrived(gin, sem_gin)
    gx[x] = gown[c] + gin[...]
    share_gx = Share(gx, x, xs)
    share_gx.start()
    drain(9)
    share_gx.finish()
    own = z * 4 + y
    gyz[own] = (gx[0] + gx[1]) + (gx[2] + gx[3])
    sems = {step: slot() for step in across}
    for step, other in across.items():
        start(gyz.at[own], gyz.at[own], sems[step], other)
    drain(3)
    for (k, n), i in sems.items():
        arrived(gyz.at[turn(z, 4 - k) * 4 + turn(y, 4 - n)], i)
    terms = [gyz[i] for i in range(16)]
    while len(terms) > 1:
        terms = [terms[i] + terms[i + 1] for i in range(0, len(terms), 2)]
    gtot[c] = terms[0]
    swap(gtot, sem_gtot)
    drain(15)
    arrived(gtot.at[1 - c], sem_gtot)
    total = jnp.concatenate([gtot[0], gtot[1]], axis=0) / (256 * W)
    r, inverse = factor(jnp.concatenate([total[:, 0:K], total[:, K : 2 * K]], axis=0))
    r_factor[...] = r
    basis[0] = dot(inverse, x0)
    basis[1] = dot(inverse, x1)
    drain(len(sent))


def on_device(sketch, inv_diag, upper, lower):
    def buf(*shape):
        return pltpu.VMEM(shape, F32)

    affine = (ROWS, W)
    part = (HALF_C, W)
    quarter = (K // 4, 2 * K)
    vmem = pl.BlockSpec(memory_space=pltpu.VMEM)
    scratch = [
        buf(2, K, W), buf(2, W, W), buf(2, W, W), buf(2, W, W), buf(*affine), buf(2, *affine), buf(2, W, W), buf(2, *affine),
        buf(*affine), buf(*affine), buf(W, W), buf(*affine),
        buf(4, *affine), buf(4, W, W), buf(4, *affine), buf(4, *affine), buf(4, *affine), buf(4, W, W),
        buf(4, *affine), buf(4, W, W), buf(4, *affine), buf(4, W, W), buf(*affine),
        buf(*affine), buf(*part), buf(W, W), buf(*part), buf(2, *part), buf(4, W, W), buf(2, *part),
        buf(4, *part), buf(4, *part), buf(4, *part), buf(2, *part), buf(2, *part),
        buf(2, *quarter), buf(*quarter), buf(4, *quarter), buf(16, *quarter), buf(2, *quarter),
        pltpu.SemaphoreType.DMA((SEMS,)), pltpu.SemaphoreType.DMA((SEMS,)), pltpu.SemaphoreType.DMA((7,)),
    ]
    return pl.pallas_call(
        kernel,
        out_shape=(jax.ShapeDtypeStruct((2, K, W), F32), jax.ShapeDtypeStruct((K, K), F32)),
        in_specs=[pl.BlockSpec(memory_space=pl.ANY)] * 4,
        out_specs=(vmem, vmem),
        scratch_shapes=scratch,
        compiler_params=pltpu.CompilerParams(
            collective_id=0, has_side_effects=True, vmem_limit_bytes=56 * 2**20
        ),
        name="sweeps",
    )(sketch, inv_diag, upper, lower)


def solution(mesh):
    placed = (P("chain", None, None),) * 4
    return jax.shard_map(
        on_device,
        mesh=mesh,
        in_specs=placed,
        out_specs=(P("chain", None, None), P()),
        check_vma=False,
    )
```

```python
import jax
import jax.numpy as jnp
from jax import lax
from jax.experimental import pallas as pl
from jax.experimental.pallas import tpu as pltpu
from jax.sharding import PartitionSpec as P

HIGH = lax.Precision.HIGHEST
MESH = pl.DeviceIdType.MESH
F32 = jnp.float32

W = 256
K = 64
HALF_M = 128
HALF_C = 32
HALF = HALF_M + HALF_C
ROWS = 2 * HALF
SEMS = 128


def dot(a, b):
    return jnp.dot(a, b, precision=HIGH, preferred_element_type=F32)


def mat(n):
    return jnp.concatenate([n[0:HALF_M], n[HALF : HALF + HALF_M]], axis=0)


def vec(n):
    return jnp.concatenate([n[HALF_M:HALF], n[HALF + HALF_M : ROWS]], axis=0)


def pack(m, c):
    return jnp.concatenate([m[0:HALF_M], c[0:HALF_C], m[HALF_M:W], c[HALF_C:K]], axis=0)


def add_vec(r, n):
    return jnp.concatenate(
        [
            r[0:HALF_M],
            r[HALF_M:HALF] + n[HALF_M:HALF],
            r[HALF : HALF + HALF_M],
            r[HALF + HALF_M : ROWS] + n[HALF + HALF_M : ROWS],
        ],
        axis=0,
    )


def compose(f, n):
    return add_vec(dot(f, mat(n)), n)


def apply(v, n):
    return dot(v, mat(n)) + vec(n)


def identity(rows, columns):
    return (
        lax.broadcasted_iota(jnp.int32, (rows, columns), 0) == lax.broadcasted_iota(jnp.int32, (rows, columns), 1)
    ).astype(F32)


def factor(gram):
    work = jnp.concatenate([gram, identity(K, K)], axis=1)
    count = K // 8
    blocks = [work[8 * b : 8 * b + 8] for b in range(count)]
    sub = lax.broadcasted_iota(jnp.int32, (8, 2 * K), 0)

    def wide(v):
        return jnp.broadcast_to(v, (8, 2 * K))

    out = []
    for b in range(count):
        columns = [{i: wide(blocks[i][:, 8 * b + j : 8 * b + j + 1]) for i in range(b, count)} for j in range(8)]
        corner = {(i, j): wide(columns[j][b][i : i + 1]) for j in range(8) for i in range(j, 8)}
        rows = [wide(blocks[b][j : j + 1]) for j in range(8)]
        scaled = []
        done = jnp.zeros((8, 2 * K), F32)
        pivots = jnp.ones((8, 2 * K), F32)
        for j in range(8):
            inverse = 1.0 / corner[j, j]
            scaled.append(rows[j] * inverse)
            pivots = jnp.where(sub == j, corner[j, j], pivots)
            done = jnp.where(sub == j, rows[j], done)
            for i in range(j + 1, 8):
                ratio = corner[i, j] * inverse
                rows[i] = rows[i] - ratio * rows[j]
                for n in range(i, 8):
                    corner[n, i] = corner[n, i] - corner[n, j] * ratio
                for n in range(b + 1, count):
                    columns[i][n] = columns[i][n] - columns[j][n] * ratio
        for i in range(b + 1, count):
            for j in range(8):
                blocks[i] = blocks[i] - columns[j][i] * scaled[j]
        out.append(done * lax.rsqrt(pivots))
    out = jnp.concatenate(out, axis=0)
    upper = jnp.where(
        lax.broadcasted_iota(jnp.int32, (K, K), 0) <= lax.broadcasted_iota(jnp.int32, (K, K), 1), out[:, 0:K], 0.0
    )
    return upper, out[:, K : 2 * K]


def kernel(
    sketch_in, inv_diag_in, upper_in, lower_in, basis, r_factor,
    sketch, inv_diag, upper, lower, own0, fc, gc, hc, y0s, y1s, dev_g, dev_h,
    xf, xg, xh, xpre, xsuf_h, xsuf_g, yf, yg, ypre, ysuf_g, row_h,
    zf, zc_in, zm_in, va, va_in, zg, entry, er, ep, ysuf_e, ends, tops, gown, gin, gx, gyz, gtot,
    send, recv, load,
):
    me = lax.axis_index("chain")
    c = lax.rem(me, 2)
    x = lax.rem(me // 2, 4)
    y = lax.rem(me // 8, 4)
    z = me // 32

    loads = []
    for src, dst in ((inv_diag_in, inv_diag), (upper_in, upper), (lower_in, lower)):
        for i in (0, 1):
            loads.append(pltpu.make_async_copy(src.at[i], dst.at[i], load.at[len(loads)]))
    loads.append(pltpu.make_async_copy(sketch_in, sketch, load.at[6]))
    for i in (0, 2, 6, 1, 3, 4, 5):
        loads[i].start()

    def at(zz, yy, xx, cc):
        return ((zz * 4 + yy) * 4 + xx) * 2 + cc

    def turn(place, k):
        return lax.rem(place + k, 4)

    sibling = at(z, y, x, 1 - c)
    xs = [at(z, y, turn(x, k), c) for k in range(4)]
    across = {(k, n): at(turn(z, k), turn(y, n), x, c) for k in (0, 1, 3, 2) for n in (0, 1, 3, 2) if (k, n) != (0, 0)}
    ys = [None, *(across[0, n] for n in (1, 2, 3))]
    zs = [None, *(across[k, 0] for k in (1, 2, 3))]

    barrier = pltpu.get_barrier_semaphore()
    for other in (sibling, *xs[1:], *across.values()):
        pl.semaphore_signal(barrier, inc=1, device_id=(other,), device_id_type=MESH)

    sent = []
    used = [0]

    def slot():
        used[0] += 1
        assert used[0] <= SEMS
        return used[0] - 1

    def start(src, dst, i, other):
        copy = pltpu.make_async_remote_copy(
            src_ref=src, dst_ref=dst, send_sem=send.at[i], recv_sem=recv.at[i], device_id=(other,), device_id_type=MESH
        )
        copy.start()
        sent.append(copy)

    def arrived(dst, i):
        pltpu.make_async_remote_copy(
            src_ref=dst, dst_ref=dst, send_sem=send.at[i], recv_sem=recv.at[i], device_id=(sibling,), device_id_type=MESH
        ).wait_recv()

    def drain(count):
        for copy in sent[:count]:
            copy.wait_send()
        del sent[:count]

    def rows_of(which, rows):
        return pl.ds(pl.multiple_of(which * rows, 8), rows)

    mine, others = rows_of(c, HALF), rows_of(1 - c, HALF)
    my_vec = pl.ds(pl.multiple_of(c * HALF + HALF_M, 8), HALF_C)

    def compose_half(f, n, which):
        r = dot(f, mat(n[...]))
        return jnp.concatenate(
            [r[0:HALF_M], r[HALF_M:HALF] + n[pl.ds(pl.multiple_of(which * HALF + HALF_M, 8), HALF_C)]], axis=0
        )

    class Gather:
        def __init__(self, ref, rows, place, peers, steps):
            self.ref, self.rows, self.place, self.peers, self.steps = ref, rows, place, peers, steps
            self.first = {k: slot() for k in steps}
            self.second = {k: slot() for k in steps}

        def part(self, k, which):
            return self.ref.at[turn(self.place, 4 - k), rows_of(which, self.rows)]

        def start(self):
            for k in self.steps:
                start(self.part(0, c), self.part(0, c), self.first[k], self.peers[k])

        def forward(self, between=None):
            for k in self.steps:
                arrived(self.part(k, c), self.first[k])
                start(self.part(k, c), self.part(k, c), self.second[k], sibling)
                if between is not None and k == self.steps[0]:
                    between()

        def finish(self):
            for k in self.steps:
                arrived(self.part(k, 1 - c), self.second[k])

    class Relay:
        cut = HALF // 2

        def __init__(self, ref, place, peers):
            self.ref, self.place, self.peers = ref, place, peers
            self.first = {(k, p): slot() for k in (1, 3, 2) for p in (0, 1)}
            self.second = {(k, p): slot() for k in (1, 3, 2) for p in (0, 1)}

        def part(self, k, p, which):
            at_row = pl.multiple_of(which * HALF + p * self.cut, 8)
            return self.ref.at[turn(self.place, 4 - k), pl.ds(at_row, self.cut)]

        def start(self):
            for k, p in ((1, 0), (3, 1), (1, 1), (3, 0)):
                start(self.part(0, p, c), self.part(0, p, c), self.first[k, p], self.peers[k])

        def inside(self, k, p):
            start(self.part(k, p, c), self.part(k, p, c), self.second[k, p], sibling)

        def relay(self):
            for k, p in ((1, 0), (3, 1)):
                arrived(self.part(k, p, c), self.first[k, p])
                start(self.part(k, p, c), self.part(k, p, c), self.first[2, p], self.peers[k])
            for k, p in ((1, 0), (3, 1)):
                self.inside(k, p)

        def forward(self):
            for k, p in ((1, 1), (3, 0), (2, 0), (2, 1)):
                arrived(self.part(k, p, c), self.first[k, p])
                self.inside(k, p)

        def finish(self):
            for k, p in self.second:
                arrived(self.part(k, p, 1 - c), self.second[k, p])

    class Share:
        def __init__(self, ref, place, peers):
            self.ref, self.place, self.peers = ref, place, peers
            self.sems = {k: slot() for k in (1, 3, 2)}

        def start(self):
            for k in (1, 3, 2):
                start(self.ref.at[self.place], self.ref.at[self.place], self.sems[k], self.peers[k])

        def finish(self):
            for k in (1, 3, 2):
                arrived(self.ref.at[turn(self.place, 4 - k)], self.sems[k])

    def swap(ref, i):
        start(ref.at[c], ref.at[c], i, sibling)

    for i in (0, 2, 6):
        loads[i].wait()
    y0s[...] = dot(pack(-upper[0], sketch[0]), inv_diag[0])
    for i in (1, 3):
        loads[i].wait()
    own0[...] = dot(pack(-upper[1], sketch[1]), inv_diag[1])
    y1s[...] = compose(y0s[...], own0[...])
    fc[c] = y1s[...]
    pl.semaphore_wait(barrier, 1 + 3 + 15)
    sem_f, sem_g, sem_h = slot(), slot(), slot()
    swap(fc, sem_f)
    for i in (4, 5):
        loads[i].wait()
    gc[c] = dot(lower[1], lower[0])
    swap(gc, sem_g)
    arrived(fc.at[1 - c], sem_f)

    xf[x, mine] = compose_half(fc[0, mine], fc.at[1], c)
    gather_xf = Relay(xf, x, xs)
    gather_xf.start()
    xf[x, others] = compose_half(fc[0, others], fc.at[1], 1 - c)
    hc[c] = dot(y0s[...] - dot(y1s[...], lower[1]), lower[0])
    swap(hc, sem_h)
    arrived(gc.at[1 - c], sem_g)
    xg[x] = dot(gc[1], gc[0])
    gather_xf.relay()

    gather_xg = Gather(xg, HALF_M, x, xs, (1, 3, 2))
    gather_xg.start()
    arrived(hc.at[1 - c], sem_h)
    late = compose(fc[0], hc[1])
    xh[x] = dot(late, gc[0]) + hc[0]
    second = c == 1
    eye = identity(W, W)
    dev_g[...] = jnp.where(second, eye, gc[1])
    dev_h[...] = jnp.where(second, 0.0, late)
    y0s[...] = jnp.where(second, compose(fc[0], y0s[...]), y0s[...])
    y1s[...] = jnp.where(second, xf[x], y1s[...])
    drain(3)
    gather_xf.forward()
    gather_xf.finish()
    q23 = compose(xf[2], xf[3])
    xsuf_h[0] = q23
    xpre[2, mine] = compose_half(xf[0, mine], xf.at[1], c)
    yf[y, mine] = compose_half(xpre[2, mine], xsuf_h.at[0], c)

    gather_yf = Relay(yf, y, ys)
    gather_yf.start()
    gather_xh = Gather(xh, HALF, x, xs, (1, 3, 2))
    gather_xh.start()
    xpre[2, others] = compose_half(xf[0, others], xf.at[1], 1 - c)
    yf[y, others] = compose_half(xpre[2, others], xsuf_h.at[0], 1 - c)
    xpre[0] = pack(eye, jnp.zeros((K, W), F32))
    xpre[1] = xf[0]
    xpre[3] = compose(xpre[2], xf[2])
    y0s[...] = compose(xpre[x], y0s[...])
    y1s[...] = compose(xpre[x], y1s[...])
    drain(12)
    gather_yf.relay()

    gather_xg.forward()
    dev_h[...] = compose(xpre[x], dev_h[...])
    gather_xg.finish()
    xsuf_g[3] = eye
    xsuf_g[2] = xg[3]
    xsuf_g[1] = dot(xg[3], xg[2])
    xsuf_g[0] = dot(xsuf_g[1], xg[1])
    yg[y] = dot(xsuf_g[0], xg[0])
    gather_yg = Gather(yg, HALF_M, y, ys, (1, 3, 2))
    gather_yg.start()
    gather_yf.forward()
    gather_yf.finish()
    q23 = compose(yf[2], yf[3])
    xsuf_h[0] = q23
    ypre[2, mine] = compose_half(yf[0, mine], yf.at[1], c)
    zf[my_vec] = dot(ypre[2, my_vec], mat(q23)) + xsuf_h[0, my_vec]

    sem_c, sem_m, sem_m2, sem_v1, sem_v2 = slot(), slot(), slot(), slot(), slot()
    start(zf.at[my_vec], zc_in, sem_c, zs[1])
    my_m = pl.ds(pl.multiple_of(c * HALF, 8), HALF_M)
    other_m = pl.ds(pl.multiple_of((1 - c) * HALF, 8), HALF_M)
    my_half, other_half = rows_of(c, HALF_M), rows_of(1 - c, HALF_M)
    zf[my_m] = dot(ypre[2, my_m], mat(q23))
    start(zf.at[my_m], zm_in.at[my_half], sem_m, zs[1])
    ypre[2, others] = compose_half(yf[0, others], yf.at[1], 1 - c)
    zf[other_m] = dot(ypre[2, other_m], mat(q23))
    gather_xh.forward()
    ypre[0] = pack(eye, jnp.zeros((K, W), F32))
    ypre[1] = yf[0]
    gather_xh.finish()
    xsuf_h[3] = jnp.zeros((ROWS, W), F32)
    xsuf_h[2] = compose(xpre[3], xh[3])

    arrived(zc_in, sem_c)
    va[...] = dot(zc_in[...], mat(zf[...])) + zf[my_vec]
    start(va, va_in.at[0], sem_v1, zs[1])
    start(va, va_in.at[1], sem_v2, zs[2])
    arrived(zm_in.at[my_half], sem_m)
    start(zm_in.at[my_half], zm_in.at[my_half], sem_m2, sibling)

    xsuf_h[1] = dot(xsuf_h[2], xg[2]) + compose(xpre[2], xh[2])
    xsuf_h[0] = dot(xsuf_h[1], xg[1]) + compose(xf[0], xh[1])
    ypre[3] = compose(ypre[2], yf[2])
    row_h[...] = compose(ypre[y], dot(xsuf_h[0], xg[0]) + xh[0])
    drain(24)

    arrived(zm_in.at[other_half], sem_m2)
    arrived(va_in.at[0], sem_v1)
    arrived(va_in.at[1], sem_v2)
    last = dot(va_in[1], zm_in[...]) + zc_in[...]
    start_row = jnp.where(z == 0, 0.0, jnp.where(z == 1, zc_in[...], jnp.where(z == 2, va_in[0], last)))

    er[y] = dot(start_row, mat(row_h[...])) + row_h[my_vec]
    share_er = Share(er, y, ys)
    share_er.start()
    entry[c] = start_row
    sem_entry = slot()
    swap(entry, sem_entry)

    gather_yg.forward()
    gather_yg.finish()
    ysuf_g[3] = eye
    ysuf_g[2] = yg[3]
    ysuf_g[1] = dot(yg[3], yg[2])
    ysuf_g[0] = dot(ysuf_g[1], yg[1])
    zg[z] = dot(ysuf_g[0], yg[0])
    gather_zg = Gather(zg, HALF_M, z, zs, (3, 2))
    gather_zg.start()

    dev_h[...] = dot(xsuf_h[x], dev_g[...]) + dev_h[...]
    dev_g[...] = dot(xsuf_g[x], dev_g[...])
    arrived(entry.at[1 - c], sem_entry)
    row = apply(jnp.concatenate([entry[0], entry[1]], axis=0), ypre[y])
    x1 = apply(row, y1s[...]) - apply(row, dev_h[...])
    x0 = apply(row, y0s[...]) - dot(x1, lower[1])

    share_er.finish()
    ysuf_e[3] = jnp.zeros((HALF_C, W), F32)
    ysuf_e[2] = er[3]
    ysuf_e[1] = dot(er[3], yg[2]) + er[2]
    ysuf_e[0] = dot(ysuf_e[1], yg[1]) + er[1]
    ep[z] = dot(ysuf_e[0], yg[0]) + er[0]

    share_ep = Share(ep, z, zs)
    share_ep.start()
    ends[c] = ysuf_e[y]
    sem_ends = slot()
    swap(ends, sem_ends)
    to_w1 = dot(ysuf_g[y], dev_g[...])
    to_w0 = dot(to_w1, lower[1])
    arrived(ends.at[1 - c], sem_ends)
    from_row = dot(jnp.concatenate([ends[0], ends[1]], axis=0), dev_g[...])
    x1 = x1 - from_row
    x0 = x0 + dot(from_row, lower[1])
    drain(23)
    gather_zg.forward()
    gather_zg.finish()
    share_ep.finish()
    two = dot(ep[3], zg[2]) + ep[2]
    three = dot(two, zg[1]) + ep[1]
    tops[c] = jnp.where(z == 3, 0.0, jnp.where(z == 2, ep[3], jnp.where(z == 1, two, three)))
    sem_tops = slot()
    swap(tops, sem_tops)
    arrived(tops.at[1 - c], sem_tops)
    top = jnp.concatenate([tops[0], tops[1]], axis=0)
    x1 = x1 - dot(top, to_w1)
    x0 = x0 + dot(top, to_w0)

    both = jnp.concatenate([x0, x1], axis=1)
    gram = lax.dot_general(both, both, (((1,), (1,)), ((), ())), precision=HIGH, preferred_element_type=F32)
    gram = jnp.concatenate([gram[0 : K // 2], gram[K // 2 : K]], axis=1)
    gown[0] = gram[0 : K // 4]
    gown[1] = gram[K // 4 : K // 2]
    sem_gin, sem_gtot = slot(), slot()
    start(gown.at[1 - c], gin, sem_gin, sibling)
    arrived(gin, sem_gin)
    gx[x] = gown[c] + gin[...]
    share_gx = Share(gx, x, xs)
    share_gx.start()
    drain(9)
    share_gx.finish()
    own = z * 4 + y
    gyz[own] = (gx[0] + gx[1]) + (gx[2] + gx[3])
    sems = {step: slot() for step in across}
    for step, other in across.items():
        start(gyz.at[own], gyz.at[own], sems[step], other)
    drain(3)
    for (k, n), i in sems.items():
        arrived(gyz.at[turn(z, 4 - k) * 4 + turn(y, 4 - n)], i)
    terms = [gyz[i] for i in range(16)]
    while len(terms) > 1:
        terms = [terms[i] + terms[i + 1] for i in range(0, len(terms), 2)]
    gtot[c] = terms[0]
    swap(gtot, sem_gtot)
    drain(15)
    arrived(gtot.at[1 - c], sem_gtot)
    total = jnp.concatenate([gtot[0], gtot[1]], axis=0) / (256 * W)
    r, inverse = factor(jnp.concatenate([total[:, 0:K], total[:, K : 2 * K]], axis=0))
    r_factor[...] = r
    basis[0] = dot(inverse, x0)
    basis[1] = dot(inverse, x1)
    drain(len(sent))


def on_device(sketch, inv_diag, upper, lower):
    def buf(*shape):
        return pltpu.VMEM(shape, F32)

    affine = (ROWS, W)
    part = (HALF_C, W)
    quarter = (K // 4, 2 * K)
    vmem = pl.BlockSpec(memory_space=pltpu.VMEM)
    scratch = [
        buf(2, K, W), buf(2, W, W), buf(2, W, W), buf(2, W, W), buf(*affine), buf(2, *affine), buf(2, W, W), buf(2, *affine),
        buf(*affine), buf(*affine), buf(W, W), buf(*affine),
        buf(4, *affine), buf(4, W, W), buf(4, *affine), buf(4, *affine), buf(4, *affine), buf(4, W, W),
        buf(4, *affine), buf(4, W, W), buf(4, *affine), buf(4, W, W), buf(*affine),
        buf(*affine), buf(*part), buf(W, W), buf(*part), buf(2, *part), buf(4, W, W), buf(2, *part),
        buf(4, *part), buf(4, *part), buf(4, *part), buf(2, *part), buf(2, *part),
        buf(2, *quarter), buf(*quarter), buf(4, *quarter), buf(16, *quarter), buf(2, *quarter),
        pltpu.SemaphoreType.DMA((SEMS,)), pltpu.SemaphoreType.DMA((SEMS,)), pltpu.SemaphoreType.DMA((7,)),
    ]
    return pl.pallas_call(
        kernel,
        out_shape=(jax.ShapeDtypeStruct((2, K, W), F32), jax.ShapeDtypeStruct((K, K), F32)),
        in_specs=[pl.BlockSpec(memory_space=pl.ANY)] * 4,
        out_specs=(vmem, vmem),
        scratch_shapes=scratch,
        compiler_params=pltpu.CompilerParams(
            collective_id=0, has_side_effects=True, vmem_limit_bytes=56 * 2**20
        ),
        name="sweeps",
    )(sketch, inv_diag, upper, lower)


def solution(mesh):
    placed = (P("chain", None, None),) * 4
    return jax.shard_map(
        on_device,
        mesh=mesh,
        in_specs=placed,
        out_specs=(P("chain", None, None), P()),
        check_vma=False,
    )
```

```python
import jax
import jax.numpy as jnp
from jax import lax
from jax.experimental import pallas as pl
from jax.experimental.pallas import tpu as pltpu
from jax.sharding import PartitionSpec as P

HIGH = lax.Precision.HIGHEST
MESH = pl.DeviceIdType.MESH
F32 = jnp.float32

W = 256
K = 64
HALF_M = 128
HALF_C = 32
HALF = HALF_M + HALF_C
ROWS = 2 * HALF
SEMS = 128


def dot(a, b):
    return jnp.dot(a, b, precision=HIGH, preferred_element_type=F32)


def mat(n):
    return jnp.concatenate([n[0:HALF_M], n[HALF : HALF + HALF_M]], axis=0)


def vec(n):
    return jnp.concatenate([n[HALF_M:HALF], n[HALF + HALF_M : ROWS]], axis=0)


def pack(m, c):
    return jnp.concatenate([m[0:HALF_M], c[0:HALF_C], m[HALF_M:W], c[HALF_C:K]], axis=0)


def add_vec(r, n):
    return jnp.concatenate(
        [
            r[0:HALF_M],
            r[HALF_M:HALF] + n[HALF_M:HALF],
            r[HALF : HALF + HALF_M],
            r[HALF + HALF_M : ROWS] + n[HALF + HALF_M : ROWS],
        ],
        axis=0,
    )


def compose(f, n):
    return add_vec(dot(f, mat(n)), n)


def apply(v, n):
    return dot(v, mat(n)) + vec(n)


def identity(rows, columns):
    return (
        lax.broadcasted_iota(jnp.int32, (rows, columns), 0) == lax.broadcasted_iota(jnp.int32, (rows, columns), 1)
    ).astype(F32)


def factor(gram):
    work = jnp.concatenate([gram, identity(K, K)], axis=1)
    count = K // 8
    blocks = [work[8 * b : 8 * b + 8] for b in range(count)]
    sub = lax.broadcasted_iota(jnp.int32, (8, 2 * K), 0)

    def wide(v):
        return jnp.broadcast_to(v, (8, 2 * K))

    out = []
    for b in range(count):
        columns = [{i: wide(blocks[i][:, 8 * b + j : 8 * b + j + 1]) for i in range(b, count)} for j in range(8)]
        corner = {(i, j): wide(columns[j][b][i : i + 1]) for j in range(8) for i in range(j, 8)}
        rows = [wide(blocks[b][j : j + 1]) for j in range(8)]
        scaled = []
        done = jnp.zeros((8, 2 * K), F32)
        pivots = jnp.ones((8, 2 * K), F32)
        for j in range(8):
            inverse = 1.0 / corner[j, j]
            scaled.append(rows[j] * inverse)
            pivots = jnp.where(sub == j, corner[j, j], pivots)
            done = jnp.where(sub == j, rows[j], done)
            for i in range(j + 1, 8):
                ratio = corner[i, j] * inverse
                rows[i] = rows[i] - ratio * rows[j]
                for n in range(i, 8):
                    corner[n, i] = corner[n, i] - corner[n, j] * ratio
                for n in range(b + 1, count):
                    columns[i][n] = columns[i][n] - columns[j][n] * ratio
        for i in range(b + 1, count):
            for j in range(8):
                blocks[i] = blocks[i] - columns[j][i] * scaled[j]
        out.append(done * lax.rsqrt(pivots))
    out = jnp.concatenate(out, axis=0)
    upper = jnp.where(
        lax.broadcasted_iota(jnp.int32, (K, K), 0) <= lax.broadcasted_iota(jnp.int32, (K, K), 1), out[:, 0:K], 0.0
    )
    return upper, out[:, K : 2 * K]


def kernel(
    sketch_in, inv_diag_in, upper_in, lower_in, basis, r_factor,
    sketch, inv_diag, upper, lower, own0, fc, gc, hc, y0s, y1s, dev_g, dev_h,
    xf, xg, xh, xpre, xsuf_h, xsuf_g, yf, yg, ypre, ysuf_g, ysum, row_h,
    zf, zc_in, zm_in, va, va_in, zg, entry, er, ep, ysuf_e, ends, tops, gown, gin, gx, gyz, gtot,
    send, recv, load,
):
    me = lax.axis_index("chain")
    c = lax.rem(me, 2)
    x = lax.rem(me // 2, 4)
    y = lax.rem(me // 8, 4)
    z = me // 32

    loads = []
    for src, dst in ((inv_diag_in, inv_diag), (upper_in, upper), (lower_in, lower)):
        for i in (0, 1):
            loads.append(pltpu.make_async_copy(src.at[i], dst.at[i], load.at[len(loads)]))
    loads.append(pltpu.make_async_copy(sketch_in, sketch, load.at[6]))
    for i in (0, 2, 6, 1, 3, 4, 5):
        loads[i].start()

    def at(zz, yy, xx, cc):
        return ((zz * 4 + yy) * 4 + xx) * 2 + cc

    def turn(place, k):
        return lax.rem(place + k, 4)

    sibling = at(z, y, x, 1 - c)
    xs = [at(z, y, turn(x, k), c) for k in range(4)]
    across = {(k, n): at(turn(z, k), turn(y, n), x, c) for k in (0, 1, 3, 2) for n in (0, 1, 3, 2) if (k, n) != (0, 0)}
    ys = [None, *(across[0, n] for n in (1, 2, 3))]
    zs = [None, *(across[k, 0] for k in (1, 2, 3))]

    barrier = pltpu.get_barrier_semaphore()
    for other in (sibling, *xs[1:], *across.values()):
        pl.semaphore_signal(barrier, inc=1, device_id=(other,), device_id_type=MESH)

    sent = []
    used = [0]

    def slot():
        used[0] += 1
        assert used[0] <= SEMS
        return used[0] - 1

    def on(condition, act):
        if condition is None:
            act()
        else:
            pl.when(condition)(act)

    def start(src, dst, i, other, condition=None):
        copy = pltpu.make_async_remote_copy(
            src_ref=src, dst_ref=dst, send_sem=send.at[i], recv_sem=recv.at[i], device_id=(other,), device_id_type=MESH
        )
        on(condition, copy.start)
        sent.append((condition, copy))

    def arrived(dst, i, condition=None):
        copy = pltpu.make_async_remote_copy(
            src_ref=dst, dst_ref=dst, send_sem=send.at[i], recv_sem=recv.at[i], device_id=(sibling,), device_id_type=MESH
        )
        on(condition, copy.wait_recv)

    def drain(count):
        for condition, copy in sent[:count]:
            on(condition, copy.wait_send)
        del sent[:count]

    def rows_of(which, rows):
        return pl.ds(pl.multiple_of(which * rows, 8), rows)

    mine, others = rows_of(c, HALF), rows_of(1 - c, HALF)
    my_vec = pl.ds(pl.multiple_of(c * HALF + HALF_M, 8), HALF_C)

    def compose_half(f, n, which):
        r = dot(f, mat(n[...]))
        return jnp.concatenate(
            [r[0:HALF_M], r[HALF_M:HALF] + n[pl.ds(pl.multiple_of(which * HALF + HALF_M, 8), HALF_C)]], axis=0
        )

    class Gather:
        def __init__(self, ref, rows, place, peers, steps, gives=None, takes=None):
            self.ref, self.rows, self.place, self.peers, self.steps = ref, rows, place, peers, steps
            self.gives = dict(zip(steps, gives)) if gives else {}
            self.takes = dict(zip(steps, takes)) if takes else {}
            self.first = {k: slot() for k in steps}
            self.second = {k: slot() for k in steps}

        def part(self, k, which):
            return self.ref.at[turn(self.place, 4 - k), rows_of(which, self.rows)]

        def start(self):
            for k in self.steps:
                start(self.part(0, c), self.part(0, c), self.first[k], self.peers[k], self.gives.get(k))

        def forward(self):
            for k in self.steps:
                arrived(self.part(k, c), self.first[k], self.takes.get(k))
                start(self.part(k, c), self.part(k, c), self.second[k], sibling, self.takes.get(k))

        def finish(self):
            for k in self.steps:
                arrived(self.part(k, 1 - c), self.second[k], self.takes.get(k))

    class Relay:
        cut = HALF // 2

        def __init__(self, ref, place, peers):
            self.ref, self.place, self.peers = ref, place, peers
            self.first = {(k, p): slot() for k in (1, 3, 2) for p in (0, 1)}
            self.second = {(k, p): slot() for k in (1, 3, 2) for p in (0, 1)}

        def part(self, k, p, which):
            at_row = pl.multiple_of(which * HALF + p * self.cut, 8)
            return self.ref.at[turn(self.place, 4 - k), pl.ds(at_row, self.cut)]

        def start(self):
            for k, p in ((1, 0), (3, 1), (1, 1), (3, 0)):
                start(self.part(0, p, c), self.part(0, p, c), self.first[k, p], self.peers[k])

        def inside(self, k, p):
            start(self.part(k, p, c), self.part(k, p, c), self.second[k, p], sibling)

        def relay(self):
            for k, p in ((1, 0), (3, 1)):
                arrived(self.part(k, p, c), self.first[k, p])
                start(self.part(k, p, c), self.part(k, p, c), self.first[2, p], self.peers[k])
            for k, p in ((1, 0), (3, 1)):
                self.inside(k, p)

        def forward(self):
            for k, p in ((1, 1), (3, 0), (2, 0), (2, 1)):
                arrived(self.part(k, p, c), self.first[k, p])
                self.inside(k, p)

        def finish(self):
            for k, p in self.second:
                arrived(self.part(k, p, 1 - c), self.second[k, p])

    class Share:
        def __init__(self, ref, place, peers):
            self.ref, self.place, self.peers = ref, place, peers
            self.sems = {k: slot() for k in (1, 3, 2)}

        def start(self):
            for k in (1, 3, 2):
                start(self.ref.at[self.place], self.ref.at[self.place], self.sems[k], self.peers[k])

        def finish(self):
            for k in (1, 3, 2):
                arrived(self.ref.at[turn(self.place, 4 - k)], self.sems[k])

    def swap(ref, i):
        start(ref.at[c], ref.at[c], i, sibling)

    for i in (0, 2, 6):
        loads[i].wait()
    y0s[...] = dot(pack(-upper[0], sketch[0]), inv_diag[0])
    for i in (1, 3):
        loads[i].wait()
    own0[...] = dot(pack(-upper[1], sketch[1]), inv_diag[1])
    y1s[...] = compose(y0s[...], own0[...])
    fc[c] = y1s[...]
    pl.semaphore_wait(barrier, 1 + 3 + 15)
    sem_f, sem_g, sem_h = slot(), slot(), slot()
    swap(fc, sem_f)
    for i in (4, 5):
        loads[i].wait()
    gc[c] = dot(lower[1], lower[0])
    swap(gc, sem_g)
    arrived(fc.at[1 - c], sem_f)

    xf[x, mine] = compose_half(fc[0, mine], fc.at[1], c)
    gather_xf = Relay(xf, x, xs)
    gather_xf.start()
    xf[x, others] = compose_half(fc[0, others], fc.at[1], 1 - c)
    hc[c] = dot(y0s[...] - dot(y1s[...], lower[1]), lower[0])
    swap(hc, sem_h)
    arrived(gc.at[1 - c], sem_g)
    xg[x] = dot(gc[1], gc[0])
    gather_xf.relay()

    gather_xg = Gather(xg, HALF_M, x, xs, (1, 3, 2))
    gather_xg.start()
    arrived(hc.at[1 - c], sem_h)
    late = compose(fc[0], hc[1])
    xh[x] = dot(late, gc[0]) + hc[0]
    second = c == 1
    eye = identity(W, W)
    dev_g[...] = jnp.where(second, eye, gc[1])
    dev_h[...] = jnp.where(second, 0.0, late)
    y0s[...] = jnp.where(second, compose(fc[0], y0s[...]), y0s[...])
    y1s[...] = jnp.where(second, xf[x], y1s[...])
    drain(3)
    gather_xf.forward()
    gather_xf.finish()
    q23 = compose(xf[2], xf[3])
    xsuf_h[0] = q23
    xpre[2, mine] = compose_half(xf[0, mine], xf.at[1], c)
    yf[y, mine] = compose_half(xpre[2, mine], xsuf_h.at[0], c)

    gather_yf = Relay(yf, y, ys)
    gather_yf.start()
    gather_xh = Gather(xh, HALF, x, xs, (1, 3, 2))
    gather_xh.start()
    xpre[2, others] = compose_half(xf[0, others], xf.at[1], 1 - c)
    yf[y, others] = compose_half(xpre[2, others], xsuf_h.at[0], 1 - c)
    xpre[0] = pack(eye, jnp.zeros((K, W), F32))
    xpre[1] = xf[0]
    xpre[3] = compose(xpre[2], xf[2])
    y0s[...] = compose(xpre[x], y0s[...])
    y1s[...] = compose(xpre[x], y1s[...])
    drain(12)
    gather_yf.relay()

    gather_xg.forward()
    dev_h[...] = compose(xpre[x], dev_h[...])
    gather_xg.finish()
    xsuf_g[3] = eye
    xsuf_g[2] = xg[3]
    xsuf_g[1] = dot(xg[3], xg[2])
    xsuf_g[0] = dot(xsuf_g[1], xg[1])
    yg[y] = dot(xsuf_g[0], xg[0])
    gather_yg = Gather(yg, HALF_M, y, ys, (1, 3, 2))
    gather_yg.start()
    gather_yf.forward()
    gather_yf.finish()
    q23 = compose(yf[2], yf[3])
    xsuf_h[0] = q23
    ypre[2, mine] = compose_half(yf[0, mine], yf.at[1], c)
    zf[my_vec] = dot(ypre[2, my_vec], mat(q23)) + xsuf_h[0, my_vec]

    sem_c, sem_m, sem_m2, sem_v1, sem_v2 = slot(), slot(), slot(), slot(), slot()
    start(zf.at[my_vec], zc_in, sem_c, zs[1])
    my_m = pl.ds(pl.multiple_of(c * HALF, 8), HALF_M)
    other_m = pl.ds(pl.multiple_of((1 - c) * HALF, 8), HALF_M)
    my_half, other_half = rows_of(c, HALF_M), rows_of(1 - c, HALF_M)
    zf[my_m] = dot(ypre[2, my_m], mat(q23))
    start(zf.at[my_m], zm_in.at[my_half], sem_m, zs[1])
    ypre[2, others] = compose_half(yf[0, others], yf.at[1], 1 - c)
    zf[other_m] = dot(ypre[2, other_m], mat(q23))
    gather_xh.forward()
    ypre[0] = pack(eye, jnp.zeros((K, W), F32))
    ypre[1] = yf[0]
    gather_xh.finish()
    xsuf_h[3] = jnp.zeros((ROWS, W), F32)
    xsuf_h[2] = compose(xpre[3], xh[3])
    xsuf_h[1] = dot(xsuf_h[2], xg[2]) + compose(xpre[2], xh[2])

    arrived(zc_in, sem_c)
    va[...] = dot(zc_in[...], mat(zf[...])) + zf[my_vec]
    start(va, va_in.at[0], sem_v1, zs[1])
    start(va, va_in.at[1], sem_v2, zs[2])
    arrived(zm_in.at[my_half], sem_m)
    start(zm_in.at[my_half], zm_in.at[my_half], sem_m2, sibling)

    ypre[3] = compose(ypre[2], yf[2])
    xsuf_h[0] = dot(xsuf_h[1], xg[1]) + compose(xf[0], xh[1])
    row_h[...] = compose(ypre[y], dot(xsuf_h[0], xg[0]) + xh[0])
    drain(24)

    arrived(zm_in.at[other_half], sem_m2)
    arrived(va_in.at[0], sem_v1)
    arrived(va_in.at[1], sem_v2)
    last = dot(va_in[1], zm_in[...]) + zc_in[...]
    start_row = jnp.where(z == 0, 0.0, jnp.where(z == 1, zc_in[...], jnp.where(z == 2, va_in[0], last)))

    er[y] = dot(start_row, mat(row_h[...])) + row_h[my_vec]
    share_er = Share(er, y, ys)
    share_er.start()
    entry[c] = start_row
    sem_entry = slot()
    swap(entry, sem_entry)
    gather_yg.forward()
    gather_yg.finish()
    ysuf_g[3] = eye
    ysuf_g[2] = yg[3]
    ysuf_g[1] = dot(yg[3], yg[2])
    ysuf_g[0] = dot(ysuf_g[1], yg[1])
    zg[z] = dot(ysuf_g[0], yg[0])
    gather_zg = Gather(zg, HALF_M, z, zs, (3, 2), ((z == 1) | (z == 2), z == 2), (z < 2, z == 0))
    gather_zg.start()

    ysum[0] = yg[0]
    ysum[1] = dot(yg[1], yg[0])
    ysum[2] = dot(yg[2], ysum[1])

    dev_h[...] = dot(xsuf_h[x], dev_g[...]) + dev_h[...]
    dev_g[...] = dot(xsuf_g[x], dev_g[...])
    arrived(entry.at[1 - c], sem_entry)
    row = apply(jnp.concatenate([entry[0], entry[1]], axis=0), ypre[y])
    x1 = apply(row, y1s[...]) - apply(row, dev_h[...])
    x0 = apply(row, y0s[...]) - dot(x1, lower[1])

    share_er.finish()
    ep[z] = dot(jnp.concatenate([er[1], er[2], er[3]], axis=1), ysum[...].reshape(3 * W, W)) + er[0]

    share_ep = Share(ep, z, zs)
    share_ep.start()
    ysuf_e[3] = jnp.zeros((HALF_C, W), F32)
    ysuf_e[2] = er[3]
    ysuf_e[1] = dot(er[3], yg[2]) + er[2]
    ysuf_e[0] = dot(ysuf_e[1], yg[1]) + er[1]
    ends[c] = ysuf_e[y]
    sem_ends = slot()
    swap(ends, sem_ends)
    to_w1 = dot(ysuf_g[y], dev_g[...])
    to_w0 = dot(to_w1, lower[1])
    arrived(ends.at[1 - c], sem_ends)
    from_row = dot(jnp.concatenate([ends[0], ends[1]], axis=0), dev_g[...])
    x1 = x1 - from_row
    x0 = x0 + dot(from_row, lower[1])
    drain(23)
    gather_zg.forward()
    gather_zg.finish()
    share_ep.finish()
    two = dot(ep[3], zg[2]) + ep[2]
    three = dot(two, zg[1]) + ep[1]
    tops[c] = jnp.where(z == 3, 0.0, jnp.where(z == 2, ep[3], jnp.where(z == 1, two, three)))
    sem_tops = slot()
    swap(tops, sem_tops)
    arrived(tops.at[1 - c], sem_tops)
    top = jnp.concatenate([tops[0], tops[1]], axis=0)
    x1 = x1 - dot(top, to_w1)
    x0 = x0 + dot(top, to_w0)

    both = jnp.concatenate([x0, x1], axis=1)
    gram = lax.dot_general(both, both, (((1,), (1,)), ((), ())), precision=HIGH, preferred_element_type=F32)
    gram = jnp.concatenate([gram[0 : K // 2], gram[K // 2 : K]], axis=1)
    gown[0] = gram[0 : K // 4]
    gown[1] = gram[K // 4 : K // 2]
    sem_gin, sem_gtot = slot(), slot()
    start(gown.at[1 - c], gin, sem_gin, sibling)
    arrived(gin, sem_gin)
    gx[x] = gown[c] + gin[...]
    share_gx = Share(gx, x, xs)
    share_gx.start()
    drain(9)
    share_gx.finish()
    own = z * 4 + y
    gyz[own] = (gx[0] + gx[1]) + (gx[2] + gx[3])
    sems = {step: slot() for step in across}
    for step, other in across.items():
        start(gyz.at[own], gyz.at[own], sems[step], other)
    drain(3)
    for (k, n), i in sems.items():
        arrived(gyz.at[turn(z, 4 - k) * 4 + turn(y, 4 - n)], i)
    terms = [gyz[i] for i in range(16)]
    while len(terms) > 1:
        terms = [terms[i] + terms[i + 1] for i in range(0, len(terms), 2)]
    gtot[c] = terms[0]
    swap(gtot, sem_gtot)
    drain(15)
    arrived(gtot.at[1 - c], sem_gtot)
    total = jnp.concatenate([gtot[0], gtot[1]], axis=0) / (256 * W)
    r, inverse = factor(jnp.concatenate([total[:, 0:K], total[:, K : 2 * K]], axis=0))
    r_factor[...] = r
    basis[0] = dot(inverse, x0)
    basis[1] = dot(inverse, x1)
    drain(len(sent))


def on_device(sketch, inv_diag, upper, lower):
    def buf(*shape):
        return pltpu.VMEM(shape, F32)

    affine = (ROWS, W)
    part = (HALF_C, W)
    quarter = (K // 4, 2 * K)
    vmem = pl.BlockSpec(memory_space=pltpu.VMEM)
    scratch = [
        buf(2, K, W), buf(2, W, W), buf(2, W, W), buf(2, W, W), buf(*affine), buf(2, *affine), buf(2, W, W), buf(2, *affine),
        buf(*affine), buf(*affine), buf(W, W), buf(*affine),
        buf(4, *affine), buf(4, W, W), buf(4, *affine), buf(4, *affine), buf(4, *affine), buf(4, W, W),
        buf(4, *affine), buf(4, W, W), buf(4, *affine), buf(4, W, W), buf(3, W, W), buf(*affine),
        buf(*affine), buf(*part), buf(W, W), buf(*part), buf(2, *part), buf(4, W, W), buf(2, *part),
        buf(4, *part), buf(4, *part), buf(4, *part), buf(2, *part), buf(2, *part),
        buf(2, *quarter), buf(*quarter), buf(4, *quarter), buf(16, *quarter), buf(2, *quarter),
        pltpu.SemaphoreType.DMA((SEMS,)), pltpu.SemaphoreType.DMA((SEMS,)), pltpu.SemaphoreType.DMA((7,)),
    ]
    return pl.pallas_call(
        kernel,
        out_shape=(jax.ShapeDtypeStruct((2, K, W), F32), jax.ShapeDtypeStruct((K, K), F32)),
        in_specs=[pl.BlockSpec(memory_space=pl.ANY)] * 4,
        out_specs=(vmem, vmem),
        scratch_shapes=scratch,
        compiler_params=pltpu.CompilerParams(
            collective_id=0, has_side_effects=True, vmem_limit_bytes=56 * 2**20
        ),
        name="sweeps",
    )(sketch, inv_diag, upper, lower)


def solution(mesh):
    placed = (P("chain", None, None),) * 4
    return jax.shard_map(
        on_device,
        mesh=mesh,
        in_specs=placed,
        out_specs=(P("chain", None, None), P()),
        check_vma=False,
    )
```

```python
import jax
import jax.numpy as jnp
from jax import lax
from jax.experimental import pallas as pl
from jax.experimental.pallas import tpu as pltpu
from jax.sharding import PartitionSpec as P

HIGH = lax.Precision.HIGHEST
MESH = pl.DeviceIdType.MESH
F32 = jnp.float32

W = 256
K = 64
HALF_M = 128
HALF_C = 32
HALF = HALF_M + HALF_C
ROWS = 2 * HALF
SEMS = 160


def dot(a, b):
    return jnp.dot(a, b, precision=HIGH, preferred_element_type=F32)


def mat(n):
    return jnp.concatenate([n[0:HALF_M], n[HALF : HALF + HALF_M]], axis=0)


def vec(n):
    return jnp.concatenate([n[HALF_M:HALF], n[HALF + HALF_M : ROWS]], axis=0)


def pack(m, c):
    return jnp.concatenate([m[0:HALF_M], c[0:HALF_C], m[HALF_M:W], c[HALF_C:K]], axis=0)


def add_vec(r, n):
    return jnp.concatenate(
        [
            r[0:HALF_M],
            r[HALF_M:HALF] + n[HALF_M:HALF],
            r[HALF : HALF + HALF_M],
            r[HALF + HALF_M : ROWS] + n[HALF + HALF_M : ROWS],
        ],
        axis=0,
    )


def compose(f, n):
    return add_vec(dot(f, mat(n)), n)


def apply(v, n):
    return dot(v, mat(n)) + vec(n)


def identity(rows, columns):
    return (
        lax.broadcasted_iota(jnp.int32, (rows, columns), 0) == lax.broadcasted_iota(jnp.int32, (rows, columns), 1)
    ).astype(F32)


def factor(gram):
    work = jnp.concatenate([gram, identity(K, K)], axis=1)
    count = K // 8
    blocks = [work[8 * b : 8 * b + 8] for b in range(count)]
    sub = lax.broadcasted_iota(jnp.int32, (8, 2 * K), 0)

    def wide(v):
        return jnp.broadcast_to(v, (8, 2 * K))

    out = []
    for b in range(count):
        columns = [{i: wide(blocks[i][:, 8 * b + j : 8 * b + j + 1]) for i in range(b, count)} for j in range(8)]
        corner = {(i, j): wide(columns[j][b][i : i + 1]) for j in range(8) for i in range(j, 8)}
        rows = [wide(blocks[b][j : j + 1]) for j in range(8)]
        scaled = []
        done = jnp.zeros((8, 2 * K), F32)
        pivots = jnp.ones((8, 2 * K), F32)
        for j in range(8):
            inverse = 1.0 / corner[j, j]
            scaled.append(rows[j] * inverse)
            pivots = jnp.where(sub == j, corner[j, j], pivots)
            done = jnp.where(sub == j, rows[j], done)
            for i in range(j + 1, 8):
                ratio = corner[i, j] * inverse
                rows[i] = rows[i] - ratio * rows[j]
                for n in range(i, 8):
                    corner[n, i] = corner[n, i] - corner[n, j] * ratio
                for n in range(b + 1, count):
                    columns[i][n] = columns[i][n] - columns[j][n] * ratio
        for i in range(b + 1, count):
            for j in range(8):
                blocks[i] = blocks[i] - columns[j][i] * scaled[j]
        out.append(done * lax.rsqrt(pivots))
    out = jnp.concatenate(out, axis=0)
    upper = jnp.where(
        lax.broadcasted_iota(jnp.int32, (K, K), 0) <= lax.broadcasted_iota(jnp.int32, (K, K), 1), out[:, 0:K], 0.0
    )
    return upper, out[:, K : 2 * K]


def kernel(
    sketch_in, inv_diag_in, upper_in, lower_in, basis, r_factor,
    sketch, inv_diag, upper, lower, own0, fc, gc, hc, y0s, y1s, dev_g, dev_h,
    xf, xg, xh, xpre, xsuf_h, xsuf_g, yf, yg, ypre, ysuf_g, ysum, row_h,
    zf, zc_in, zm_in, va, va_in, zg, entry, er, ep, ysuf_e, ends, tops, gown, gx, gyz, gtot,
    send, recv, load,
):
    me = lax.axis_index("chain")
    c = lax.rem(me, 2)
    x = lax.rem(me // 2, 4)
    y = lax.rem(me // 8, 4)
    z = me // 32

    loads = []
    for src, dst in ((inv_diag_in, inv_diag), (upper_in, upper), (lower_in, lower)):
        for i in (0, 1):
            loads.append(pltpu.make_async_copy(src.at[i], dst.at[i], load.at[len(loads)]))
    loads.append(pltpu.make_async_copy(sketch_in, sketch, load.at[6]))
    for i in (0, 2, 6, 1, 3, 4, 5):
        loads[i].start()

    def at(zz, yy, xx, cc):
        return ((zz * 4 + yy) * 4 + xx) * 2 + cc

    def turn(place, k):
        return lax.rem(place + k, 4)

    sibling = at(z, y, x, 1 - c)
    xs = [at(z, y, turn(x, k), c) for k in range(4)]
    across = {(k, n): at(turn(z, k), turn(y, n), x, c) for k in (0, 1, 3, 2) for n in (0, 1, 3, 2) if (k, n) != (0, 0)}
    ys = [None, *(across[0, n] for n in (1, 2, 3))]
    zs = [None, *(across[k, 0] for k in (1, 2, 3))]

    barrier = pltpu.get_barrier_semaphore()
    for other in (sibling, *xs[1:], *(at(z, y, turn(x, k), 1 - c) for k in (1, 2, 3)), *across.values()):
        pl.semaphore_signal(barrier, inc=1, device_id=(other,), device_id_type=MESH)

    sent = []
    used = [0]

    def slot():
        used[0] += 1
        assert used[0] <= SEMS
        return used[0] - 1

    def on(condition, act):
        if condition is None:
            act()
        else:
            pl.when(condition)(act)

    def start(src, dst, i, other, condition=None):
        copy = pltpu.make_async_remote_copy(
            src_ref=src, dst_ref=dst, send_sem=send.at[i], recv_sem=recv.at[i], device_id=(other,), device_id_type=MESH
        )
        on(condition, copy.start)
        sent.append((condition, copy))

    def arrived(dst, i, condition=None):
        copy = pltpu.make_async_remote_copy(
            src_ref=dst, dst_ref=dst, send_sem=send.at[i], recv_sem=recv.at[i], device_id=(sibling,), device_id_type=MESH
        )
        on(condition, copy.wait_recv)

    def drain(count):
        for condition, copy in sent[:count]:
            on(condition, copy.wait_send)
        del sent[:count]

    def rows_of(which, rows):
        return pl.ds(pl.multiple_of(which * rows, 8), rows)

    mine, others = rows_of(c, HALF), rows_of(1 - c, HALF)
    my_vec = pl.ds(pl.multiple_of(c * HALF + HALF_M, 8), HALF_C)

    def compose_half(f, n, which):
        r = dot(f, mat(n[...]))
        return jnp.concatenate(
            [r[0:HALF_M], r[HALF_M:HALF] + n[pl.ds(pl.multiple_of(which * HALF + HALF_M, 8), HALF_C)]], axis=0
        )

    class Gather:
        def __init__(self, ref, rows, place, peers, steps, gives=None, takes=None):
            self.ref, self.rows, self.place, self.peers, self.steps = ref, rows, place, peers, steps
            self.gives = dict(zip(steps, gives)) if gives else {}
            self.takes = dict(zip(steps, takes)) if takes else {}
            self.first = {k: slot() for k in steps}
            self.second = {k: slot() for k in steps}

        def part(self, k, which):
            return self.ref.at[turn(self.place, 4 - k), rows_of(which, self.rows)]

        def start(self):
            for k in self.steps:
                start(self.part(0, c), self.part(0, c), self.first[k], self.peers[k], self.gives.get(k))

        def forward(self):
            for k in self.steps:
                arrived(self.part(k, c), self.first[k], self.takes.get(k))
                start(self.part(k, c), self.part(k, c), self.second[k], sibling, self.takes.get(k))

        def finish(self):
            for k in self.steps:
                arrived(self.part(k, 1 - c), self.second[k], self.takes.get(k))

    class Relay:
        handed = ((1, 0), (3, 3), (1, 1), (3, 2))
        piece = HALF // 4

        def __init__(self, ref, place, peers):
            self.ref, self.place, self.peers = ref, place, peers
            self.first = {key: slot() for key in (*self.handed, (1, "rest"), (3, "rest"))}
            self.far = {key: slot() for key in self.handed}
            self.second = {key: slot() for key in ((1, 0), (3, 1), (1, 1), (3, 0), (2, None))}

        def rows(self, k, low, count, which):
            at_row = pl.multiple_of(which * HALF + low, 8)
            return self.ref.at[turn(self.place, 4 - k), pl.ds(at_row, count)]

        def quarter(self, k, q):
            return self.rows(k, q * self.piece, self.piece, c)

        def half(self, k, p, which):
            return self.rows(k, p * 2 * self.piece, 2 * self.piece, which)

        def start(self):
            for k, q in self.handed:
                start(self.quarter(0, q), self.quarter(0, q), self.first[k, q], self.peers[k])
            for k, p in ((1, 1), (3, 0)):
                start(self.half(0, p, c), self.half(0, p, c), self.first[k, "rest"], self.peers[k])

        def inside(self, k, p):
            start(self.half(k, p, c), self.half(k, p, c), self.second[k, p], sibling)

        def relay(self):
            for k, q in self.handed:
                arrived(self.quarter(k, q), self.first[k, q])
                start(self.quarter(k, q), self.quarter(k, q), self.far[k, q], self.peers[k])
            self.inside(1, 0)
            self.inside(3, 1)

        def forward(self):
            for k, p in ((1, 1), (3, 0)):
                arrived(self.half(k, p, c), self.first[k, "rest"])
                self.inside(k, p)
            for k, q in self.handed:
                arrived(self.quarter(2, q), self.far[k, q])
            start(self.rows(2, 0, HALF, c), self.rows(2, 0, HALF, c), self.second[2, None], sibling)

        def finish(self):
            for k, p in self.second:
                part = self.rows(2, 0, HALF, 1 - c) if p is None else self.half(k, p, 1 - c)
                arrived(part, self.second[k, p])

    class Share:
        def __init__(self, ref, place, peers):
            self.ref, self.place, self.peers = ref, place, peers
            self.sems = {k: slot() for k in (1, 3, 2)}

        def start(self):
            for k in (1, 3, 2):
                start(self.ref.at[self.place], self.ref.at[self.place], self.sems[k], self.peers[k])

        def finish(self):
            for k in (1, 3, 2):
                arrived(self.ref.at[turn(self.place, 4 - k)], self.sems[k])

    def swap(ref, i):
        start(ref.at[c], ref.at[c], i, sibling)

    for i in (0, 2, 6):
        loads[i].wait()
    y0s[...] = dot(pack(-upper[0], sketch[0]), inv_diag[0])
    for i in (1, 3):
        loads[i].wait()
    own0[...] = dot(pack(-upper[1], sketch[1]), inv_diag[1])
    y1s[...] = compose(y0s[...], own0[...])
    fc[c] = y1s[...]
    pl.semaphore_wait(barrier, 1 + 3 + 3 + 15)
    sem_f, sem_g, sem_h = slot(), slot(), slot()
    swap(fc, sem_f)
    for i in (4, 5):
        loads[i].wait()
    gc[c] = dot(lower[1], lower[0])
    swap(gc, sem_g)
    arrived(fc.at[1 - c], sem_f)

    xf[x, mine] = compose_half(fc[0, mine], fc.at[1], c)
    gather_xf = Relay(xf, x, xs)
    gather_xf.start()
    xf[x, others] = compose_half(fc[0, others], fc.at[1], 1 - c)
    hc[c] = dot(y0s[...] - dot(y1s[...], lower[1]), lower[0])
    swap(hc, sem_h)
    arrived(gc.at[1 - c], sem_g)
    xg[x] = dot(gc[1], gc[0])
    gather_xf.relay()

    gather_xg = Gather(xg, HALF_M, x, xs, (1, 3, 2))
    gather_xg.start()
    arrived(hc.at[1 - c], sem_h)
    late = compose(fc[0], hc[1])
    xh[x] = dot(late, gc[0]) + hc[0]
    second = c == 1
    eye = identity(W, W)
    dev_g[...] = jnp.where(second, eye, gc[1])
    dev_h[...] = jnp.where(second, 0.0, late)
    y0s[...] = jnp.where(second, compose(fc[0], y0s[...]), y0s[...])
    y1s[...] = jnp.where(second, xf[x], y1s[...])
    drain(3)
    gather_xf.forward()
    gather_xf.finish()
    q23 = compose(xf[2], xf[3])
    xsuf_h[0] = q23
    xpre[2, mine] = compose_half(xf[0, mine], xf.at[1], c)
    yf[y, mine] = compose_half(xpre[2, mine], xsuf_h.at[0], c)

    gather_yf = Relay(yf, y, ys)
    gather_yf.start()
    gather_xh = Gather(xh, HALF, x, xs, (1, 3, 2))
    gather_xh.start()
    xpre[2, others] = compose_half(xf[0, others], xf.at[1], 1 - c)
    yf[y, others] = compose_half(xpre[2, others], xsuf_h.at[0], 1 - c)
    xpre[0] = pack(eye, jnp.zeros((K, W), F32))
    xpre[1] = xf[0]
    xpre[3] = compose(xpre[2], xf[2])
    y0s[...] = compose(xpre[x], y0s[...])
    y1s[...] = compose(xpre[x], y1s[...])
    drain(12)
    gather_yf.relay()

    gather_xg.forward()
    dev_h[...] = compose(xpre[x], dev_h[...])
    gather_xg.finish()
    xsuf_g[3] = eye
    xsuf_g[2] = xg[3]
    xsuf_g[1] = dot(xg[3], xg[2])
    xsuf_g[0] = dot(xsuf_g[1], xg[1])
    yg[y] = dot(xsuf_g[0], xg[0])
    gather_yg = Gather(yg, HALF_M, y, ys, (1, 3, 2))
    gather_yg.start()
    gather_yf.forward()
    gather_yf.finish()
    q23 = compose(yf[2], yf[3])
    xsuf_h[0] = q23
    ypre[2, mine] = compose_half(yf[0, mine], yf.at[1], c)
    zf[my_vec] = dot(ypre[2, my_vec], mat(q23)) + xsuf_h[0, my_vec]

    sem_c, sem_m, sem_m2, sem_v1, sem_v2 = slot(), slot(), slot(), slot(), slot()
    start(zf.at[my_vec], zc_in, sem_c, zs[1])
    my_m = pl.ds(pl.multiple_of(c * HALF, 8), HALF_M)
    other_m = pl.ds(pl.multiple_of((1 - c) * HALF, 8), HALF_M)
    my_half, other_half = rows_of(c, HALF_M), rows_of(1 - c, HALF_M)
    zf[my_m] = dot(ypre[2, my_m], mat(q23))
    start(zf.at[my_m], zm_in.at[my_half], sem_m, zs[1])
    ypre[2, others] = compose_half(yf[0, others], yf.at[1], 1 - c)
    zf[other_m] = dot(ypre[2, other_m], mat(q23))
    gather_xh.forward()
    ypre[0] = pack(eye, jnp.zeros((K, W), F32))
    ypre[1] = yf[0]
    gather_xh.finish()
    xsuf_h[3] = jnp.zeros((ROWS, W), F32)
    xsuf_h[2] = compose(xpre[3], xh[3])
    xsuf_h[1] = dot(xsuf_h[2], xg[2]) + compose(xpre[2], xh[2])

    arrived(zc_in, sem_c)
    va[...] = dot(zc_in[...], mat(zf[...])) + zf[my_vec]
    start(va, va_in.at[0], sem_v1, zs[1])
    start(va, va_in.at[1], sem_v2, zs[2])
    arrived(zm_in.at[my_half], sem_m)
    start(zm_in.at[my_half], zm_in.at[my_half], sem_m2, sibling)

    ypre[3] = compose(ypre[2], yf[2])
    xsuf_h[0] = dot(xsuf_h[1], xg[1]) + compose(xf[0], xh[1])
    row_h[...] = compose(ypre[y], dot(xsuf_h[0], xg[0]) + xh[0])
    drain(24)

    arrived(zm_in.at[other_half], sem_m2)
    arrived(va_in.at[0], sem_v1)
    arrived(va_in.at[1], sem_v2)
    last = dot(va_in[1], zm_in[...]) + zc_in[...]
    start_row = jnp.where(z == 0, 0.0, jnp.where(z == 1, zc_in[...], jnp.where(z == 2, va_in[0], last)))

    er[y] = dot(start_row, mat(row_h[...])) + row_h[my_vec]
    share_er = Share(er, y, ys)
    share_er.start()
    entry[c] = start_row
    sem_entry = slot()
    swap(entry, sem_entry)
    gather_yg.forward()
    gather_yg.finish()
    ysuf_g[3] = eye
    ysuf_g[2] = yg[3]
    ysuf_g[1] = dot(yg[3], yg[2])
    ysuf_g[0] = dot(ysuf_g[1], yg[1])
    zg[z] = dot(ysuf_g[0], yg[0])
    gather_zg = Gather(zg, HALF_M, z, zs, (3, 2), ((z == 1) | (z == 2), z == 2), (z < 2, z == 0))
    gather_zg.start()

    ysum[0] = yg[0]
    ysum[1] = dot(yg[1], yg[0])
    ysum[2] = dot(yg[2], ysum[1])

    dev_h[...] = dot(xsuf_h[x], dev_g[...]) + dev_h[...]
    dev_g[...] = dot(xsuf_g[x], dev_g[...])
    arrived(entry.at[1 - c], sem_entry)
    row = apply(jnp.concatenate([entry[0], entry[1]], axis=0), ypre[y])
    x1 = apply(row, y1s[...]) - apply(row, dev_h[...])
    x0 = apply(row, y0s[...]) - dot(x1, lower[1])

    share_er.finish()
    ep[z] = dot(jnp.concatenate([er[1], er[2], er[3]], axis=1), ysum[...].reshape(3 * W, W)) + er[0]

    share_ep = Share(ep, z, zs)
    share_ep.start()
    ysuf_e[3] = jnp.zeros((HALF_C, W), F32)
    ysuf_e[2] = er[3]
    ysuf_e[1] = dot(er[3], yg[2]) + er[2]
    ysuf_e[0] = dot(ysuf_e[1], yg[1]) + er[1]
    ends[c] = ysuf_e[y]
    sem_ends = slot()
    swap(ends, sem_ends)
    to_w1 = dot(ysuf_g[y], dev_g[...])
    to_w0 = dot(to_w1, lower[1])
    arrived(ends.at[1 - c], sem_ends)
    from_row = dot(jnp.concatenate([ends[0], ends[1]], axis=0), dev_g[...])
    x1 = x1 - from_row
    x0 = x0 + dot(from_row, lower[1])
    drain(23)
    gather_zg.forward()
    gather_zg.finish()
    share_ep.finish()
    two = dot(ep[3], zg[2]) + ep[2]
    three = dot(two, zg[1]) + ep[1]
    tops[c] = jnp.where(z == 3, 0.0, jnp.where(z == 2, ep[3], jnp.where(z == 1, two, three)))
    sem_tops = slot()
    swap(tops, sem_tops)
    arrived(tops.at[1 - c], sem_tops)
    top = jnp.concatenate([tops[0], tops[1]], axis=0)
    x1 = x1 - dot(top, to_w1)
    x0 = x0 + dot(top, to_w0)

    both = jnp.concatenate([x0, x1], axis=1)
    gram = lax.dot_general(both, both, (((1,), (1,)), ((), ())), precision=HIGH, preferred_element_type=F32)
    gram = jnp.concatenate([gram[0 : K // 2], gram[K // 2 : K]], axis=1)
    gown[0] = gram[0 : K // 4]
    gown[1] = gram[K // 4 : K // 2]
    mates = {(k, f): slot() for k in (1, 3, 2, 0) for f in (1, 0) if (k, f) != (0, 0)}
    here = x * 2 + c
    for (k, f), i in mates.items():
        other = c if f == 0 else 1 - c
        start(gown.at[other], gx.at[here], i, at(z, y, turn(x, k), other))
    gx[here] = gown[c]
    drain(9)
    for (k, f), i in mates.items():
        arrived(gx.at[turn(x, 4 - k) * 2 + (c if f == 0 else 1 - c)], i)
    own = z * 4 + y
    gyz[own] = ((gx[0] + gx[1]) + (gx[2] + gx[3])) + ((gx[4] + gx[5]) + (gx[6] + gx[7]))
    sems = {step: slot() for step in across}
    for step, other in across.items():
        start(gyz.at[own], gyz.at[own], sems[step], other)
    drain(3)
    for (k, n), i in sems.items():
        arrived(gyz.at[turn(z, 4 - k) * 4 + turn(y, 4 - n)], i)
    terms = [gyz[i] for i in range(16)]
    while len(terms) > 1:
        terms = [terms[i] + terms[i + 1] for i in range(0, len(terms), 2)]
    gtot[c] = terms[0]
    sem_gtot = slot()
    swap(gtot, sem_gtot)
    drain(15)
    arrived(gtot.at[1 - c], sem_gtot)
    total = jnp.concatenate([gtot[0], gtot[1]], axis=0) / (256 * W)
    r, inverse = factor(jnp.concatenate([total[:, 0:K], total[:, K : 2 * K]], axis=0))
    r_factor[...] = r
    basis[0] = dot(inverse, x0)
    basis[1] = dot(inverse, x1)
    drain(len(sent))


def on_device(sketch, inv_diag, upper, lower):
    def buf(*shape):
        return pltpu.VMEM(shape, F32)

    affine = (ROWS, W)
    part = (HALF_C, W)
    quarter = (K // 4, 2 * K)
    vmem = pl.BlockSpec(memory_space=pltpu.VMEM)
    scratch = [
        buf(2, K, W), buf(2, W, W), buf(2, W, W), buf(2, W, W), buf(*affine), buf(2, *affine), buf(2, W, W), buf(2, *affine),
        buf(*affine), buf(*affine), buf(W, W), buf(*affine),
        buf(4, *affine), buf(4, W, W), buf(4, *affine), buf(4, *affine), buf(4, *affine), buf(4, W, W),
        buf(4, *affine), buf(4, W, W), buf(4, *affine), buf(4, W, W), buf(3, W, W), buf(*affine),
        buf(*affine), buf(*part), buf(W, W), buf(*part), buf(2, *part), buf(4, W, W), buf(2, *part),
        buf(4, *part), buf(4, *part), buf(4, *part), buf(2, *part), buf(2, *part),
        buf(2, *quarter), buf(8, *quarter), buf(16, *quarter), buf(2, *quarter),
        pltpu.SemaphoreType.DMA((SEMS,)), pltpu.SemaphoreType.DMA((SEMS,)), pltpu.SemaphoreType.DMA((7,)),
    ]
    return pl.pallas_call(
        kernel,
        out_shape=(pltpu.VMEM((2, K, W), F32), pltpu.VMEM((K, K), F32)),
        in_specs=[pl.BlockSpec(memory_space=pl.ANY)] * 4,
        out_specs=(vmem, vmem),
        scratch_shapes=scratch,
        compiler_params=pltpu.CompilerParams(
            collective_id=0, has_side_effects=True, vmem_limit_bytes=56 * 2**20
        ),
        name="sweeps",
    )(sketch, inv_diag, upper, lower)


def solution(mesh):
    placed = (P("chain", None, None),) * 4
    return jax.shard_map(
        on_device,
        mesh=mesh,
        in_specs=placed,
        out_specs=(P("chain", None, None), P()),
        check_vma=False,
    )
```

```python
import jax
import jax.numpy as jnp
from jax import lax
from jax.experimental import pallas as pl
from jax.experimental.pallas import tpu as pltpu
from jax.sharding import PartitionSpec as P

HIGH = lax.Precision.HIGHEST
MESH = pl.DeviceIdType.MESH
F32 = jnp.float32

W = 256
K = 64
HALF_M = 128
HALF_C = 32
HALF = HALF_M + HALF_C
ROWS = 2 * HALF
SEMS = 160


def dot(a, b):
    return jnp.dot(a, b, precision=HIGH, preferred_element_type=F32)


def mat(n):
    return jnp.concatenate([n[0:HALF_M], n[HALF : HALF + HALF_M]], axis=0)


def vec(n):
    return jnp.concatenate([n[HALF_M:HALF], n[HALF + HALF_M : ROWS]], axis=0)


def pack(m, c):
    return jnp.concatenate([m[0:HALF_M], c[0:HALF_C], m[HALF_M:W], c[HALF_C:K]], axis=0)


def add_vec(r, n):
    return jnp.concatenate(
        [
            r[0:HALF_M],
            r[HALF_M:HALF] + n[HALF_M:HALF],
            r[HALF : HALF + HALF_M],
            r[HALF + HALF_M : ROWS] + n[HALF + HALF_M : ROWS],
        ],
        axis=0,
    )


def compose(f, n):
    return add_vec(dot(f, mat(n)), n)


def apply(v, n):
    return dot(v, mat(n)) + vec(n)


def identity(rows, columns):
    return (
        lax.broadcasted_iota(jnp.int32, (rows, columns), 0) == lax.broadcasted_iota(jnp.int32, (rows, columns), 1)
    ).astype(F32)


def factor(gram):
    work = jnp.concatenate([gram, identity(K, K)], axis=1)
    count = K // 8
    blocks = [work[8 * b : 8 * b + 8] for b in range(count)]
    sub = lax.broadcasted_iota(jnp.int32, (8, 2 * K), 0)

    def wide(v):
        return jnp.broadcast_to(v, (8, 2 * K))

    out = []
    for b in range(count):
        columns = [{i: wide(blocks[i][:, 8 * b + j : 8 * b + j + 1]) for i in range(b, count)} for j in range(8)]
        corner = {(i, j): wide(columns[j][b][i : i + 1]) for j in range(8) for i in range(j, 8)}
        rows = [wide(blocks[b][j : j + 1]) for j in range(8)]
        scaled = []
        done = jnp.zeros((8, 2 * K), F32)
        pivots = jnp.ones((8, 2 * K), F32)
        for j in range(8):
            inverse = 1.0 / corner[j, j]
            scaled.append(rows[j] * inverse)
            pivots = jnp.where(sub == j, corner[j, j], pivots)
            done = jnp.where(sub == j, rows[j], done)
            for i in range(j + 1, 8):
                ratio = corner[i, j] * inverse
                rows[i] = rows[i] - ratio * rows[j]
                for n in range(i, 8):
                    corner[n, i] = corner[n, i] - corner[n, j] * ratio
                for n in range(b + 1, count):
                    columns[i][n] = columns[i][n] - columns[j][n] * ratio
        for i in range(b + 1, count):
            for j in range(8):
                blocks[i] = blocks[i] - columns[j][i] * scaled[j]
        out.append(done * lax.rsqrt(pivots))
    out = jnp.concatenate(out, axis=0)
    upper = jnp.where(
        lax.broadcasted_iota(jnp.int32, (K, K), 0) <= lax.broadcasted_iota(jnp.int32, (K, K), 1), out[:, 0:K], 0.0
    )
    return upper, out[:, K : 2 * K]


def kernel(
    sketch_in, inv_diag_in, upper_in, lower_in, basis, r_factor,
    sketch, inv_diag, upper, lower, own0, fc, gc, hc, y0s, y1s, dev_g, dev_h,
    xf, xg, xh, xpre, xsuf_h, xsuf_g, yf, yg, ypre, ysuf_g, ysum, row_h,
    zf, zc_in, zm_in, va, va_in, zg, entry, er, ep, ysuf_e, ends, tops, gown, gx, gyz, gtot,
    send, recv, load,
):
    me = lax.axis_index("chain")
    c = lax.rem(me, 2)
    x = lax.rem(me // 2, 4)
    y = lax.rem(me // 8, 4)
    z = me // 32

    loads = []
    for src, dst in ((inv_diag_in, inv_diag), (upper_in, upper), (lower_in, lower)):
        for i in (0, 1):
            loads.append(pltpu.make_async_copy(src.at[i], dst.at[i], load.at[len(loads)]))
    loads.append(pltpu.make_async_copy(sketch_in, sketch, load.at[6]))
    for i in (0, 2, 6, 1, 3, 4, 5):
        loads[i].start()

    def at(zz, yy, xx, cc):
        return ((zz * 4 + yy) * 4 + xx) * 2 + cc

    def turn(place, k):
        return lax.rem(place + k, 4)

    sibling = at(z, y, x, 1 - c)
    xs = [at(z, y, turn(x, k), c) for k in range(4)]
    steps = sorted(((k, n) for k in range(4) for n in range(4)), key=lambda s: -sum(min(v, 4 - v) for v in s))
    across = {(k, n): at(turn(z, k), turn(y, n), x, c) for k, n in steps if (k, n) != (0, 0)}
    ys = [None, *(across[0, n] for n in (1, 2, 3))]
    zs = [None, *(across[k, 0] for k in (1, 2, 3))]

    barrier = pltpu.get_barrier_semaphore()
    for other in (*zs[1:], *ys[1:], *xs[1:], sibling):
        pl.semaphore_signal(barrier, inc=1, device_id=(other,), device_id_type=MESH)

    sent = []
    used = [0]

    def slot():
        used[0] += 1
        assert used[0] <= SEMS
        return used[0] - 1

    def on(condition, act):
        if condition is None:
            act()
        else:
            pl.when(condition)(act)

    def start(src, dst, i, other, condition=None):
        copy = pltpu.make_async_remote_copy(
            src_ref=src, dst_ref=dst, send_sem=send.at[i], recv_sem=recv.at[i], device_id=(other,), device_id_type=MESH
        )
        on(condition, copy.start)
        sent.append((condition, copy))

    def arrived(dst, i, condition=None):
        copy = pltpu.make_async_remote_copy(
            src_ref=dst, dst_ref=dst, send_sem=send.at[i], recv_sem=recv.at[i], device_id=(sibling,), device_id_type=MESH
        )
        on(condition, copy.wait_recv)

    def drain(count):
        for condition, copy in sent[:count]:
            on(condition, copy.wait_send)
        del sent[:count]

    def rows_of(which, rows):
        return pl.ds(pl.multiple_of(which * rows, 8), rows)

    mine, others = rows_of(c, HALF), rows_of(1 - c, HALF)
    my_vec = pl.ds(pl.multiple_of(c * HALF + HALF_M, 8), HALF_C)

    def compose_half(f, n, which):
        r = dot(f, mat(n[...]))
        return jnp.concatenate(
            [r[0:HALF_M], r[HALF_M:HALF] + n[pl.ds(pl.multiple_of(which * HALF + HALF_M, 8), HALF_C)]], axis=0
        )

    class Gather:
        def __init__(self, ref, rows, place, peers, steps, gives=None, takes=None):
            self.ref, self.rows, self.place, self.peers, self.steps = ref, rows, place, peers, steps
            self.gives = dict(zip(steps, gives)) if gives else {}
            self.takes = dict(zip(steps, takes)) if takes else {}
            self.first = {k: slot() for k in steps}
            self.second = {k: slot() for k in steps}

        def part(self, k, which):
            return self.ref.at[turn(self.place, 4 - k), rows_of(which, self.rows)]

        def start(self):
            for k in self.steps:
                start(self.part(0, c), self.part(0, c), self.first[k], self.peers[k], self.gives.get(k))

        def forward(self):
            for k in self.steps:
                arrived(self.part(k, c), self.first[k], self.takes.get(k))
                start(self.part(k, c), self.part(k, c), self.second[k], sibling, self.takes.get(k))

        def finish(self):
            for k in self.steps:
                arrived(self.part(k, 1 - c), self.second[k], self.takes.get(k))

    class Relay:
        handed = ((1, 0), (3, 3), (1, 1), (3, 2))
        piece = HALF // 4

        def __init__(self, ref, place, peers):
            self.ref, self.place, self.peers = ref, place, peers
            self.first = {key: slot() for key in (*self.handed, (1, "rest"), (3, "rest"))}
            self.far = {key: slot() for key in self.handed}
            self.second = {key: slot() for key in ((1, 0), (3, 1), (1, 1), (3, 0), (2, None))}

        def rows(self, k, low, count, which):
            at_row = pl.multiple_of(which * HALF + low, 8)
            return self.ref.at[turn(self.place, 4 - k), pl.ds(at_row, count)]

        def quarter(self, k, q):
            return self.rows(k, q * self.piece, self.piece, c)

        def half(self, k, p, which):
            return self.rows(k, p * 2 * self.piece, 2 * self.piece, which)

        def start(self):
            for k, q in self.handed:
                start(self.quarter(0, q), self.quarter(0, q), self.first[k, q], self.peers[k])
            for k, p in ((1, 1), (3, 0)):
                start(self.half(0, p, c), self.half(0, p, c), self.first[k, "rest"], self.peers[k])

        def inside(self, k, p):
            start(self.half(k, p, c), self.half(k, p, c), self.second[k, p], sibling)

        def relay(self):
            for k, q in self.handed:
                arrived(self.quarter(k, q), self.first[k, q])
                start(self.quarter(k, q), self.quarter(k, q), self.far[k, q], self.peers[k])
            self.inside(1, 0)
            self.inside(3, 1)

        def forward(self):
            for k, p in ((1, 1), (3, 0)):
                arrived(self.half(k, p, c), self.first[k, "rest"])
                self.inside(k, p)
            for k, q in self.handed:
                arrived(self.quarter(2, q), self.far[k, q])
            start(self.rows(2, 0, HALF, c), self.rows(2, 0, HALF, c), self.second[2, None], sibling)

        def finish(self):
            for k, p in self.second:
                part = self.rows(2, 0, HALF, 1 - c) if p is None else self.half(k, p, 1 - c)
                arrived(part, self.second[k, p])

    class Share:
        def __init__(self, ref, place, peers):
            self.ref, self.place, self.peers = ref, place, peers
            self.sems = {k: slot() for k in (1, 3, 2)}

        def start(self):
            for k in (2, 1, 3):
                start(self.ref.at[self.place], self.ref.at[self.place], self.sems[k], self.peers[k])

        def finish(self):
            for k in (1, 3, 2):
                arrived(self.ref.at[turn(self.place, 4 - k)], self.sems[k])

    def swap(ref, i):
        start(ref.at[c], ref.at[c], i, sibling)

    for i in (0, 2, 6):
        loads[i].wait()
    y0s[...] = dot(pack(-upper[0], sketch[0]), inv_diag[0])
    for i in (1, 3):
        loads[i].wait()
    own0[...] = dot(pack(-upper[1], sketch[1]), inv_diag[1])
    y1s[...] = compose(y0s[...], own0[...])
    fc[c] = y1s[...]
    pl.semaphore_wait(barrier, 1 + 3 + 3 + 3)
    sem_f, sem_g, sem_h = slot(), slot(), slot()
    swap(fc, sem_f)
    for i in (4, 5):
        loads[i].wait()
    gc[c] = dot(lower[1], lower[0])
    swap(gc, sem_g)
    arrived(fc.at[1 - c], sem_f)

    xf[x, mine] = compose_half(fc[0, mine], fc.at[1], c)
    gather_xf = Relay(xf, x, xs)
    gather_xf.start()
    xf[x, others] = compose_half(fc[0, others], fc.at[1], 1 - c)
    hc[c] = dot(y0s[...] - dot(y1s[...], lower[1]), lower[0])
    swap(hc, sem_h)
    arrived(gc.at[1 - c], sem_g)
    xg[x] = dot(gc[1], gc[0])
    gather_xf.relay()

    gather_xg = Gather(xg, HALF_M, x, xs, (1, 3, 2))
    gather_xg.start()
    arrived(hc.at[1 - c], sem_h)
    late = compose(fc[0], hc[1])
    xh[x] = dot(late, gc[0]) + hc[0]
    second = c == 1
    eye = identity(W, W)
    dev_g[...] = jnp.where(second, eye, gc[1])
    dev_h[...] = jnp.where(second, 0.0, late)
    y0s[...] = jnp.where(second, compose(fc[0], y0s[...]), y0s[...])
    y1s[...] = jnp.where(second, xf[x], y1s[...])
    drain(3)
    gather_xf.forward()
    gather_xf.finish()
    q23 = compose(xf[2], xf[3])
    xsuf_h[0] = q23
    xpre[2, mine] = compose_half(xf[0, mine], xf.at[1], c)
    yf[y, mine] = compose_half(xpre[2, mine], xsuf_h.at[0], c)

    gather_yf = Relay(yf, y, ys)
    gather_yf.start()
    gather_xh = Gather(xh, HALF, x, xs, (1, 3, 2))
    gather_xh.start()
    xpre[2, others] = compose_half(xf[0, others], xf.at[1], 1 - c)
    yf[y, others] = compose_half(xpre[2, others], xsuf_h.at[0], 1 - c)
    xpre[0] = pack(eye, jnp.zeros((K, W), F32))
    xpre[1] = xf[0]
    xpre[3] = compose(xpre[2], xf[2])
    y0s[...] = compose(xpre[x], y0s[...])
    y1s[...] = compose(xpre[x], y1s[...])
    drain(12)
    gather_yf.relay()

    gather_xg.forward()
    dev_h[...] = compose(xpre[x], dev_h[...])
    gather_xg.finish()
    xsuf_g[3] = eye
    xsuf_g[2] = xg[3]
    xsuf_g[1] = dot(xg[3], xg[2])
    yg[y] = dot(xsuf_g[1], dot(xg[1], xg[0]))
    gather_yg = Gather(yg, HALF_M, y, ys, (1, 3, 2))
    gather_yg.start()
    xsuf_g[0] = dot(xsuf_g[1], xg[1])
    gather_yf.forward()
    gather_yf.finish()
    q23 = compose(yf[2], yf[3])
    xsuf_h[0] = q23
    ypre[2, mine] = compose_half(yf[0, mine], yf.at[1], c)
    zf[my_vec] = dot(ypre[2, my_vec], mat(q23)) + xsuf_h[0, my_vec]

    sem_c, sem_m, sem_m2, sem_v1, sem_v2 = slot(), slot(), slot(), slot(), slot()
    start(zf.at[my_vec], zc_in, sem_c, zs[1])
    my_m = pl.ds(pl.multiple_of(c * HALF, 8), HALF_M)
    other_m = pl.ds(pl.multiple_of((1 - c) * HALF, 8), HALF_M)
    my_half, other_half = rows_of(c, HALF_M), rows_of(1 - c, HALF_M)
    zf[my_m] = dot(ypre[2, my_m], mat(q23))
    start(zf.at[my_m], zm_in.at[my_half], sem_m, zs[1])
    ypre[2, others] = compose_half(yf[0, others], yf.at[1], 1 - c)
    zf[other_m] = dot(ypre[2, other_m], mat(q23))
    gather_xh.forward()
    ypre[0] = pack(eye, jnp.zeros((K, W), F32))
    ypre[1] = yf[0]
    gather_xh.finish()
    xsuf_h[3] = jnp.zeros((ROWS, W), F32)
    xsuf_h[2] = compose(xpre[3], xh[3])
    xsuf_h[1] = dot(xsuf_h[2], xg[2]) + compose(xpre[2], xh[2])

    arrived(zc_in, sem_c)
    va[...] = dot(zc_in[...], mat(zf[...])) + zf[my_vec]
    start(va, va_in.at[1], sem_v2, zs[2])
    start(va, va_in.at[0], sem_v1, zs[1])
    arrived(zm_in.at[my_half], sem_m)
    start(zm_in.at[my_half], zm_in.at[my_half], sem_m2, sibling)

    ypre[3] = compose(ypre[2], yf[2])
    xsuf_h[0] = dot(xsuf_h[1], xg[1]) + compose(xf[0], xh[1])
    row_h[...] = compose(ypre[y], dot(xsuf_h[0], xg[0]) + xh[0])
    drain(24)

    arrived(zm_in.at[other_half], sem_m2)
    arrived(va_in.at[0], sem_v1)
    arrived(va_in.at[1], sem_v2)
    last = dot(va_in[1], zm_in[...]) + zc_in[...]
    start_row = jnp.where(z == 0, 0.0, jnp.where(z == 1, zc_in[...], jnp.where(z == 2, va_in[0], last)))

    er[y] = dot(start_row, mat(row_h[...])) + row_h[my_vec]
    share_er = Share(er, y, ys)
    share_er.start()
    entry[c] = start_row
    sem_entry = slot()
    swap(entry, sem_entry)
    gather_yg.forward()
    gather_yg.finish()
    ysuf_g[3] = eye
    ysuf_g[2] = yg[3]
    ysum[1] = dot(yg[1], yg[0])
    ysuf_g[1] = dot(yg[3], yg[2])
    zg[z] = dot(ysuf_g[1], ysum[1])
    gather_zg = Gather(zg, HALF_M, z, zs, (3, 2), ((z == 1) | (z == 2), z == 2), (z < 2, z == 0))
    gather_zg.start()

    ysum[0] = yg[0]
    ysum[2] = dot(yg[2], ysum[1])
    ysuf_g[0] = dot(ysuf_g[1], yg[1])

    dev_h[...] = dot(xsuf_h[x], dev_g[...]) + dev_h[...]
    dev_g[...] = dot(xsuf_g[x], dev_g[...])
    share_er.finish()
    ep[z] = dot(jnp.concatenate([er[1], er[2], er[3]], axis=1), ysum[...].reshape(3 * W, W)) + er[0]

    share_ep = Share(ep, z, zs)
    share_ep.start()
    ysuf_e[3] = jnp.zeros((HALF_C, W), F32)
    ysuf_e[2] = er[3]
    ysuf_e[1] = dot(er[3], yg[2]) + er[2]
    ysuf_e[0] = dot(ysuf_e[1], yg[1]) + er[1]
    ends[c] = ysuf_e[y]
    sem_ends = slot()
    swap(ends, sem_ends)
    arrived(entry.at[1 - c], sem_entry)
    row = apply(jnp.concatenate([entry[0], entry[1]], axis=0), ypre[y])
    x1 = apply(row, y1s[...]) - apply(row, dev_h[...])
    x0 = apply(row, y0s[...]) - dot(x1, lower[1])
    to_w1 = dot(ysuf_g[y], dev_g[...])
    to_w0 = dot(to_w1, lower[1])
    arrived(ends.at[1 - c], sem_ends)
    from_row = dot(jnp.concatenate([ends[0], ends[1]], axis=0), dev_g[...])
    x1 = x1 - from_row
    x0 = x0 + dot(from_row, lower[1])
    drain(23)
    gather_zg.forward()
    gather_zg.finish()
    share_ep.finish()
    two = dot(ep[3], zg[2]) + ep[2]
    three = dot(two, zg[1]) + ep[1]
    tops[c] = jnp.where(z == 3, 0.0, jnp.where(z == 2, ep[3], jnp.where(z == 1, two, three)))
    sem_tops = slot()
    swap(tops, sem_tops)
    arrived(tops.at[1 - c], sem_tops)
    top = jnp.concatenate([tops[0], tops[1]], axis=0)
    x1 = x1 - dot(top, to_w1)
    x0 = x0 + dot(top, to_w0)

    both = jnp.concatenate([x0, x1], axis=1)
    gram = lax.dot_general(both, both, (((1,), (1,)), ((), ())), precision=HIGH, preferred_element_type=F32)
    gram = jnp.concatenate([gram[0 : K // 2], gram[K // 2 : K]], axis=1)
    gown[0] = gram[0 : K // 4]
    gown[1] = gram[K // 4 : K // 2]
    mates = {(k, f): slot() for k in (2, 1, 3, 0) for f in (1, 0) if (k, f) != (0, 0)}
    here = x * 2 + c
    for (k, f), i in mates.items():
        other = c if f == 0 else 1 - c
        start(gown.at[other], gx.at[here], i, at(z, y, turn(x, k), other))
    gx[here] = gown[c]
    drain(9)
    for (k, f), i in mates.items():
        arrived(gx.at[turn(x, 4 - k) * 2 + (c if f == 0 else 1 - c)], i)
    own = z * 4 + y
    gyz[own] = ((gx[0] + gx[1]) + (gx[2] + gx[3])) + ((gx[4] + gx[5]) + (gx[6] + gx[7]))
    sems = {step: slot() for step in across}
    for step, other in across.items():
        start(gyz.at[own], gyz.at[own], sems[step], other)
    drain(3)
    for (k, n), i in sems.items():
        arrived(gyz.at[turn(z, 4 - k) * 4 + turn(y, 4 - n)], i)
    terms = [gyz[i] for i in range(16)]
    while len(terms) > 1:
        terms = [terms[i] + terms[i + 1] for i in range(0, len(terms), 2)]
    gtot[c] = terms[0]
    sem_gtot = slot()
    swap(gtot, sem_gtot)
    drain(15)
    arrived(gtot.at[1 - c], sem_gtot)
    total = jnp.concatenate([gtot[0], gtot[1]], axis=0) / (256 * W)
    r, inverse = factor(jnp.concatenate([total[:, 0:K], total[:, K : 2 * K]], axis=0))
    r_factor[...] = r
    basis[0] = dot(inverse, x0)
    basis[1] = dot(inverse, x1)
    drain(len(sent))


def on_device(sketch, inv_diag, upper, lower):
    def buf(*shape):
        return pltpu.VMEM(shape, F32)

    affine = (ROWS, W)
    part = (HALF_C, W)
    quarter = (K // 4, 2 * K)
    vmem = pl.BlockSpec(memory_space=pltpu.VMEM)
    scratch = [
        buf(2, K, W), buf(2, W, W), buf(2, W, W), buf(2, W, W), buf(*affine), buf(2, *affine), buf(2, W, W), buf(2, *affine),
        buf(*affine), buf(*affine), buf(W, W), buf(*affine),
        buf(4, *affine), buf(4, W, W), buf(4, *affine), buf(4, *affine), buf(4, *affine), buf(4, W, W),
        buf(4, *affine), buf(4, W, W), buf(4, *affine), buf(4, W, W), buf(3, W, W), buf(*affine),
        buf(*affine), buf(*part), buf(W, W), buf(*part), buf(2, *part), buf(4, W, W), buf(2, *part),
        buf(4, *part), buf(4, *part), buf(4, *part), buf(2, *part), buf(2, *part),
        buf(2, *quarter), buf(8, *quarter), buf(16, *quarter), buf(2, *quarter),
        pltpu.SemaphoreType.DMA((SEMS,)), pltpu.SemaphoreType.DMA((SEMS,)), pltpu.SemaphoreType.DMA((7,)),
    ]
    return pl.pallas_call(
        kernel,
        out_shape=(pltpu.VMEM((2, K, W), F32), pltpu.VMEM((K, K), F32)),
        in_specs=[pl.BlockSpec(memory_space=pl.ANY)] * 4,
        out_specs=(vmem, vmem),
        scratch_shapes=scratch,
        compiler_params=pltpu.CompilerParams(
            collective_id=0, has_side_effects=True, vmem_limit_bytes=56 * 2**20
        ),
        name="sweeps",
    )(sketch, inv_diag, upper, lower)


def solution(mesh):
    placed = (P("chain", None, None),) * 4
    return jax.shard_map(
        on_device,
        mesh=mesh,
        in_specs=placed,
        out_specs=(P("chain", None, None), P()),
        check_vma=False,
    )
```

```python
import jax
import jax.numpy as jnp
from jax import lax
from jax.experimental import pallas as pl
from jax.experimental.pallas import tpu as pltpu
from jax.sharding import PartitionSpec as P

HIGH = lax.Precision.HIGHEST
MESH = pl.DeviceIdType.MESH
F32 = jnp.float32

W = 256
K = 64
HALF_M = 128
HALF_C = 32
HALF = HALF_M + HALF_C
ROWS = 2 * HALF
SEMS = 160


def dot(a, b):
    return jnp.dot(a, b, precision=HIGH, preferred_element_type=F32)


def mat(n):
    return jnp.concatenate([n[0:HALF_M], n[HALF : HALF + HALF_M]], axis=0)


def vec(n):
    return jnp.concatenate([n[HALF_M:HALF], n[HALF + HALF_M : ROWS]], axis=0)


def pack(m, c):
    return jnp.concatenate([m[0:HALF_M], c[0:HALF_C], m[HALF_M:W], c[HALF_C:K]], axis=0)


def add_vec(r, n):
    return jnp.concatenate(
        [
            r[0:HALF_M],
            r[HALF_M:HALF] + n[HALF_M:HALF],
            r[HALF : HALF + HALF_M],
            r[HALF + HALF_M : ROWS] + n[HALF + HALF_M : ROWS],
        ],
        axis=0,
    )


def compose(f, n):
    return add_vec(dot(f, mat(n)), n)


def apply(v, n):
    return dot(v, mat(n)) + vec(n)


def identity(rows, columns):
    return (
        lax.broadcasted_iota(jnp.int32, (rows, columns), 0) == lax.broadcasted_iota(jnp.int32, (rows, columns), 1)
    ).astype(F32)


def factor(gram):
    work = jnp.concatenate([gram, identity(K, K)], axis=1)
    count = K // 8
    blocks = [work[8 * b : 8 * b + 8] for b in range(count)]
    sub = lax.broadcasted_iota(jnp.int32, (8, 2 * K), 0)

    def wide(v):
        return jnp.broadcast_to(v, (8, 2 * K))

    out = []
    for b in range(count):
        columns = [{i: wide(blocks[i][:, 8 * b + j : 8 * b + j + 1]) for i in range(b, count)} for j in range(8)]
        corner = {(i, j): wide(columns[j][b][i : i + 1]) for j in range(8) for i in range(j, 8)}
        rows = [wide(blocks[b][j : j + 1]) for j in range(8)]
        scaled = []
        done = jnp.zeros((8, 2 * K), F32)
        pivots = jnp.ones((8, 2 * K), F32)
        for j in range(8):
            inverse = 1.0 / corner[j, j]
            scaled.append(rows[j] * inverse)
            pivots = jnp.where(sub == j, corner[j, j], pivots)
            done = jnp.where(sub == j, rows[j], done)
            for i in range(j + 1, 8):
                ratio = corner[i, j] * inverse
                rows[i] = rows[i] - ratio * rows[j]
                for n in range(i, 8):
                    corner[n, i] = corner[n, i] - corner[n, j] * ratio
                for n in range(b + 1, count):
                    columns[i][n] = columns[i][n] - columns[j][n] * ratio
        for i in range(b + 1, count):
            for j in range(8):
                blocks[i] = blocks[i] - columns[j][i] * scaled[j]
        out.append(done * lax.rsqrt(pivots))
    out = jnp.concatenate(out, axis=0)
    upper = jnp.where(
        lax.broadcasted_iota(jnp.int32, (K, K), 0) <= lax.broadcasted_iota(jnp.int32, (K, K), 1), out[:, 0:K], 0.0
    )
    return upper, out[:, K : 2 * K]


def kernel(
    sketch_in, inv_diag_in, upper_in, lower_in, basis, r_factor,
    sketch, inv_diag, upper, lower, own0, fc, gc, hc, y0s, y1s, dev_g, dev_h,
    xf, xg, xh, xpre, xsuf_h, xsuf_g, yf, yg, ypre, ysuf_g, ysum, row_h,
    zf, zc_in, zm_in, va, va_in, zg, entry, er, ep, ysuf_e, ends, tops, gown, gx, gyz, gtot,
    send, recv, load, heard,
):
    me = lax.axis_index("chain")
    c = lax.rem(me, 2)
    x = lax.rem(me // 2, 4)
    y = lax.rem(me // 8, 4)
    z = me // 32

    loads = []
    for src, dst in ((inv_diag_in, inv_diag), (upper_in, upper), (lower_in, lower)):
        for i in (0, 1):
            loads.append(pltpu.make_async_copy(src.at[i], dst.at[i], load.at[len(loads)]))
    loads.append(pltpu.make_async_copy(sketch_in, sketch, load.at[6]))
    for i in (0, 2, 6, 1, 3, 4, 5):
        loads[i].start()

    def at(zz, yy, xx, cc):
        return ((zz * 4 + yy) * 4 + xx) * 2 + cc

    def turn(place, k):
        return lax.rem(place + k, 4)

    sibling = at(z, y, x, 1 - c)
    xs = [at(z, y, turn(x, k), c) for k in range(4)]
    steps = sorted(((k, n) for k in range(4) for n in range(4)), key=lambda s: -sum(min(v, 4 - v) for v in s))
    across = {(k, n): at(turn(z, k), turn(y, n), x, c) for k, n in steps if (k, n) != (0, 0)}
    ys = [None, *(across[0, n] for n in (1, 2, 3))]
    zs = [None, *(across[k, 0] for k in (1, 2, 3))]

    barrier = pltpu.get_barrier_semaphore()
    above, below = z < 3, z > 0

    def greet(other):
        pl.semaphore_signal(barrier, inc=1, device_id=(other,), device_id_type=MESH)

    pl.when(above)(lambda: greet(zs[1]))
    pl.when(below)(lambda: greet(zs[3]))
    for other in (ys[1], ys[3], xs[1], xs[3], sibling):
        greet(other)

    sent = []
    used = [0]

    def slot():
        used[0] += 1
        assert used[0] <= SEMS
        return used[0] - 1

    def on(condition, act):
        if condition is None:
            act()
        else:
            pl.when(condition)(act)

    def start(src, dst, i, other, condition=None):
        copy = pltpu.make_async_remote_copy(
            src_ref=src, dst_ref=dst, send_sem=send.at[i], recv_sem=recv.at[i], device_id=(other,), device_id_type=MESH
        )
        on(condition, copy.start)
        sent.append((condition, copy))

    def arrived(dst, i, condition=None):
        copy = pltpu.make_async_remote_copy(
            src_ref=dst, dst_ref=dst, send_sem=send.at[i], recv_sem=recv.at[i], device_id=(sibling,), device_id_type=MESH
        )
        on(condition, copy.wait_recv)

    def drain(count):
        for condition, copy in sent[:count]:
            on(condition, copy.wait_send)
        del sent[:count]

    def rows_of(which, rows):
        return pl.ds(pl.multiple_of(which * rows, 8), rows)

    mine, others = rows_of(c, HALF), rows_of(1 - c, HALF)
    my_vec = pl.ds(pl.multiple_of(c * HALF + HALF_M, 8), HALF_C)

    def compose_half(f, n, which):
        r = dot(f, mat(n[...]))
        return jnp.concatenate(
            [r[0:HALF_M], r[HALF_M:HALF] + n[pl.ds(pl.multiple_of(which * HALF + HALF_M, 8), HALF_C)]], axis=0
        )

    class Gather:
        def __init__(self, ref, rows, place, peers, steps, gives=None, takes=None):
            self.ref, self.rows, self.place, self.peers, self.steps = ref, rows, place, peers, steps
            self.gives = dict(zip(steps, gives)) if gives else {}
            self.takes = dict(zip(steps, takes)) if takes else {}
            self.first = {k: slot() for k in steps}
            self.second = {k: slot() for k in steps}

        def part(self, k, which):
            return self.ref.at[turn(self.place, 4 - k), rows_of(which, self.rows)]

        def start(self):
            for k in self.steps:
                start(self.part(0, c), self.part(0, c), self.first[k], self.peers[k], self.gives.get(k))

        def forward(self):
            for k in self.steps:
                arrived(self.part(k, c), self.first[k], self.takes.get(k))
                start(self.part(k, c), self.part(k, c), self.second[k], sibling, self.takes.get(k))

        def finish(self):
            for k in self.steps:
                arrived(self.part(k, 1 - c), self.second[k], self.takes.get(k))

    class Relay:
        handed = ((1, 0), (3, 3), (1, 1), (3, 2))
        piece = HALF // 4

        def __init__(self, ref, place, peers):
            self.ref, self.place, self.peers = ref, place, peers
            self.first = {key: slot() for key in (*self.handed, (1, "rest"), (3, "rest"))}
            self.far = {key: slot() for key in self.handed}
            self.second = {key: slot() for key in ((1, 0), (3, 1), (1, 1), (3, 0), (2, None))}

        def rows(self, k, low, count, which):
            at_row = pl.multiple_of(which * HALF + low, 8)
            return self.ref.at[turn(self.place, 4 - k), pl.ds(at_row, count)]

        def quarter(self, k, q):
            return self.rows(k, q * self.piece, self.piece, c)

        def half(self, k, p, which):
            return self.rows(k, p * 2 * self.piece, 2 * self.piece, which)

        def start(self):
            for k, q in self.handed:
                start(self.quarter(0, q), self.quarter(0, q), self.first[k, q], self.peers[k])
            for k, p in ((1, 1), (3, 0)):
                start(self.half(0, p, c), self.half(0, p, c), self.first[k, "rest"], self.peers[k])

        def inside(self, k, p):
            start(self.half(k, p, c), self.half(k, p, c), self.second[k, p], sibling)

        def relay(self):
            for k, q in self.handed:
                arrived(self.quarter(k, q), self.first[k, q])
                start(self.quarter(k, q), self.quarter(k, q), self.far[k, q], self.peers[k])
            self.inside(1, 0)
            self.inside(3, 1)

        def forward(self):
            for k, p in ((1, 1), (3, 0)):
                arrived(self.half(k, p, c), self.first[k, "rest"])
                self.inside(k, p)
            for k, q in self.handed:
                arrived(self.quarter(2, q), self.far[k, q])
            start(self.rows(2, 0, HALF, c), self.rows(2, 0, HALF, c), self.second[2, None], sibling)

        def finish(self):
            for k, p in self.second:
                part = self.rows(2, 0, HALF, 1 - c) if p is None else self.half(k, p, 1 - c)
                arrived(part, self.second[k, p])

    class Share:
        def __init__(self, ref, place, peers, gives=None, takes=None):
            self.ref, self.place, self.peers = ref, place, peers
            self.gives, self.takes = gives or {}, takes or {}
            self.sems = {k: slot() for k in (1, 3, 2)}

        def start(self):
            own = self.ref.at[self.place]
            for k in (2, 1, 3):
                start(own, own, self.sems[k], self.peers[k], self.gives.get(k))

        def finish(self):
            for k in (1, 3, 2):
                arrived(self.ref.at[turn(self.place, 4 - k)], self.sems[k], self.takes.get(k))

    def swap(ref, i):
        start(ref.at[c], ref.at[c], i, sibling)

    for i in (0, 2, 6):
        loads[i].wait()
    y0s[...] = dot(pack(-upper[0], sketch[0]), inv_diag[0])
    for i in (1, 3):
        loads[i].wait()
    own0[...] = dot(pack(-upper[1], sketch[1]), inv_diag[1])
    y1s[...] = compose(y0s[...], own0[...])
    fc[c] = y1s[...]
    pl.semaphore_wait(barrier, 5 + jnp.where(above, 1, 0) + jnp.where(below, 1, 0))
    pl.when(z == 2)(lambda: pl.semaphore_signal(heard, inc=1, device_id=(zs[3],), device_id_type=MESH))
    sem_f, sem_g, sem_h = slot(), slot(), slot()
    swap(fc, sem_f)
    for i in (4, 5):
        loads[i].wait()
    gc[c] = dot(lower[1], lower[0])
    swap(gc, sem_g)
    arrived(fc.at[1 - c], sem_f)

    xf[x, mine] = compose_half(fc[0, mine], fc.at[1], c)
    gather_xf = Relay(xf, x, xs)
    gather_xf.start()
    xf[x, others] = compose_half(fc[0, others], fc.at[1], 1 - c)
    hc[c] = dot(y0s[...] - dot(y1s[...], lower[1]), lower[0])
    swap(hc, sem_h)
    arrived(gc.at[1 - c], sem_g)
    xg[x] = dot(gc[1], gc[0])
    gather_xf.relay()

    gather_xg = Gather(xg, HALF_M, x, xs, (1, 3, 2))
    gather_xg.start()
    arrived(hc.at[1 - c], sem_h)
    late = compose(fc[0], hc[1])
    xh[x] = dot(late, gc[0]) + hc[0]
    second = c == 1
    eye = identity(W, W)
    dev_g[...] = jnp.where(second, eye, gc[1])
    dev_h[...] = jnp.where(second, 0.0, late)
    y0s[...] = jnp.where(second, compose(fc[0], y0s[...]), y0s[...])
    y1s[...] = jnp.where(second, xf[x], y1s[...])
    drain(3)
    gather_xf.forward()
    gather_xf.finish()
    q23 = compose(xf[2], xf[3])
    xsuf_h[0] = q23
    xpre[2, mine] = compose_half(xf[0, mine], xf.at[1], c)
    yf[y, mine] = compose_half(xpre[2, mine], xsuf_h.at[0], c)

    gather_yf = Relay(yf, y, ys)
    gather_yf.start()
    gather_xh = Gather(xh, HALF, x, xs, (1, 3, 2))
    gather_xh.start()
    xpre[2, others] = compose_half(xf[0, others], xf.at[1], 1 - c)
    yf[y, others] = compose_half(xpre[2, others], xsuf_h.at[0], 1 - c)
    xpre[0] = pack(eye, jnp.zeros((K, W), F32))
    xpre[1] = xf[0]
    xpre[3] = compose(xpre[2], xf[2])
    y0s[...] = compose(xpre[x], y0s[...])
    y1s[...] = compose(xpre[x], y1s[...])
    drain(12)
    gather_yf.relay()

    gather_xg.forward()
    dev_h[...] = compose(xpre[x], dev_h[...])
    gather_xg.finish()
    xsuf_g[3] = eye
    xsuf_g[2] = xg[3]
    xsuf_g[1] = dot(xg[3], xg[2])
    yg[y] = dot(xsuf_g[1], dot(xg[1], xg[0]))
    gather_yg = Gather(yg, HALF_M, y, ys, (1, 3, 2))
    gather_yg.start()
    xsuf_g[0] = dot(xsuf_g[1], xg[1])
    gather_yf.forward()
    gather_yf.finish()
    q23 = compose(yf[2], yf[3])
    xsuf_h[0] = q23
    ypre[2, mine] = compose_half(yf[0, mine], yf.at[1], c)
    zf[my_vec] = dot(ypre[2, my_vec], mat(q23)) + xsuf_h[0, my_vec]

    sem_c, sem_m, sem_m2, sem_v1, sem_v2 = slot(), slot(), slot(), slot(), slot()
    even, odd = lax.rem(z, 2) == 0, lax.rem(z, 2) == 1
    start(zf.at[my_vec], zc_in, sem_c, zs[1], even)
    my_m = pl.ds(pl.multiple_of(c * HALF, 8), HALF_M)
    other_m = pl.ds(pl.multiple_of((1 - c) * HALF, 8), HALF_M)
    my_half, other_half = rows_of(c, HALF_M), rows_of(1 - c, HALF_M)
    zf[my_m] = dot(ypre[2, my_m], mat(q23))
    start(zf.at[my_m], zm_in.at[my_half], sem_m, zs[1], z == 2)
    ypre[2, others] = compose_half(yf[0, others], yf.at[1], 1 - c)
    zf[other_m] = dot(ypre[2, other_m], mat(q23))
    gather_xh.forward()
    ypre[0] = pack(eye, jnp.zeros((K, W), F32))
    ypre[1] = yf[0]
    gather_xh.finish()
    xsuf_h[3] = jnp.zeros((ROWS, W), F32)
    xsuf_h[2] = compose(xpre[3], xh[3])
    xsuf_h[1] = dot(xsuf_h[2], xg[2]) + compose(xpre[2], xh[2])

    arrived(zc_in, sem_c, z == 1)

    @pl.when(z == 1)
    def _():
        pl.semaphore_wait(heard, 1)
        va[...] = dot(zc_in[...], mat(zf[...])) + zf[my_vec]

    start(va, va_in.at[1], sem_v2, zs[2], z == 1)
    start(va, va_in.at[0], sem_v1, zs[1], z == 1)
    arrived(zm_in.at[my_half], sem_m, z == 3)
    start(zm_in.at[my_half], zm_in.at[my_half], sem_m2, sibling, z == 3)

    ypre[3] = compose(ypre[2], yf[2])
    xsuf_h[0] = dot(xsuf_h[1], xg[1]) + compose(xf[0], xh[1])
    row_h[...] = compose(ypre[y], dot(xsuf_h[0], xg[0]) + xh[0])
    drain(24)

    arrived(zc_in, sem_c, z == 3)
    arrived(zm_in.at[other_half], sem_m2, z == 3)
    arrived(va_in.at[0], sem_v1, z == 2)
    arrived(va_in.at[1], sem_v2, z == 3)
    last = dot(va_in[1], zm_in[...]) + zc_in[...]
    start_row = jnp.where(z == 0, 0.0, jnp.where(z == 1, zc_in[...], jnp.where(z == 2, va_in[0], last)))

    er[y] = dot(start_row, mat(row_h[...])) + row_h[my_vec]
    share_er = Share(er, y, ys)
    share_er.start()
    entry[c] = start_row
    sem_entry = slot()
    swap(entry, sem_entry)
    gather_yg.forward()
    gather_yg.finish()
    ysuf_g[3] = eye
    ysuf_g[2] = yg[3]
    ysum[1] = dot(yg[1], yg[0])
    ysuf_g[1] = dot(yg[3], yg[2])
    zg[z] = dot(ysuf_g[1], ysum[1])
    gather_zg = Gather(zg, HALF_M, z, zs, (3, 2), ((z == 1) | (z == 2), z == 2), (z < 2, z == 0))
    gather_zg.start()

    ysum[0] = yg[0]
    ysum[2] = dot(yg[2], ysum[1])
    ysuf_g[0] = dot(ysuf_g[1], yg[1])

    dev_h[...] = dot(xsuf_h[x], dev_g[...]) + dev_h[...]
    dev_g[...] = dot(xsuf_g[x], dev_g[...])
    share_er.finish()
    ep[z] = dot(jnp.concatenate([er[1], er[2], er[3]], axis=1), ysum[...].reshape(3 * W, W)) + er[0]

    share_ep = Share(ep, z, zs, {1: z == 3, 2: z >= 2, 3: z >= 1}, {1: z == 0, 2: z <= 1, 3: z <= 2})
    share_ep.start()
    ysuf_e[3] = jnp.zeros((HALF_C, W), F32)
    ysuf_e[2] = er[3]
    ysuf_e[1] = dot(er[3], yg[2]) + er[2]
    ysuf_e[0] = dot(ysuf_e[1], yg[1]) + er[1]
    ends[c] = ysuf_e[y]
    sem_ends = slot()
    swap(ends, sem_ends)
    arrived(entry.at[1 - c], sem_entry)
    row = apply(jnp.concatenate([entry[0], entry[1]], axis=0), ypre[y])
    x1 = apply(row, y1s[...]) - apply(row, dev_h[...])
    x0 = apply(row, y0s[...]) - dot(x1, lower[1])
    to_w1 = dot(ysuf_g[y], dev_g[...])
    to_w0 = dot(to_w1, lower[1])
    arrived(ends.at[1 - c], sem_ends)
    from_row = dot(jnp.concatenate([ends[0], ends[1]], axis=0), dev_g[...])
    x1 = x1 - from_row
    x0 = x0 + dot(from_row, lower[1])
    drain(23)
    gather_zg.forward()
    gather_zg.finish()
    share_ep.finish()
    two = dot(ep[3], zg[2]) + ep[2]
    three = dot(two, zg[1]) + ep[1]
    tops[c] = jnp.where(z == 3, 0.0, jnp.where(z == 2, ep[3], jnp.where(z == 1, two, three)))
    sem_tops = slot()
    swap(tops, sem_tops)
    arrived(tops.at[1 - c], sem_tops)
    top = jnp.concatenate([tops[0], tops[1]], axis=0)
    x1 = x1 - dot(top, to_w1)
    x0 = x0 + dot(top, to_w0)

    both = jnp.concatenate([x0, x1], axis=1)
    gram = lax.dot_general(both, both, (((1,), (1,)), ((), ())), precision=HIGH, preferred_element_type=F32)
    gram = jnp.concatenate([gram[0 : K // 2], gram[K // 2 : K]], axis=1)
    gown[0] = gram[0 : K // 4]
    gown[1] = gram[K // 4 : K // 2]
    mates = {(k, f): slot() for k in (2, 1, 3, 0) for f in (1, 0) if (k, f) != (0, 0)}
    here = x * 2 + c
    for (k, f), i in mates.items():
        other = c if f == 0 else 1 - c
        start(gown.at[other], gx.at[here], i, at(z, y, turn(x, k), other))
    gx[here] = gown[c]
    drain(9)
    for (k, f), i in mates.items():
        arrived(gx.at[turn(x, 4 - k) * 2 + (c if f == 0 else 1 - c)], i)
    own = z * 4 + y
    gyz[own] = ((gx[0] + gx[1]) + (gx[2] + gx[3])) + ((gx[4] + gx[5]) + (gx[6] + gx[7]))
    sems = {step: slot() for step in across}
    for step, other in across.items():
        start(gyz.at[own], gyz.at[own], sems[step], other)
    drain(3)
    for (k, n), i in sems.items():
        arrived(gyz.at[turn(z, 4 - k) * 4 + turn(y, 4 - n)], i)
    terms = [gyz[i] for i in range(16)]
    while len(terms) > 1:
        terms = [terms[i] + terms[i + 1] for i in range(0, len(terms), 2)]
    gtot[c] = terms[0]
    sem_gtot = slot()
    swap(gtot, sem_gtot)
    drain(15)
    arrived(gtot.at[1 - c], sem_gtot)
    total = jnp.concatenate([gtot[0], gtot[1]], axis=0) / (256 * W)
    r, inverse = factor(jnp.concatenate([total[:, 0:K], total[:, K : 2 * K]], axis=0))
    r_factor[...] = r
    basis[0] = dot(inverse, x0)
    basis[1] = dot(inverse, x1)
    drain(len(sent))


def on_device(sketch, inv_diag, upper, lower):
    def buf(*shape):
        return pltpu.VMEM(shape, F32)

    affine = (ROWS, W)
    part = (HALF_C, W)
    quarter = (K // 4, 2 * K)
    vmem = pl.BlockSpec(memory_space=pltpu.VMEM)
    scratch = [
        buf(2, K, W), buf(2, W, W), buf(2, W, W), buf(2, W, W), buf(*affine), buf(2, *affine), buf(2, W, W), buf(2, *affine),
        buf(*affine), buf(*affine), buf(W, W), buf(*affine),
        buf(4, *affine), buf(4, W, W), buf(4, *affine), buf(4, *affine), buf(4, *affine), buf(4, W, W),
        buf(4, *affine), buf(4, W, W), buf(4, *affine), buf(4, W, W), buf(3, W, W), buf(*affine),
        buf(*affine), buf(*part), buf(W, W), buf(*part), buf(2, *part), buf(4, W, W), buf(2, *part),
        buf(4, *part), buf(4, *part), buf(4, *part), buf(2, *part), buf(2, *part),
        buf(2, *quarter), buf(8, *quarter), buf(16, *quarter), buf(2, *quarter),
        pltpu.SemaphoreType.DMA((SEMS,)), pltpu.SemaphoreType.DMA((SEMS,)), pltpu.SemaphoreType.DMA((7,)),
        pltpu.SemaphoreType.REGULAR,
    ]
    return pl.pallas_call(
        kernel,
        out_shape=(pltpu.VMEM((2, K, W), F32), pltpu.VMEM((K, K), F32)),
        in_specs=[pl.BlockSpec(memory_space=pl.ANY)] * 4,
        out_specs=(vmem, vmem),
        scratch_shapes=scratch,
        compiler_params=pltpu.CompilerParams(
            collective_id=0, has_side_effects=True, vmem_limit_bytes=56 * 2**20
        ),
        name="sweeps",
    )(sketch, inv_diag, upper, lower)


def solution(mesh):
    placed = (P("chain", None, None),) * 4
    return jax.shard_map(
        on_device,
        mesh=mesh,
        in_specs=placed,
        out_specs=(P("chain", None, None), P()),
        check_vma=False,
    )
```

```python
import jax
import jax.numpy as jnp
from jax import lax
from jax.experimental import pallas as pl
from jax.experimental.pallas import tpu as pltpu
from jax.sharding import PartitionSpec as P

HIGH = lax.Precision.HIGHEST
MESH = pl.DeviceIdType.MESH
F32 = jnp.float32

W = 256
K = 64
HALF_M = 128
HALF_C = 32
HALF = HALF_M + HALF_C
ROWS = 2 * HALF
SEMS = 160


def dot(a, b):
    return jnp.dot(a, b, precision=HIGH, preferred_element_type=F32)


def mat(n):
    return jnp.concatenate([n[0:HALF_M], n[HALF : HALF + HALF_M]], axis=0)


def vec(n):
    return jnp.concatenate([n[HALF_M:HALF], n[HALF + HALF_M : ROWS]], axis=0)


def pack(m, c):
    return jnp.concatenate([m[0:HALF_M], c[0:HALF_C], m[HALF_M:W], c[HALF_C:K]], axis=0)


def add_vec(r, n):
    return jnp.concatenate(
        [
            r[0:HALF_M],
            r[HALF_M:HALF] + n[HALF_M:HALF],
            r[HALF : HALF + HALF_M],
            r[HALF + HALF_M : ROWS] + n[HALF + HALF_M : ROWS],
        ],
        axis=0,
    )


def compose(f, n):
    return add_vec(dot(f, mat(n)), n)


def apply(v, n):
    return dot(v, mat(n)) + vec(n)


def identity(rows, columns):
    return (
        lax.broadcasted_iota(jnp.int32, (rows, columns), 0) == lax.broadcasted_iota(jnp.int32, (rows, columns), 1)
    ).astype(F32)


def factor(gram):
    work = jnp.concatenate([gram, identity(K, K)], axis=1)
    count = K // 8
    blocks = [work[8 * b : 8 * b + 8] for b in range(count)]
    sub = lax.broadcasted_iota(jnp.int32, (8, 2 * K), 0)

    def wide(v):
        return jnp.broadcast_to(v, (8, 2 * K))

    out = []
    for b in range(count):
        columns = [{i: wide(blocks[i][:, 8 * b + j : 8 * b + j + 1]) for i in range(b, count)} for j in range(8)]
        corner = {(i, j): wide(columns[j][b][i : i + 1]) for j in range(8) for i in range(j, 8)}
        rows = [wide(blocks[b][j : j + 1]) for j in range(8)]
        scaled = []
        done = jnp.zeros((8, 2 * K), F32)
        pivots = jnp.ones((8, 2 * K), F32)
        for j in range(8):
            inverse = 1.0 / corner[j, j]
            scaled.append(rows[j] * inverse)
            pivots = jnp.where(sub == j, corner[j, j], pivots)
            done = jnp.where(sub == j, rows[j], done)
            for i in range(j + 1, 8):
                ratio = corner[i, j] * inverse
                rows[i] = rows[i] - ratio * rows[j]
                for n in range(i, 8):
                    corner[n, i] = corner[n, i] - corner[n, j] * ratio
                for n in range(b + 1, count):
                    columns[i][n] = columns[i][n] - columns[j][n] * ratio
        for i in range(b + 1, count):
            for j in range(8):
                blocks[i] = blocks[i] - columns[j][i] * scaled[j]
        out.append(done * lax.rsqrt(pivots))
    out = jnp.concatenate(out, axis=0)
    upper = jnp.where(
        lax.broadcasted_iota(jnp.int32, (K, K), 0) <= lax.broadcasted_iota(jnp.int32, (K, K), 1), out[:, 0:K], 0.0
    )
    return upper, out[:, K : 2 * K]


def kernel(
    sketch_in, inv_diag_in, upper_in, lower_in, basis, r_factor,
    sketch, inv_diag, upper, lower, own0, fc, gc, hc, y0s, y1s, dev_g, dev_h,
    xf, xg, xh, xpre, xsuf_h, xsuf_g, yf, yg, ypre, ysuf_g, ysum, row_h,
    zf, zc_in, zm_in, va, va_in, zg, entry, er, ep, ysuf_e, ends, tops, gown, gx, gyz, gtot,
    send, recv, load, heard,
):
    me = lax.axis_index("chain")
    c = lax.rem(me, 2)
    x = lax.rem(me // 2, 4)
    y = lax.rem(me // 8, 4)
    z = me // 32

    loads = []
    for src, dst in ((inv_diag_in, inv_diag), (upper_in, upper), (lower_in, lower)):
        for i in (0, 1):
            loads.append(pltpu.make_async_copy(src.at[i], dst.at[i], load.at[len(loads)]))
    loads.append(pltpu.make_async_copy(sketch_in, sketch, load.at[6]))
    for i in (0, 2, 6, 1, 3, 4, 5):
        loads[i].start()

    def at(zz, yy, xx, cc):
        return ((zz * 4 + yy) * 4 + xx) * 2 + cc

    def turn(place, k):
        return lax.rem(place + k, 4)

    sibling = at(z, y, x, 1 - c)
    xs = [at(z, y, turn(x, k), c) for k in range(4)]
    steps = sorted(((k, n) for k in range(4) for n in range(4)), key=lambda s: -sum(min(v, 4 - v) for v in s))
    across = {(k, n): at(turn(z, k), turn(y, n), x, c) for k, n in steps if (k, n) != (0, 0)}
    ys = [None, *(across[0, n] for n in (1, 2, 3))]
    zs = [None, *(across[k, 0] for k in (1, 2, 3))]

    barrier = pltpu.get_barrier_semaphore()
    above, below = z < 3, z > 0

    def greet(other):
        pl.semaphore_signal(barrier, inc=1, device_id=(other,), device_id_type=MESH)

    pl.when(above)(lambda: greet(zs[1]))
    pl.when(below)(lambda: greet(zs[3]))
    for other in (ys[1], ys[3], xs[1], xs[3], sibling):
        greet(other)

    sent = []
    used = [0]

    def slot():
        used[0] += 1
        assert used[0] <= SEMS
        return used[0] - 1

    def on(condition, act):
        if condition is None:
            act()
        else:
            pl.when(condition)(act)

    def start(src, dst, i, other, condition=None):
        copy = pltpu.make_async_remote_copy(
            src_ref=src, dst_ref=dst, send_sem=send.at[i], recv_sem=recv.at[i], device_id=(other,), device_id_type=MESH
        )
        on(condition, copy.start)
        sent.append((condition, copy))

    def arrived(dst, i, condition=None):
        copy = pltpu.make_async_remote_copy(
            src_ref=dst, dst_ref=dst, send_sem=send.at[i], recv_sem=recv.at[i], device_id=(sibling,), device_id_type=MESH
        )
        on(condition, copy.wait_recv)

    def drain(count):
        for condition, copy in sent[:count]:
            on(condition, copy.wait_send)
        del sent[:count]

    def rows_of(which, rows):
        return pl.ds(pl.multiple_of(which * rows, 8), rows)

    mine, others = rows_of(c, HALF), rows_of(1 - c, HALF)
    my_vec = pl.ds(pl.multiple_of(c * HALF + HALF_M, 8), HALF_C)

    def compose_half(f, n, which):
        r = dot(f, mat(n[...]))
        return jnp.concatenate(
            [r[0:HALF_M], r[HALF_M:HALF] + n[pl.ds(pl.multiple_of(which * HALF + HALF_M, 8), HALF_C)]], axis=0
        )

    class Gather:
        def __init__(self, ref, rows, place, peers, steps, gives=None, takes=None):
            self.ref, self.rows, self.place, self.peers, self.steps = ref, rows, place, peers, steps
            self.gives = dict(zip(steps, gives)) if gives else {}
            self.takes = dict(zip(steps, takes)) if takes else {}
            self.first = {k: slot() for k in steps}
            self.second = {k: slot() for k in steps}

        def part(self, k, which):
            return self.ref.at[turn(self.place, 4 - k), rows_of(which, self.rows)]

        def start(self):
            for k in self.steps:
                start(self.part(0, c), self.part(0, c), self.first[k], self.peers[k], self.gives.get(k))

        def forward(self):
            for k in self.steps:
                arrived(self.part(k, c), self.first[k], self.takes.get(k))
                start(self.part(k, c), self.part(k, c), self.second[k], sibling, self.takes.get(k))

        def finish(self):
            for k in self.steps:
                arrived(self.part(k, 1 - c), self.second[k], self.takes.get(k))

    class Relay:
        handed = ((1, 0), (3, 3), (1, 1), (3, 2))
        piece = HALF // 4

        def __init__(self, ref, place, peers):
            self.ref, self.place, self.peers = ref, place, peers
            self.first = {key: slot() for key in (*self.handed, (1, "rest"), (3, "rest"))}
            self.far = {key: slot() for key in self.handed}
            self.second = {key: slot() for key in ((1, 0), (3, 1), (1, 1), (3, 0), (2, 0), (2, 1))}

        def rows(self, k, low, count, which):
            at_row = pl.multiple_of(which * HALF + low, 8)
            return self.ref.at[turn(self.place, 4 - k), pl.ds(at_row, count)]

        def quarter(self, k, q):
            return self.rows(k, q * self.piece, self.piece, c)

        def half(self, k, p, which):
            return self.rows(k, p * 2 * self.piece, 2 * self.piece, which)

        def start(self):
            for k, q in self.handed:
                start(self.quarter(0, q), self.quarter(0, q), self.first[k, q], self.peers[k])
            for k, p in ((1, 1), (3, 0)):
                start(self.half(0, p, c), self.half(0, p, c), self.first[k, "rest"], self.peers[k])

        def inside(self, k, p):
            start(self.half(k, p, c), self.half(k, p, c), self.second[k, p], sibling)

        def relay(self):
            for k, q in self.handed:
                arrived(self.quarter(k, q), self.first[k, q])
                start(self.quarter(k, q), self.quarter(k, q), self.far[k, q], self.peers[k])
            self.inside(1, 0)
            self.inside(3, 1)

        def forward(self):
            for k, p in ((1, 1), (3, 0)):
                arrived(self.half(k, p, c), self.first[k, "rest"])
                self.inside(k, p)
            for k, p in ((1, 0), (3, 1)):
                for q in (2 * p, 2 * p + 1):
                    arrived(self.quarter(2, q), self.far[k, q])
                self.inside(2, p)

        def finish(self):
            for k, p in self.second:
                arrived(self.half(k, p, 1 - c), self.second[k, p])

    class Share:
        def __init__(self, ref, place, peers, gives=None, takes=None):
            self.ref, self.place, self.peers = ref, place, peers
            self.gives, self.takes = gives or {}, takes or {}
            self.sems = {k: slot() for k in (1, 3, 2)}

        def start(self):
            own = self.ref.at[self.place]
            for k in (2, 1, 3):
                start(own, own, self.sems[k], self.peers[k], self.gives.get(k))

        def finish(self):
            for k in (1, 3, 2):
                arrived(self.ref.at[turn(self.place, 4 - k)], self.sems[k], self.takes.get(k))

    def swap(ref, i):
        start(ref.at[c], ref.at[c], i, sibling)

    for i in (0, 2, 6):
        loads[i].wait()
    y0s[...] = dot(pack(-upper[0], sketch[0]), inv_diag[0])
    for i in (1, 3):
        loads[i].wait()
    own0[...] = dot(pack(-upper[1], sketch[1]), inv_diag[1])
    y1s[...] = compose(y0s[...], own0[...])
    fc[c] = y1s[...]
    pl.semaphore_wait(barrier, 5 + jnp.where(above, 1, 0) + jnp.where(below, 1, 0))
    pl.when(z == 2)(lambda: pl.semaphore_signal(heard, inc=1, device_id=(zs[3],), device_id_type=MESH))
    sem_f, sem_g, sem_h = slot(), slot(), slot()
    swap(fc, sem_f)
    for i in (4, 5):
        loads[i].wait()
    gc[c] = dot(lower[1], lower[0])
    swap(gc, sem_g)
    arrived(fc.at[1 - c], sem_f)

    xf[x, mine] = compose_half(fc[0, mine], fc.at[1], c)
    gather_xf = Relay(xf, x, xs)
    gather_xf.start()
    xf[x, others] = compose_half(fc[0, others], fc.at[1], 1 - c)
    hc[c] = dot(y0s[...] - dot(y1s[...], lower[1]), lower[0])
    swap(hc, sem_h)
    arrived(gc.at[1 - c], sem_g)
    xg[x] = dot(gc[1], gc[0])
    gather_xf.relay()

    gather_xg = Gather(xg, HALF_M, x, xs, (1, 3, 2))
    gather_xg.start()
    arrived(hc.at[1 - c], sem_h)
    late = compose(fc[0], hc[1])
    xh[x] = dot(late, gc[0]) + hc[0]
    gather_xh = Gather(xh, HALF, x, xs, (1, 3, 2))
    gather_xh.start()
    second = c == 1
    eye = identity(W, W)
    dev_g[...] = jnp.where(second, eye, gc[1])
    dev_h[...] = jnp.where(second, 0.0, late)
    y0s[...] = jnp.where(second, compose(fc[0], y0s[...]), y0s[...])
    y1s[...] = jnp.where(second, xf[x], y1s[...])
    drain(3)
    gather_xf.forward()
    gather_xf.finish()
    q23 = compose(xf[2], xf[3])
    xsuf_h[0] = q23
    xpre[2, mine] = compose_half(xf[0, mine], xf.at[1], c)
    yf[y, mine] = compose_half(xpre[2, mine], xsuf_h.at[0], c)

    gather_yf = Relay(yf, y, ys)
    gather_yf.start()
    xpre[2, others] = compose_half(xf[0, others], xf.at[1], 1 - c)
    yf[y, others] = compose_half(xpre[2, others], xsuf_h.at[0], 1 - c)
    xpre[0] = pack(eye, jnp.zeros((K, W), F32))
    xpre[1] = xf[0]
    xpre[3] = compose(xpre[2], xf[2])
    y0s[...] = compose(xpre[x], y0s[...])
    y1s[...] = compose(xpre[x], y1s[...])
    drain(12)
    gather_yf.relay()

    gather_xg.forward()
    dev_h[...] = compose(xpre[x], dev_h[...])
    gather_xg.finish()
    xsuf_g[3] = eye
    xsuf_g[2] = xg[3]
    xsuf_g[1] = dot(xg[3], xg[2])
    yg[y] = dot(xsuf_g[1], dot(xg[1], xg[0]))
    gather_yg = Gather(yg, HALF_M, y, ys, (1, 3, 2))
    gather_yg.start()
    xsuf_g[0] = dot(xsuf_g[1], xg[1])
    gather_yf.forward()
    gather_yf.finish()
    q23 = compose(yf[2], yf[3])
    xsuf_h[0] = q23
    ypre[2, mine] = compose_half(yf[0, mine], yf.at[1], c)
    zf[my_vec] = dot(ypre[2, my_vec], mat(q23)) + xsuf_h[0, my_vec]

    sem_c, sem_m, sem_m2, sem_v1, sem_v2 = slot(), slot(), slot(), slot(), slot()
    even, odd = lax.rem(z, 2) == 0, lax.rem(z, 2) == 1
    start(zf.at[my_vec], zc_in, sem_c, zs[1], even)
    my_m = pl.ds(pl.multiple_of(c * HALF, 8), HALF_M)
    other_m = pl.ds(pl.multiple_of((1 - c) * HALF, 8), HALF_M)
    my_half, other_half = rows_of(c, HALF_M), rows_of(1 - c, HALF_M)
    zf[my_m] = dot(ypre[2, my_m], mat(q23))
    start(zf.at[my_m], zm_in.at[my_half], sem_m, zs[1], z == 2)
    ypre[2, others] = compose_half(yf[0, others], yf.at[1], 1 - c)
    zf[other_m] = dot(ypre[2, other_m], mat(q23))
    gather_xh.forward()
    ypre[0] = pack(eye, jnp.zeros((K, W), F32))
    ypre[1] = yf[0]
    gather_xh.finish()
    xsuf_h[3] = jnp.zeros((ROWS, W), F32)
    xsuf_h[2] = compose(xpre[3], xh[3])
    xsuf_h[1] = dot(xsuf_h[2], xg[2]) + compose(xpre[2], xh[2])

    arrived(zc_in, sem_c, z == 1)

    @pl.when(z == 1)
    def _():
        pl.semaphore_wait(heard, 1)
        va[...] = dot(zc_in[...], mat(zf[...])) + zf[my_vec]

    start(va, va_in.at[1], sem_v2, zs[2], z == 1)
    start(va, va_in.at[0], sem_v1, zs[1], z == 1)
    arrived(zm_in.at[my_half], sem_m, z == 3)
    start(zm_in.at[my_half], zm_in.at[my_half], sem_m2, sibling, z == 3)

    ypre[3] = compose(ypre[2], yf[2])
    xsuf_h[0] = dot(xsuf_h[1], xg[1]) + compose(xf[0], xh[1])
    row_h[...] = compose(ypre[y], dot(xsuf_h[0], xg[0]) + xh[0])
    drain(24)

    gather_yg.forward()
    arrived(zc_in, sem_c, z == 3)
    arrived(zm_in.at[other_half], sem_m2, z == 3)
    arrived(va_in.at[0], sem_v1, z == 2)
    arrived(va_in.at[1], sem_v2, z == 3)
    last = dot(va_in[1], zm_in[...]) + zc_in[...]
    start_row = jnp.where(z == 0, 0.0, jnp.where(z == 1, zc_in[...], jnp.where(z == 2, va_in[0], last)))

    er[y] = dot(start_row, mat(row_h[...])) + row_h[my_vec]
    share_er = Share(er, y, ys)
    share_er.start()
    entry[c] = start_row
    sem_entry = slot()
    swap(entry, sem_entry)
    gather_yg.finish()
    ysuf_g[3] = eye
    ysuf_g[2] = yg[3]
    ysum[1] = dot(yg[1], yg[0])
    ysuf_g[1] = dot(yg[3], yg[2])
    zg[z] = dot(ysuf_g[1], ysum[1])
    gather_zg = Gather(zg, HALF_M, z, zs, (3, 2), ((z == 1) | (z == 2), z == 2), (z < 2, z == 0))
    gather_zg.start()

    ysum[0] = yg[0]
    ysum[2] = dot(yg[2], ysum[1])
    ysuf_g[0] = dot(ysuf_g[1], yg[1])

    dev_h[...] = dot(xsuf_h[x], dev_g[...]) + dev_h[...]
    dev_g[...] = dot(xsuf_g[x], dev_g[...])
    share_er.finish()
    ep[z] = dot(jnp.concatenate([er[1], er[2], er[3]], axis=1), ysum[...].reshape(3 * W, W)) + er[0]

    share_ep = Share(ep, z, zs, {1: z == 3, 2: z >= 2, 3: z >= 1}, {1: z == 0, 2: z <= 1, 3: z <= 2})
    share_ep.start()
    ysuf_e[3] = jnp.zeros((HALF_C, W), F32)
    ysuf_e[2] = er[3]
    ysuf_e[1] = dot(er[3], yg[2]) + er[2]
    ysuf_e[0] = dot(ysuf_e[1], yg[1]) + er[1]
    ends[c] = ysuf_e[y]
    sem_ends = slot()
    swap(ends, sem_ends)
    arrived(entry.at[1 - c], sem_entry)
    row = apply(jnp.concatenate([entry[0], entry[1]], axis=0), ypre[y])
    x1 = apply(row, y1s[...]) - apply(row, dev_h[...])
    x0 = apply(row, y0s[...]) - dot(x1, lower[1])
    to_w1 = dot(ysuf_g[y], dev_g[...])
    to_w0 = dot(to_w1, lower[1])
    arrived(ends.at[1 - c], sem_ends)
    from_row = dot(jnp.concatenate([ends[0], ends[1]], axis=0), dev_g[...])
    x1 = x1 - from_row
    x0 = x0 + dot(from_row, lower[1])
    drain(23)
    gather_zg.forward()
    gather_zg.finish()
    share_ep.finish()
    two = dot(ep[3], zg[2]) + ep[2]
    three = dot(two, zg[1]) + ep[1]
    tops[c] = jnp.where(z == 3, 0.0, jnp.where(z == 2, ep[3], jnp.where(z == 1, two, three)))
    sem_tops = slot()
    swap(tops, sem_tops)
    arrived(tops.at[1 - c], sem_tops)
    top = jnp.concatenate([tops[0], tops[1]], axis=0)
    x1 = x1 - dot(top, to_w1)
    x0 = x0 + dot(top, to_w0)

    both = jnp.concatenate([x0, x1], axis=1)
    gram = lax.dot_general(both, both, (((1,), (1,)), ((), ())), precision=HIGH, preferred_element_type=F32)
    gram = jnp.concatenate([gram[0 : K // 2], gram[K // 2 : K]], axis=1)
    gown[0] = gram[0 : K // 4]
    gown[1] = gram[K // 4 : K // 2]
    mates = {(k, f): slot() for k in (2, 1, 3, 0) for f in (1, 0) if (k, f) != (0, 0)}
    here = x * 2 + c
    for (k, f), i in mates.items():
        other = c if f == 0 else 1 - c
        start(gown.at[other], gx.at[here], i, at(z, y, turn(x, k), other))
    gx[here] = gown[c]
    drain(9)
    for (k, f), i in mates.items():
        arrived(gx.at[turn(x, 4 - k) * 2 + (c if f == 0 else 1 - c)], i)
    own = z * 4 + y
    gyz[own] = ((gx[0] + gx[1]) + (gx[2] + gx[3])) + ((gx[4] + gx[5]) + (gx[6] + gx[7]))
    sems = {step: slot() for step in across}
    for step, other in across.items():
        start(gyz.at[own], gyz.at[own], sems[step], other)
    drain(3)
    for (k, n), i in sems.items():
        arrived(gyz.at[turn(z, 4 - k) * 4 + turn(y, 4 - n)], i)
    terms = [gyz[i] for i in range(16)]
    while len(terms) > 1:
        terms = [terms[i] + terms[i + 1] for i in range(0, len(terms), 2)]
    gtot[c] = terms[0]
    sem_gtot = slot()
    swap(gtot, sem_gtot)
    drain(15)
    arrived(gtot.at[1 - c], sem_gtot)
    total = jnp.concatenate([gtot[0], gtot[1]], axis=0) / (256 * W)
    r, inverse = factor(jnp.concatenate([total[:, 0:K], total[:, K : 2 * K]], axis=0))
    r_factor[...] = r
    basis[0] = dot(inverse, x0)
    basis[1] = dot(inverse, x1)
    drain(len(sent))


def on_device(sketch, inv_diag, upper, lower):
    def buf(*shape):
        return pltpu.VMEM(shape, F32)

    affine = (ROWS, W)
    part = (HALF_C, W)
    quarter = (K // 4, 2 * K)
    vmem = pl.BlockSpec(memory_space=pltpu.VMEM)
    scratch = [
        buf(2, K, W), buf(2, W, W), buf(2, W, W), buf(2, W, W), buf(*affine), buf(2, *affine), buf(2, W, W), buf(2, *affine),
        buf(*affine), buf(*affine), buf(W, W), buf(*affine),
        buf(4, *affine), buf(4, W, W), buf(4, *affine), buf(4, *affine), buf(4, *affine), buf(4, W, W),
        buf(4, *affine), buf(4, W, W), buf(4, *affine), buf(4, W, W), buf(3, W, W), buf(*affine),
        buf(*affine), buf(*part), buf(W, W), buf(*part), buf(2, *part), buf(4, W, W), buf(2, *part),
        buf(4, *part), buf(4, *part), buf(4, *part), buf(2, *part), buf(2, *part),
        buf(2, *quarter), buf(8, *quarter), buf(16, *quarter), buf(2, *quarter),
        pltpu.SemaphoreType.DMA((SEMS,)), pltpu.SemaphoreType.DMA((SEMS,)), pltpu.SemaphoreType.DMA((7,)),
        pltpu.SemaphoreType.REGULAR,
    ]
    return pl.pallas_call(
        kernel,
        out_shape=(pltpu.VMEM((2, K, W), F32), pltpu.VMEM((K, K), F32)),
        in_specs=[pl.BlockSpec(memory_space=pl.ANY)] * 4,
        out_specs=(vmem, vmem),
        scratch_shapes=scratch,
        compiler_params=pltpu.CompilerParams(
            collective_id=0, has_side_effects=True, vmem_limit_bytes=56 * 2**20
        ),
        name="sweeps",
    )(sketch, inv_diag, upper, lower)


def solution(mesh):
    placed = (P("chain", None, None),) * 4
    return jax.shard_map(
        on_device,
        mesh=mesh,
        in_specs=placed,
        out_specs=(P("chain", None, None), P()),
        check_vma=False,
    )
```

```python
import jax
import jax.numpy as jnp
from jax import lax
from jax.experimental import pallas as pl
from jax.experimental.pallas import tpu as pltpu
from jax.sharding import PartitionSpec as P

HIGH = lax.Precision.HIGHEST
MESH = pl.DeviceIdType.MESH
F32 = jnp.float32

W = 256
K = 64
HALF_M = 128
HALF_C = 32
HALF = HALF_M + HALF_C
ROWS = 2 * HALF
SEMS = 160


def dot(a, b):
    return jnp.dot(a, b, precision=HIGH, preferred_element_type=F32)


def mat(n):
    return jnp.concatenate([n[0:HALF_M], n[HALF : HALF + HALF_M]], axis=0)


def vec(n):
    return jnp.concatenate([n[HALF_M:HALF], n[HALF + HALF_M : ROWS]], axis=0)


def pack(m, c):
    return jnp.concatenate([m[0:HALF_M], c[0:HALF_C], m[HALF_M:W], c[HALF_C:K]], axis=0)


def add_vec(r, n):
    return jnp.concatenate(
        [
            r[0:HALF_M],
            r[HALF_M:HALF] + n[HALF_M:HALF],
            r[HALF : HALF + HALF_M],
            r[HALF + HALF_M : ROWS] + n[HALF + HALF_M : ROWS],
        ],
        axis=0,
    )


def compose(f, n):
    return add_vec(dot(f, mat(n)), n)


def apply(v, n):
    return dot(v, mat(n)) + vec(n)


def identity(rows, columns):
    return (
        lax.broadcasted_iota(jnp.int32, (rows, columns), 0) == lax.broadcasted_iota(jnp.int32, (rows, columns), 1)
    ).astype(F32)


def factor(gram):
    work = jnp.concatenate([gram, identity(K, K)], axis=1)
    count = K // 8
    blocks = [work[8 * b : 8 * b + 8] for b in range(count)]
    sub = lax.broadcasted_iota(jnp.int32, (8, 2 * K), 0)

    def wide(v):
        return jnp.broadcast_to(v, (8, 2 * K))

    out = []
    for b in range(count):
        columns = [{i: wide(blocks[i][:, 8 * b + j : 8 * b + j + 1]) for i in range(b, count)} for j in range(8)]
        corner = {(i, j): wide(columns[j][b][i : i + 1]) for j in range(8) for i in range(j, 8)}
        rows = [wide(blocks[b][j : j + 1]) for j in range(8)]
        scaled = []
        done = jnp.zeros((8, 2 * K), F32)
        pivots = jnp.ones((8, 2 * K), F32)
        for j in range(8):
            inverse = 1.0 / corner[j, j]
            scaled.append(rows[j] * inverse)
            pivots = jnp.where(sub == j, corner[j, j], pivots)
            done = jnp.where(sub == j, rows[j], done)
            for i in range(j + 1, 8):
                ratio = corner[i, j] * inverse
                rows[i] = rows[i] - ratio * rows[j]
                for n in range(i, 8):
                    corner[n, i] = corner[n, i] - corner[n, j] * ratio
                for n in range(b + 1, count):
                    columns[i][n] = columns[i][n] - columns[j][n] * ratio
        for i in range(b + 1, count):
            for j in range(8):
                blocks[i] = blocks[i] - columns[j][i] * scaled[j]
        out.append(done * lax.rsqrt(pivots))
    out = jnp.concatenate(out, axis=0)
    upper = jnp.where(
        lax.broadcasted_iota(jnp.int32, (K, K), 0) <= lax.broadcasted_iota(jnp.int32, (K, K), 1), out[:, 0:K], 0.0
    )
    return upper, out[:, K : 2 * K]


def kernel(
    sketch_in, inv_diag_in, upper_in, lower_in, basis, r_factor,
    sketch, inv_diag, upper, lower, own0, fc, gc, hc, y0s, y1s, dev_g, dev_h,
    xf, xg, xh, xpre, xsuf_h, xsuf_g, yf, yg, ypre, ysuf_g, ysum, row_h, pairs_x, pairs_y,
    zf, zc_in, zm_in, va, va_in, zg, entry, er, ep, ysuf_e, ends, tops, gown, gx, gyz, gtot,
    send, recv, load, heard,
):
    me = lax.axis_index("chain")
    c = lax.rem(me, 2)
    x = lax.rem(me // 2, 4)
    y = lax.rem(me // 8, 4)
    z = me // 32

    loads = []
    for src, dst in ((inv_diag_in, inv_diag), (upper_in, upper), (lower_in, lower)):
        for i in (0, 1):
            loads.append(pltpu.make_async_copy(src.at[i], dst.at[i], load.at[len(loads)]))
    loads.append(pltpu.make_async_copy(sketch_in, sketch, load.at[6]))
    for i in (0, 2, 6, 1, 3, 4, 5):
        loads[i].start()

    def at(zz, yy, xx, cc):
        return ((zz * 4 + yy) * 4 + xx) * 2 + cc

    def turn(place, k):
        return lax.rem(place + k, 4)

    sibling = at(z, y, x, 1 - c)
    xs = [at(z, y, turn(x, k), c) for k in range(4)]
    steps = sorted(((k, n) for k in range(4) for n in range(4)), key=lambda s: -sum(min(v, 4 - v) for v in s))
    across = {(k, n): at(turn(z, k), turn(y, n), x, c) for k, n in steps if (k, n) != (0, 0)}
    ys = [None, *(across[0, n] for n in (1, 2, 3))]
    zs = [None, *(across[k, 0] for k in (1, 2, 3))]

    barrier = pltpu.get_barrier_semaphore()
    above, below = z < 3, z > 0

    def greet(other):
        pl.semaphore_signal(barrier, inc=1, device_id=(other,), device_id_type=MESH)

    pl.when(above)(lambda: greet(zs[1]))
    pl.when(below)(lambda: greet(zs[3]))
    for other in (ys[1], ys[3], xs[1], xs[3], sibling):
        greet(other)

    sent = []
    used = [0]

    def slot():
        used[0] += 1
        assert used[0] <= SEMS
        return used[0] - 1

    def on(condition, act):
        if condition is None:
            act()
        else:
            pl.when(condition)(act)

    def start(src, dst, i, other, condition=None):
        copy = pltpu.make_async_remote_copy(
            src_ref=src, dst_ref=dst, send_sem=send.at[i], recv_sem=recv.at[i], device_id=(other,), device_id_type=MESH
        )
        on(condition, copy.start)
        sent.append((condition, copy))

    def arrived(dst, i, condition=None):
        copy = pltpu.make_async_remote_copy(
            src_ref=dst, dst_ref=dst, send_sem=send.at[i], recv_sem=recv.at[i], device_id=(sibling,), device_id_type=MESH
        )
        on(condition, copy.wait_recv)

    def drain(count):
        for condition, copy in sent[:count]:
            on(condition, copy.wait_send)
        del sent[:count]

    def rows_of(which, rows):
        return pl.ds(pl.multiple_of(which * rows, 8), rows)

    mine, others = rows_of(c, HALF), rows_of(1 - c, HALF)
    my_vec = pl.ds(pl.multiple_of(c * HALF + HALF_M, 8), HALF_C)

    def compose_half(f, n, which):
        r = dot(f, mat(n[...]))
        return jnp.concatenate(
            [r[0:HALF_M], r[HALF_M:HALF] + n[pl.ds(pl.multiple_of(which * HALF + HALF_M, 8), HALF_C)]], axis=0
        )

    class Gather:
        def __init__(self, ref, rows, place, peers, steps, gives=None, takes=None):
            self.ref, self.rows, self.place, self.peers, self.steps = ref, rows, place, peers, steps
            self.gives = dict(zip(steps, gives)) if gives else {}
            self.takes = dict(zip(steps, takes)) if takes else {}
            self.first = {k: slot() for k in steps}
            self.second = {k: slot() for k in steps}

        def part(self, k, which):
            return self.ref.at[turn(self.place, 4 - k), rows_of(which, self.rows)]

        def start(self):
            for k in self.steps:
                start(self.part(0, c), self.part(0, c), self.first[k], self.peers[k], self.gives.get(k))

        def forward(self):
            for k in self.steps:
                arrived(self.part(k, c), self.first[k], self.takes.get(k))
                start(self.part(k, c), self.part(k, c), self.second[k], sibling, self.takes.get(k))

        def finish(self):
            for k in self.steps:
                arrived(self.part(k, 1 - c), self.second[k], self.takes.get(k))

    class Relay:
        handed = ((1, 0), (3, 3), (1, 1), (3, 2))
        piece = HALF // 4

        def __init__(self, ref, place, peers):
            self.ref, self.place, self.peers = ref, place, peers
            self.first = {key: slot() for key in (*self.handed, (1, "rest"), (3, "rest"))}
            self.far = {key: slot() for key in self.handed}
            self.second = {key: slot() for key in ((1, 0), (3, 1), (1, 1), (3, 0), (2, 0), (2, 1))}

        def rows(self, k, low, count, which):
            at_row = pl.multiple_of(which * HALF + low, 8)
            return self.ref.at[turn(self.place, 4 - k), pl.ds(at_row, count)]

        def quarter(self, k, q):
            return self.rows(k, q * self.piece, self.piece, c)

        def half(self, k, p, which):
            return self.rows(k, p * 2 * self.piece, 2 * self.piece, which)

        def start(self):
            for k, q in self.handed:
                start(self.quarter(0, q), self.quarter(0, q), self.first[k, q], self.peers[k])
            for k, p in ((1, 1), (3, 0)):
                start(self.half(0, p, c), self.half(0, p, c), self.first[k, "rest"], self.peers[k])

        def inside(self, k, p):
            start(self.half(k, p, c), self.half(k, p, c), self.second[k, p], sibling)

        def relay(self):
            for k, q in self.handed:
                arrived(self.quarter(k, q), self.first[k, q])
                start(self.quarter(k, q), self.quarter(k, q), self.far[k, q], self.peers[k])
            self.inside(1, 0)
            self.inside(3, 1)

        def forward(self):
            for k, p in ((1, 1), (3, 0)):
                arrived(self.half(k, p, c), self.first[k, "rest"])
                self.inside(k, p)
            for k, p in ((1, 0), (3, 1)):
                for q in (2 * p, 2 * p + 1):
                    arrived(self.quarter(2, q), self.far[k, q])
                self.inside(2, p)

        def finish(self, pairs):
            def pair(i):
                pairs[i] = compose(self.ref[2 * i], self.ref[2 * i + 1])

            own_pair = self.place // 2
            for far in (False, True):
                for k, p in self.second:
                    if (k == 2) == far:
                        arrived(self.half(k, p, 1 - c), self.second[k, p])
                pair(1 - own_pair if far else own_pair)

    class Share:
        def __init__(self, ref, place, peers, gives=None, takes=None):
            self.ref, self.place, self.peers = ref, place, peers
            self.gives, self.takes = gives or {}, takes or {}
            self.sems = {k: slot() for k in (1, 3, 2)}

        def start(self):
            own = self.ref.at[self.place]
            for k in (2, 1, 3):
                start(own, own, self.sems[k], self.peers[k], self.gives.get(k))

        def finish(self):
            for k in (1, 3, 2):
                arrived(self.ref.at[turn(self.place, 4 - k)], self.sems[k], self.takes.get(k))

    def swap(ref, i):
        start(ref.at[c], ref.at[c], i, sibling)

    for i in (0, 2, 6):
        loads[i].wait()
    y0s[...] = dot(pack(-upper[0], sketch[0]), inv_diag[0])
    for i in (1, 3):
        loads[i].wait()
    own0[...] = dot(pack(-upper[1], sketch[1]), inv_diag[1])
    y1s[...] = compose(y0s[...], own0[...])
    fc[c] = y1s[...]
    pl.semaphore_wait(barrier, 5 + jnp.where(above, 1, 0) + jnp.where(below, 1, 0))
    pl.when(z == 2)(lambda: pl.semaphore_signal(heard, inc=1, device_id=(zs[3],), device_id_type=MESH))
    sem_f, sem_g, sem_h = slot(), slot(), slot()
    swap(fc, sem_f)
    for i in (4, 5):
        loads[i].wait()
    gc[c] = dot(lower[1], lower[0])
    swap(gc, sem_g)
    arrived(fc.at[1 - c], sem_f)

    xf[x, mine] = compose_half(fc[0, mine], fc.at[1], c)
    gather_xf = Relay(xf, x, xs)
    gather_xf.start()
    xf[x, others] = compose_half(fc[0, others], fc.at[1], 1 - c)
    hc[c] = dot(y0s[...] - dot(y1s[...], lower[1]), lower[0])
    swap(hc, sem_h)
    arrived(gc.at[1 - c], sem_g)
    xg[x] = dot(gc[1], gc[0])
    gather_xf.relay()

    gather_xg = Gather(xg, HALF_M, x, xs, (1, 3, 2))
    gather_xg.start()
    arrived(hc.at[1 - c], sem_h)
    late = compose(fc[0], hc[1])
    xh[x] = dot(late, gc[0]) + hc[0]
    gather_xh = Gather(xh, HALF, x, xs, (1, 3, 2))
    gather_xh.start()
    second = c == 1
    eye = identity(W, W)
    dev_g[...] = jnp.where(second, eye, gc[1])
    dev_h[...] = jnp.where(second, 0.0, late)
    y0s[...] = jnp.where(second, compose(fc[0], y0s[...]), y0s[...])
    y1s[...] = jnp.where(second, xf[x], y1s[...])
    drain(3)
    gather_xf.forward()
    gather_xf.finish(pairs_x)
    yf[y, mine] = compose_half(pairs_x[0, mine], pairs_x.at[1], c)

    gather_yf = Relay(yf, y, ys)
    gather_yf.start()
    xpre[2] = pairs_x[0]
    yf[y, others] = compose_half(pairs_x[0, others], pairs_x.at[1], 1 - c)
    xpre[0] = pack(eye, jnp.zeros((K, W), F32))
    xpre[1] = xf[0]
    xpre[3] = compose(xpre[2], xf[2])
    y0s[...] = compose(xpre[x], y0s[...])
    y1s[...] = compose(xpre[x], y1s[...])
    drain(12)
    gather_yf.relay()

    gather_xg.forward()
    dev_h[...] = compose(xpre[x], dev_h[...])
    gather_xg.finish()
    xsuf_g[3] = eye
    xsuf_g[2] = xg[3]
    xsuf_g[1] = dot(xg[3], xg[2])
    yg[y] = dot(xsuf_g[1], dot(xg[1], xg[0]))
    gather_yg = Gather(yg, HALF_M, y, ys, (1, 3, 2))
    gather_yg.start()
    xsuf_g[0] = dot(xsuf_g[1], xg[1])
    gather_yf.forward()
    gather_yf.finish(pairs_y)
    ypre[2] = pairs_y[0]
    zf[my_vec] = dot(pairs_y[0, my_vec], mat(pairs_y[1])) + pairs_y[1, my_vec]

    sem_c, sem_m, sem_m2, sem_v1, sem_v2 = slot(), slot(), slot(), slot(), slot()
    even, odd = lax.rem(z, 2) == 0, lax.rem(z, 2) == 1
    start(zf.at[my_vec], zc_in, sem_c, zs[1], even)
    my_m = pl.ds(pl.multiple_of(c * HALF, 8), HALF_M)
    other_m = pl.ds(pl.multiple_of((1 - c) * HALF, 8), HALF_M)
    my_half, other_half = rows_of(c, HALF_M), rows_of(1 - c, HALF_M)
    zf[my_m] = dot(pairs_y[0, my_m], mat(pairs_y[1]))
    start(zf.at[my_m], zm_in.at[my_half], sem_m, zs[1], z == 2)
    zf[other_m] = dot(pairs_y[0, other_m], mat(pairs_y[1]))
    gather_xh.forward()
    ypre[0] = pack(eye, jnp.zeros((K, W), F32))
    ypre[1] = yf[0]
    gather_xh.finish()
    xsuf_h[3] = jnp.zeros((ROWS, W), F32)
    xsuf_h[2] = compose(xpre[3], xh[3])
    xsuf_h[1] = dot(xsuf_h[2], xg[2]) + compose(xpre[2], xh[2])

    arrived(zc_in, sem_c, z == 1)

    @pl.when(z == 1)
    def _():
        pl.semaphore_wait(heard, 1)
        va[...] = dot(zc_in[...], mat(zf[...])) + zf[my_vec]

    start(va, va_in.at[1], sem_v2, zs[2], z == 1)
    start(va, va_in.at[0], sem_v1, zs[1], z == 1)
    arrived(zm_in.at[my_half], sem_m, z == 3)
    start(zm_in.at[my_half], zm_in.at[my_half], sem_m2, sibling, z == 3)

    ypre[3] = compose(ypre[2], yf[2])
    xsuf_h[0] = dot(xsuf_h[1], xg[1]) + compose(xf[0], xh[1])
    row_h[...] = compose(ypre[y], dot(xsuf_h[0], xg[0]) + xh[0])
    drain(24)

    gather_yg.forward()
    arrived(zc_in, sem_c, z == 3)
    arrived(zm_in.at[other_half], sem_m2, z == 3)
    arrived(va_in.at[0], sem_v1, z == 2)
    arrived(va_in.at[1], sem_v2, z == 3)
    last = dot(va_in[1], zm_in[...]) + zc_in[...]
    start_row = jnp.where(z == 0, 0.0, jnp.where(z == 1, zc_in[...], jnp.where(z == 2, va_in[0], last)))

    er[y] = dot(start_row, mat(row_h[...])) + row_h[my_vec]
    share_er = Share(er, y, ys)
    share_er.start()
    entry[c] = start_row
    sem_entry = slot()
    swap(entry, sem_entry)
    gather_yg.finish()
    ysuf_g[3] = eye
    ysuf_g[2] = yg[3]
    ysum[1] = dot(yg[1], yg[0])
    ysuf_g[1] = dot(yg[3], yg[2])
    zg[z] = dot(ysuf_g[1], ysum[1])
    gather_zg = Gather(zg, HALF_M, z, zs, (3, 2), ((z == 1) | (z == 2), z == 2), (z < 2, z == 0))
    gather_zg.start()

    ysum[0] = yg[0]
    ysum[2] = dot(yg[2], ysum[1])
    ysuf_g[0] = dot(ysuf_g[1], yg[1])

    dev_h[...] = dot(xsuf_h[x], dev_g[...]) + dev_h[...]
    dev_g[...] = dot(xsuf_g[x], dev_g[...])
    share_er.finish()
    ep[z] = dot(jnp.concatenate([er[1], er[2], er[3]], axis=1), ysum[...].reshape(3 * W, W)) + er[0]

    share_ep = Share(ep, z, zs, {1: z == 3, 2: z >= 2, 3: z >= 1}, {1: z == 0, 2: z <= 1, 3: z <= 2})
    share_ep.start()
    ysuf_e[3] = jnp.zeros((HALF_C, W), F32)
    ysuf_e[2] = er[3]
    ysuf_e[1] = dot(er[3], yg[2]) + er[2]
    ysuf_e[0] = dot(ysuf_e[1], yg[1]) + er[1]
    ends[c] = ysuf_e[y]
    sem_ends = slot()
    swap(ends, sem_ends)
    arrived(entry.at[1 - c], sem_entry)
    row = apply(jnp.concatenate([entry[0], entry[1]], axis=0), ypre[y])
    x1 = apply(row, y1s[...]) - apply(row, dev_h[...])
    x0 = apply(row, y0s[...]) - dot(x1, lower[1])
    to_w1 = dot(ysuf_g[y], dev_g[...])
    to_w0 = dot(to_w1, lower[1])
    arrived(ends.at[1 - c], sem_ends)
    from_row = dot(jnp.concatenate([ends[0], ends[1]], axis=0), dev_g[...])
    x1 = x1 - from_row
    x0 = x0 + dot(from_row, lower[1])
    drain(23)
    gather_zg.forward()
    gather_zg.finish()
    share_ep.finish()
    two = dot(ep[3], zg[2]) + ep[2]
    three = dot(two, zg[1]) + ep[1]
    tops[c] = jnp.where(z == 3, 0.0, jnp.where(z == 2, ep[3], jnp.where(z == 1, two, three)))
    sem_tops = slot()
    swap(tops, sem_tops)
    arrived(tops.at[1 - c], sem_tops)
    top = jnp.concatenate([tops[0], tops[1]], axis=0)
    x1 = x1 - dot(top, to_w1)
    x0 = x0 + dot(top, to_w0)

    both = jnp.concatenate([x0, x1], axis=1)
    gram = lax.dot_general(both, both, (((1,), (1,)), ((), ())), precision=HIGH, preferred_element_type=F32)
    gram = jnp.concatenate([gram[0 : K // 2], gram[K // 2 : K]], axis=1)
    gown[0] = gram[0 : K // 4]
    gown[1] = gram[K // 4 : K // 2]
    mates = {(k, f): slot() for k in (2, 1, 3, 0) for f in (1, 0) if (k, f) != (0, 0)}
    here = x * 2 + c
    for (k, f), i in mates.items():
        other = c if f == 0 else 1 - c
        start(gown.at[other], gx.at[here], i, at(z, y, turn(x, k), other))
    gx[here] = gown[c]
    drain(9)
    for (k, f), i in mates.items():
        arrived(gx.at[turn(x, 4 - k) * 2 + (c if f == 0 else 1 - c)], i)
    own = z * 4 + y
    gyz[own] = ((gx[0] + gx[1]) + (gx[2] + gx[3])) + ((gx[4] + gx[5]) + (gx[6] + gx[7]))
    sems = {step: slot() for step in across}
    for step, other in across.items():
        start(gyz.at[own], gyz.at[own], sems[step], other)
    drain(3)
    for (k, n), i in sems.items():
        arrived(gyz.at[turn(z, 4 - k) * 4 + turn(y, 4 - n)], i)
    terms = [gyz[i] for i in range(16)]
    while len(terms) > 1:
        terms = [terms[i] + terms[i + 1] for i in range(0, len(terms), 2)]
    gtot[c] = terms[0]
    sem_gtot = slot()
    swap(gtot, sem_gtot)
    drain(15)
    arrived(gtot.at[1 - c], sem_gtot)
    total = jnp.concatenate([gtot[0], gtot[1]], axis=0) / (256 * W)
    r, inverse = factor(jnp.concatenate([total[:, 0:K], total[:, K : 2 * K]], axis=0))
    r_factor[...] = r
    basis[0] = dot(inverse, x0)
    basis[1] = dot(inverse, x1)
    drain(len(sent))


def on_device(sketch, inv_diag, upper, lower):
    def buf(*shape):
        return pltpu.VMEM(shape, F32)

    affine = (ROWS, W)
    part = (HALF_C, W)
    quarter = (K // 4, 2 * K)
    vmem = pl.BlockSpec(memory_space=pltpu.VMEM)
    scratch = [
        buf(2, K, W), buf(2, W, W), buf(2, W, W), buf(2, W, W), buf(*affine), buf(2, *affine), buf(2, W, W), buf(2, *affine),
        buf(*affine), buf(*affine), buf(W, W), buf(*affine),
        buf(4, *affine), buf(4, W, W), buf(4, *affine), buf(4, *affine), buf(4, *affine), buf(4, W, W),
        buf(4, *affine), buf(4, W, W), buf(4, *affine), buf(4, W, W), buf(3, W, W), buf(*affine), buf(2, *affine), buf(2, *affine),
        buf(*affine), buf(*part), buf(W, W), buf(*part), buf(2, *part), buf(4, W, W), buf(2, *part),
        buf(4, *part), buf(4, *part), buf(4, *part), buf(2, *part), buf(2, *part),
        buf(2, *quarter), buf(8, *quarter), buf(16, *quarter), buf(2, *quarter),
        pltpu.SemaphoreType.DMA((SEMS,)), pltpu.SemaphoreType.DMA((SEMS,)), pltpu.SemaphoreType.DMA((7,)),
        pltpu.SemaphoreType.REGULAR,
    ]
    return pl.pallas_call(
        kernel,
        out_shape=(pltpu.VMEM((2, K, W), F32), pltpu.VMEM((K, K), F32)),
        in_specs=[pl.BlockSpec(memory_space=pl.ANY)] * 4,
        out_specs=(vmem, vmem),
        scratch_shapes=scratch,
        compiler_params=pltpu.CompilerParams(
            collective_id=0, has_side_effects=True, vmem_limit_bytes=56 * 2**20
        ),
        name="sweeps",
    )(sketch, inv_diag, upper, lower)


def solution(mesh):
    placed = (P("chain", None, None),) * 4
    return jax.shard_map(
        on_device,
        mesh=mesh,
        in_specs=placed,
        out_specs=(P("chain", None, None), P()),
        check_vma=False,
    )
```
